128 devices in a mesh: ctx: 32 (over z, x, y_hi), tp: 4 (over y_lo, core).
Axes of the slice: x: 4, y: 4 (y_hi: 2, y_lo: 2; y = y_hi * 2 + y_lo), z: 4, core: 2. Of those that a mesh axis runs over, the one named last changes fastest.
Arguments:
- tokens: bfloat16 [16384, 4096], P(('ctx', 'tp')), may hold values from -6 to 6
- proj_weight: bfloat16 [4096, 3, 2048], P('ctx', None, 'tp'), may hold values from -0.09375 to 0.09375
- filter_taps: float32 [2048, 128], P('tp'), may hold values from -0.5 to 0.5
- skip_gain: float32 [2048], P('tp'), may hold values from 0.5 to 1.5
- out_grad: bfloat16 [16384, 2048], P('ctx', 'tp'), may hold values from -6 to 6
Outputs:
- filtered: bfloat16 [16384, 2048], P('ctx', 'tp')
- tokens_grad: bfloat16 [16384, 4096], P(('ctx', 'tp'))
- filter_grad: float32 [2048, 128], P('tp')
- skip_grad: float32 [2048], P('tp')
The draws below stay inside these ranges and needn't reach their ends.
All inputs are finite; a program needn't handle non-finite values.
Results may differ from the reference program's by a relative error of at most 0.03.
Values may be sent and summed in bfloat16 or wider, within the bound.
A program may use at most 128 MiB of HBM per device.

```python
import jax
import jax.numpy as jnp
from jax import lax

D = 4096
C = 2048
TAPS = 128
TOKENS = 16384
N_TP = 4


def block_scale(key, shape, pieces, smallest, high):
    gain, own = 1.0, jax.random.fold_in(key, 6)
    for position, shards_of in pieces:
        heights = jnp.exp(jax.random.uniform(jax.random.fold_in(own, position), (shards_of,), jnp.float32, smallest / len(pieces), high / len(pieces)))
        gain = gain * jnp.repeat(heights, shape[position] // shards_of).reshape([-1 if axis == position else 1 for axis in range(len(shape))])
    return gain


def gaussian(stream_key, dims, width, reach, pieces=(), kind=jnp.bfloat16):
    array = width * jax.random.normal(stream_key, dims, jnp.float32)
    if pieces:
        array = array * block_scale(stream_key, dims, pieces, -0.22, 0.18)
    return jnp.clip(array, -reach, reach).astype(kind)


def setup_inputs(seed: int = 0) -> dict:
    seeds = jax.random.split(jax.random.key(seed), 6)
    return {
        "tokens": gaussian(seeds[0], (TOKENS, D), 1.0, 6.0, ((0, 128),)),
        "proj_weight": gaussian(seeds[1], (D, 3, C), D ** -0.5, 0.09375, ((0, 32), (2, 4))),
        "filter_taps": gaussian(seeds[2], (C, TAPS), 0.09, 0.5, ((0, 4),), jnp.float32),
        "skip_gain": jnp.clip(0.5 + 1.0 * jax.random.uniform(seeds[3], (C,), jnp.float32) ** block_scale(seeds[3], (C,), ((0, 4),), -0.2, 0.2), 0.5, 1.5),
        "out_grad": gaussian(seeds[4], (TOKENS, C), 1.0, 6.0, ((0, 32), (1, 4))),
    }


def reference(tokens, proj_weight, filter_taps, skip_gain, out_grad):
    f32 = jnp.float32
    bf16 = jnp.bfloat16
    query = jnp.dot(tokens, proj_weight[:, 0, :], preferred_element_type=f32).astype(bf16)
    key_proj = jnp.dot(tokens, proj_weight[:, 1, :], preferred_element_type=f32).astype(bf16)
    value = jnp.dot(tokens, proj_weight[:, 2, :], preferred_element_type=f32).astype(bf16)
    gated = (key_proj.astype(f32) * value.astype(f32)).astype(bf16)
    gated_f = gated.astype(f32)
    gated_pad = jnp.concatenate([jnp.zeros((TAPS, C), f32), gated_f], 0)

    def forward_tap(step, total):
        index = jnp.asarray(step).astype(jnp.int32)
        shifted = lax.dynamic_slice_in_dim(gated_pad, TAPS - index, TOKENS, 0)
        tap_value = lax.dynamic_slice_in_dim(filter_taps, index, 1, 1)[:, 0]
        return total + shifted * tap_value[None, :]

    mixed = lax.fori_loop(0, TAPS, forward_tap, skip_gain[None, :] * gated_f)
    filtered = (query.astype(f32) * mixed).astype(bf16)

    grad = out_grad.astype(f32)
    query_grad = grad * mixed
    mixed_grad = (grad * query.astype(f32)).astype(bf16)
    mixed_f = mixed_grad.astype(f32)
    mixed_pad = jnp.concatenate([mixed_f, jnp.zeros((TAPS, C), f32)], 0)

    def backward_tap(step, total):
        index = jnp.asarray(step).astype(jnp.int32)
        shifted = lax.dynamic_slice_in_dim(mixed_pad, index, TOKENS, 0)
        tap_value = lax.dynamic_slice_in_dim(filter_taps, index, 1, 1)[:, 0]
        return total + shifted * tap_value[None, :]

    gated_grad = lax.fori_loop(0, TAPS, backward_tap, skip_gain[None, :] * mixed_f)
    proj_grad = jnp.stack([query_grad, gated_grad * value.astype(f32), gated_grad * key_proj.astype(f32)], 1).astype(bf16)

    block = C // N_TP
    summed = jnp.zeros((TOKENS, D), f32)
    for member in range(N_TP):
        left = proj_grad[:, :, member * block:(member + 1) * block].reshape(TOKENS, 3 * block)
        right = proj_weight[:, :, member * block:(member + 1) * block].reshape(D, 3 * block)
        partial_value = jnp.dot(left, right.T, preferred_element_type=f32).astype(bf16)
        summed = summed + lax.optimization_barrier(partial_value).astype(f32)
    tokens_grad = summed.astype(bf16)

    scale = TOKENS ** -0.5

    def filter_column(index):
        shifted = lax.dynamic_slice_in_dim(gated_pad, TAPS - index, TOKENS, 0)
        return jnp.sum(mixed_f * shifted, 0)

    filter_grad = lax.map(filter_column, jnp.arange(TAPS, dtype=jnp.int32)).T * scale
    skip_grad = jnp.sum(mixed_f * gated_f, 0) * scale
    return (filtered, tokens_grad, filter_grad, skip_grad)
```

```python
import numpy as np
import jax
import jax.numpy as jnp
from jax import lax
from jax.sharding import PartitionSpec as P


def passed_along(x, axis, by):
    peers = lax.axis_size(axis)
    pairs = [(i, i + by) for i in range(peers) if 0 <= i + by < peers]
    return lax.ppermute(x, axis, pairs)


def transforms(taps):
    k = np.arange(taps)[:, None]
    n = np.arange(2 * taps)[None, :]
    angle = np.pi * (2 * k + 1) * n / (2 * taps)
    forward = np.concatenate([np.cos(angle), -np.sin(angle)], 0)
    inverse = np.concatenate([np.cos(angle), -np.sin(angle)], 0).T / taps
    return forward[:, :taps].astype(np.float32), inverse.astype(np.float32)


def split_bf16(m):
    hi = jnp.asarray(m).astype(jnp.bfloat16)
    return hi, (jnp.asarray(m) - hi.astype(jnp.float32)).astype(jnp.bfloat16)


def mm(a, b):
    return jnp.dot(a, b, preferred_element_type=jnp.float32)


def shards(tokens, proj_weight, filter_taps, skip_gain, out_grad):
    f32 = jnp.float32
    bf16 = jnp.bfloat16
    taps = filter_taps.shape[1]
    width = filter_taps.shape[0]
    rows = out_grad.shape[0]
    blocks = rows // taps
    forward, inverse = transforms(taps)
    slab = lax.all_gather(tokens, "tp", axis=0, tiled=True)
    piece = lax.all_gather(proj_weight.reshape(-1, 3 * width), "ctx", axis=0, tiled=True)
    projected = jnp.dot(slab, piece, preferred_element_type=f32).astype(bf16)
    query, key, value = (projected[:, i * width : (i + 1) * width].astype(f32) for i in range(3))
    grad = out_grad.astype(f32)
    gated = (key * value).astype(bf16)
    mixed_grad = (grad * query).astype(bf16)
    gated_f = gated.astype(f32)
    mixed_f = mixed_grad.astype(f32)
    earlier = passed_along(gated[rows - taps :], "ctx", 1)
    later = passed_along(mixed_grad[:taps], "ctx", -1)
    ext_g = jnp.concatenate([earlier, gated], 0).reshape(blocks + 1, taps, width)
    ext_m = jnp.concatenate([mixed_grad, later], 0).reshape(blocks + 1, taps, width)
    f_hi, f_lo = split_bf16(forward)
    i_hi, i_lo = split_bf16(inverse)
    spectrum = jnp.dot(jnp.asarray(forward), filter_taps.T, precision=lax.Precision.HIGHEST)
    hr, hi = spectrum[:taps], spectrum[taps:]
    sign = jnp.asarray(np.where(np.arange(taps) % 2 == 0, 1.0, -1.0).astype(np.float32))[:, None]

    def analyse(x):
        out = jnp.einsum("kn,bnc->bkc", f_hi, x, preferred_element_type=f32)
        return out + jnp.einsum("kn,bnc->bkc", f_lo, x, preferred_element_type=f32)

    def rot(re, im):
        return sign * im, -sign * re

    def synth(re, im, part):
        m_hi = i_hi[part * taps : (part + 1) * taps]
        m_lo = i_lo[part * taps : (part + 1) * taps]
        y = jnp.concatenate([re, im], -2)
        y_hi, y_lo = split_bf16(y)
        out = jnp.einsum("nk,...kc->...nc", m_hi, y_hi, preferred_element_type=f32)
        out = out + jnp.einsum("nk,...kc->...nc", m_lo, y_hi, preferred_element_type=f32)
        return out + jnp.einsum("nk,...kc->...nc", m_hi, y_lo, preferred_element_type=f32)

    v = analyse(ext_g)
    u = analyse(ext_m)
    vr, vi, ur, ui = v[:, :taps], v[:, taps:], u[:, :taps], u[:, taps:]
    rr, ri = rot(vr[1:], vi[1:])
    xr, xi = vr[:-1] + rr, vi[:-1] + ri
    rr, ri = rot(ur[1:], ui[1:])
    mr, mi = ur[:-1] + rr, ui[:-1] + ri
    dr, di = rot(ur[:-1], ui[:-1])
    mixed = synth(hr * xr - hi * xi, hr * xi + hi * xr, 1).reshape(rows, width) + skip_gain[None, :] * gated_f
    gated_grad = synth(hr * mr + hi * mi, hr * mi - hi * mr, 0).reshape(rows, width) + skip_gain[None, :] * mixed_f
    filter_local = synth(jnp.sum(xr * dr + xi * di, 0), jnp.sum(xr * di - xi * dr, 0), 0)
    skip_local = jnp.sum(mixed_f * gated_f, 0)
    filtered = (query * mixed).astype(bf16)
    proj_grad = jnp.concatenate([grad * mixed, gated_grad * value, gated_grad * key], 1).astype(bf16)
    peers = lax.axis_size("ctx")
    both = jnp.concatenate([filter_local, jnp.broadcast_to(skip_local, (taps, width))], 0)
    both = both.reshape(2 * taps // 8, 8, width)
    both = lax.all_to_all(both.reshape(peers, -1, width), "ctx", 0, 0, tiled=False)
    both = lax.all_gather(jnp.sum(both, 0), "ctx", axis=0, tiled=True)
    scale = (rows * peers) ** (-0.5)
    terms = lax.dot_general(proj_grad, piece, (((1,), (1,)), ((), ())), preferred_element_type=f32)
    tokens_grad = lax.psum_scatter(terms.astype(bf16), "tp", scatter_dimension=0, tiled=True)
    return (filtered, tokens_grad.astype(bf16), both[:taps].T * scale, both[taps] * scale)


def solution(mesh):
    placed = (P(("ctx", "tp"), None), P("ctx", None, "tp"), P("tp", None), P("tp"), P("ctx", "tp"))
    return jax.shard_map(
        shards,
        mesh=mesh,
        in_specs=placed,
        out_specs=(P("ctx", "tp"), P(("ctx", "tp"), None), P("tp", None), P("tp")),
        check_vma=False,
    )
```

```python
import functools

import numpy as np
import jax
import jax.numpy as jnp
from jax import lax
from jax.experimental import pallas as pl
from jax.experimental.pallas import tpu as pltpu
from jax.sharding import PartitionSpec as P

MESH = pl.DeviceIdType.MESH
F32 = jnp.float32
BF16 = jnp.bfloat16
TAPS = 128
LANES = 128
BLOCKS = 4
GROUPS = 4
NZ, NX, NH = 4, 4, 2


def transforms():
    k = np.arange(TAPS)[:, None]
    n = np.arange(2 * TAPS)[None, :]
    angle = np.pi * (2 * k + 1) * n / (2 * TAPS)
    both = np.concatenate([np.cos(angle), -np.sin(angle)], 0)
    return both[:, :TAPS].astype(np.float32), (both.T / TAPS).astype(np.float32)


def split_bf16(m):
    hi = m.astype(BF16)
    return hi, (m - hi.astype(F32)).astype(BF16)


def dot(a, b):
    return jnp.dot(a, b, preferred_element_type=F32)


def dot_nt(a, b):
    return lax.dot_general(a, b, (((1,), (1,)), ((), ())), preferred_element_type=F32)


def kernel(
    tokens, w_in, taps, skip, og, f_hi, f_lo, i_hi, i_lo,
    filt, tgrad, fgrad,
    wbuf, slab, acc, pacc, qkv, pg, gbuf, mbuf, hg, hm, vs, us, hs,
    fgbuf, zrecv, s1, xrecv, s2, hrecv,
    ps1, pr1, ps2, pr2, ps3, pr3,
    loc_sem, p0_send, p0_recv, ring_send, ring_recv, tok_send, tok_recv, halo_send, halo_recv,
    rs_send, rs_recv, ar_send, ar_recv,
):
    ctx = lax.axis_index("ctx")
    tp = lax.axis_index("tp")
    n_ctx = NZ * NX * NH
    z, x, h = ctx // (NX * NH), (ctx // NH) % NX, ctx % NH
    a, b = tp // 2, tp % 2

    def at(zz, xx, hh):
        return {"ctx": (zz * NX + xx) * NH + hh, "tp": tp}

    def turn(v, by):
        return (v + by + 4) % 4

    sibling = {"ctx": ctx, "tp": 2 * a + 1 - b}
    across = {"ctx": ctx, "tp": 2 * (1 - a) + b}
    after = {"ctx": (ctx + 1) % n_ctx, "tp": tp}
    before = {"ctx": (ctx + n_ctx - 1) % n_ctx, "tp": tp}
    h_peer = at(z, x, 1 - h)
    z_peer = [None] + [at(turn(z, d), x, h) for d in (1, 2, 3)]
    x_peer = [None] + [at(z, turn(x, d), h) for d in (1, 2, 3)]

    barrier = pltpu.get_barrier_semaphore()
    greeted = [sibling, across, after, before, h_peer] + z_peer[1:] + x_peer[1:]
    for peer in greeted:
        pl.semaphore_signal(barrier, inc=1, device_id=peer, device_id_type=MESH)
    pl.semaphore_wait(barrier, len(greeted))

    def remote(src, dst, send, recv, peer):
        return pltpu.make_async_remote_copy(
            src_ref=src, dst_ref=dst, send_sem=send, recv_sem=recv, device_id=peer, device_id_type=MESH
        )

    def p0(g):
        return remote(w_in.at[g], wbuf.at[g, z, x, h], p0_send.at[g], p0_recv.at[g], h_peer)

    def own(g):
        return pltpu.make_async_copy(w_in.at[g], wbuf.at[g, z, x, h], loc_sem.at[g])

    def ring(g, phase, half, way, sender):
        step = -1 if way == 0 else 1
        along_x = (half == 0) == (phase < 2)
        zz, xx = z, x
        if along_x:
            xx = turn(x, sender)
            if phase in (1, 3):
                xx = turn(xx, step)
        else:
            zz = turn(z, sender)
            if phase in (1, 3):
                zz = turn(zz, step)
        part = wbuf.at[g]
        if phase == 0:
            ref = part.at[zz, xx, :, half]
        elif phase == 1:
            ref = part.at[zz, xx, way, half]
        elif phase == 2:
            ref = part.at[:, xx, :, half] if along_x else part.at[zz, :, :, half]
        else:
            ref = part.at[:, xx, way, half] if along_x else part.at[zz, :, way, half]
        peer = (x_peer if along_x else z_peer)[1 if way == 0 else 3]
        slot = ((g * 4 + phase) * 2 + half) * 2 + way
        return remote(ref, ref, ring_send.at[slot], ring_recv.at[slot], peer)

    def start_ring(g, phase):
        for half in (0, 1):
            for way in (0, 1):
                ring(g, phase, half, way, 0).start()

    def wait_ring(g, phase):
        for half in (0, 1):
            for way in (0, 1):
                ring(g, phase, half, way, -1 if way == 0 else 1).wait_recv()

    def token_copy(which):
        mine = slab.at[tp]
        far = slab.at[2 * (1 - a) + b]
        if which == 0:
            return remote(tokens, mine, tok_send.at[0], tok_recv.at[0], sibling)
        if which == 1:
            return remote(tokens, mine, tok_send.at[1], tok_recv.at[1], across)
        return remote(far, far, tok_send.at[2], tok_recv.at[2], sibling)

    def token_landed(which):
        ref = slab.at[(2 * a + 1 - b, 2 * (1 - a) + b, 2 * (1 - a) + 1 - b)[which]]
        return remote(ref, ref, tok_send.at[which], tok_recv.at[which], sibling)

    p0(0).start()
    for g in range(GROUPS):
        own(g).start()
    p0(1).start()
    token_copy(1).start()
    token_copy(0).start()
    tokens_own = pltpu.make_async_copy(tokens, slab.at[tp], loc_sem.at[GROUPS])
    tokens_own.start()
    p0(2).start()
    p0(3).start()

    def land_p0(g):
        own(g).wait()
        wref = wbuf.at[g, z, x, 1 - h]
        remote(wref, wref, p0_send.at[g], p0_recv.at[g], h_peer).wait_recv()

    land_p0(0)
    start_ring(0, 0)
    wait_ring(0, 0)
    start_ring(0, 1)
    wait_ring(0, 1)
    start_ring(0, 2)

    def filter_spectrum(g, carry):
        t_hi, t_lo = split_bf16(taps[pl.ds(g * LANES, LANES), :])
        hs[g] = dot_nt(f_hi[...], t_hi) + (dot_nt(f_hi[...], t_lo) + dot_nt(f_lo[...], t_hi))
        return carry

    lax.fori_loop(0, GROUPS, filter_spectrum, 0)

    def clear(i, carry):
        acc[pl.ds(i * 64, 64), :] = jnp.zeros((64, acc.shape[1]), F32)
        return carry

    lax.fori_loop(0, acc.shape[0] // 64, clear, 0)
    depth = NX * NH * TAPS

    def halo_up(g, ref):
        return remote(ref, hg.at[g], halo_send.at[g], halo_recv.at[g], after)

    def halo_down(g, ref):
        return remote(ref, hm.at[g], halo_send.at[GROUPS + g], halo_recv.at[GROUPS + g], before)

    def compute(g):
        pacc[...] = jnp.zeros_like(pacc)

        def project(zz, carry):
            w = wbuf[g, zz].reshape(depth, 3 * LANES)
            s = slab[:, :, pl.ds(pl.multiple_of(zz * depth, depth), depth)].reshape(BLOCKS * TAPS, depth)
            pacc[...] += dot(s, w)
            return carry

        lax.fori_loop(0, NZ, project, 0)
        cols = pl.ds(pl.multiple_of(g * LANES, LANES), LANES)
        qkv[...] = pacc[...].astype(BF16)
        q = qkv[:, :LANES].astype(F32)
        k = qkv[:, LANES : 2 * LANES].astype(F32)
        v = qkv[:, 2 * LANES :].astype(F32)
        gbuf[...] = (k * v).astype(BF16).reshape(BLOCKS, TAPS, LANES)
        mbuf[...] = (og[:, cols].astype(F32) * q).astype(BF16).reshape(BLOCKS, TAPS, LANES)
        up, down = halo_up(g, gbuf.at[BLOCKS - 1]), halo_down(g, mbuf.at[0])
        up.start()
        down.start()
        for i in range(BLOCKS):
            vs[i + 1] = dot(f_hi[...], gbuf[i])
            us[i] = dot(f_hi[...], mbuf[i])
        up.wait()
        down.wait()
        zero = jnp.zeros((TAPS, LANES), BF16)
        vs[0] = dot(f_hi[...], jnp.where(ctx == 0, zero, hg[g]))
        us[BLOCKS] = dot(f_hi[...], jnp.where(ctx == n_ctx - 1, zero, hm[g]))
        sign = 1.0 - 2.0 * (lax.broadcasted_iota(jnp.int32, (TAPS, LANES), 0) % 2).astype(F32)
        hr, hi = hs[g, :TAPS], hs[g, TAPS:]
        gain = skip[:, cols]
        cr = jnp.zeros((TAPS, LANES), F32)
        ci = jnp.zeros((TAPS, LANES), F32)
        direct = jnp.zeros((1, LANES), F32)
        for i in range(BLOCKS):
            rows = slice(i * TAPS, (i + 1) * TAPS)
            xr = vs[i, :TAPS] + sign * vs[i + 1, TAPS:]
            xi = vs[i, TAPS:] - sign * vs[i + 1, :TAPS]
            mr = us[i, :TAPS] + sign * us[i + 1, TAPS:]
            mi = us[i, TAPS:] - sign * us[i + 1, :TAPS]
            dr = sign * us[i, TAPS:]
            di = -sign * us[i, :TAPS]
            cr = cr + (dr * xr + di * xi)
            ci = ci + (di * xr - dr * xi)
            y = jnp.concatenate([hr * xr - hi * xi, hr * xi + hi * xr], 0).astype(BF16)
            w = jnp.concatenate([hr * mr + hi * mi, hr * mi - hi * mr], 0).astype(BF16)
            gf, mf = gbuf[i].astype(F32), mbuf[i].astype(F32)
            mixed = dot(i_hi[TAPS:, :], y) + gain * gf
            back = dot(i_hi[:TAPS, :], w) + gain * mf
            direct = direct + jnp.sum(gf * mf, 0, keepdims=True)
            qb = qkv[rows, :LANES].astype(F32)
            kb = qkv[rows, LANES : 2 * LANES].astype(F32)
            vb = qkv[rows, 2 * LANES :].astype(F32)
            filt[rows, cols] = (qb * mixed).astype(BF16)
            pg[rows, :LANES] = (og[rows, cols].astype(F32) * mixed).astype(BF16)
            pg[rows, LANES : 2 * LANES] = (back * vb).astype(BF16)
            pg[rows, 2 * LANES :] = (back * kb).astype(BF16)
        c_hi, c_lo = split_bf16(jnp.concatenate([cr, ci], 0))
        i_top = i_hi[:TAPS, :]
        part = dot(i_top, c_hi) + (dot(i_top, c_lo) + dot(i_lo[:TAPS, :], c_hi))
        first = lax.broadcasted_iota(jnp.int32, (TAPS, LANES), 0) == 0
        fgbuf[:, cols] = jnp.where(first, direct, part)

    def add_terms(g, zz):
        for xx in range(NX):
            w = wbuf[g, zz, xx].reshape(NH * TAPS, 3 * LANES)
            at_cols = pl.ds(pl.multiple_of(zz * depth + xx * NH * TAPS, NH * TAPS), NH * TAPS)
            acc[:, at_cols] += dot_nt(pg[...], w)

    def group(g, carry):
        @pl.when(g < GROUPS - 1)
        def _():
            land_p0(g + 1)
            start_ring(g + 1, 0)

        wait_ring(g, 2)
        start_ring(g, 3)

        @pl.when(g < GROUPS - 1)
        def _():
            wait_ring(g + 1, 0)
            start_ring(g + 1, 1)
            wait_ring(g + 1, 1)
            start_ring(g + 1, 2)

        @pl.when(g == 0)
        def _():
            token_landed(1).wait_recv()
            token_copy(2).start()
            tokens_own.wait()
            token_landed(0).wait_recv()
            token_landed(2).wait_recv()

        wait_ring(g, 3)
        compute(g)

        @pl.when(g < GROUPS - 1)
        def _():
            def step(zz, carry):
                add_terms(g, zz)
                return carry

            lax.fori_loop(0, NZ, step, 0)

        return carry

    lax.fori_loop(0, GROUPS, group, 0)

    def ar(slot, src, dst, peer):
        return remote(src, dst, ar_send.at[slot], ar_recv.at[slot], peer)

    z_out = [ar(d - 1, fgbuf.at[pl.ds(turn(z, d) * 32, 32), :], zrecv.at[d - 1], z_peer[d]) for d in (1, 2, 3)]
    for c in z_out:
        c.start()

    def rows_of(t):
        return pl.ds(pl.multiple_of(t * TAPS, TAPS), TAPS)

    mine, near = rows_of(tp), rows_of(2 * a + 1 - b)
    far, far_near = rows_of(2 * (1 - a) + b), rows_of(2 * (1 - a) + 1 - b)

    def rs(kind, zz, src, dst, peer):
        slot = kind * NZ + zz
        return remote(src.at[zz], dst.at[zz], rs_send.at[slot], rs_recv.at[slot], peer)

    def tail(zz, carry):
        @pl.when(zz < NZ)
        def _():
            add_terms(GROUPS - 1, zz)
            at_cols = pl.ds(pl.multiple_of(zz * depth, depth), depth)
            ps1[zz] = acc[far_near, at_cols].astype(BF16)
            rs(0, zz, ps1, pr1, sibling).start()
            ps3[zz] = acc[near, at_cols].astype(BF16)
            rs(2, zz, ps3, pr3, sibling).start()

        @pl.when(zz > 0)
        def _():
            prev = zz - 1
            rs(0, prev, ps1, pr1, sibling).wait_recv()
            at_cols = pl.ds(pl.multiple_of(prev * depth, depth), depth)
            ps2[prev] = (acc[far, at_cols] + pr1[prev].astype(F32)).astype(BF16)
            rs(1, prev, ps2, pr2, across).start()

        return carry

    lax.fori_loop(0, NZ + 1, tail, 0)

    for c in z_out:
        c.wait_recv()
    s1[...] = fgbuf[pl.ds(pl.multiple_of(z * 32, 32), 32), :] + zrecv[0] + zrecv[1] + zrecv[2]
    x_out = [ar(2 + d, s1.at[pl.ds(turn(x, d) * 8, 8), :], xrecv.at[d - 1], x_peer[d]) for d in (1, 2, 3)]
    for c in x_out:
        c.start()
    for c in x_out:
        c.wait_recv()
    s2[...] = s1[pl.ds(pl.multiple_of(x * 8, 8), 8), :] + xrecv[0] + xrecv[1] + xrecv[2]
    width = s2.shape[1] // 2
    h_out = ar(6, s2.at[:, pl.ds(pl.multiple_of((1 - h) * width, width), width)], hrecv, h_peer)
    h_out.start()
    h_out.wait_recv()
    scale = (BLOCKS * TAPS * n_ctx) ** (-0.5)
    part8 = pl.ds(pl.multiple_of(z * 32 + x * 8, 8), 8)
    here = pl.ds(pl.multiple_of(h * width, width), width)
    there = pl.ds(pl.multiple_of((1 - h) * width, width), width)
    fgrad[part8, here] = (s2[:, here] + hrecv[...]) * scale
    h_back = ar(7, fgrad.at[part8, here], fgrad.at[part8, here], h_peer)
    h_back.start()
    ar(7, fgrad.at[part8, there], fgrad.at[part8, there], h_peer).wait_recv()
    x_back = [ar(7 + d, fgrad.at[part8, :], fgrad.at[part8, :], x_peer[d]) for d in (1, 2, 3)]
    for c in x_back:
        c.start()
    for d in (1, 2, 3):
        got = fgrad.at[pl.ds(pl.multiple_of(z * 32 + turn(x, -d) * 8, 8), 8), :]
        ar(7 + d, got, got, x_peer[d]).wait_recv()
    part32 = pl.ds(pl.multiple_of(z * 32, 32), 32)
    z_back = [ar(10 + d, fgrad.at[part32, :], fgrad.at[part32, :], z_peer[d]) for d in (1, 2, 3)]
    for c in z_back:
        c.start()
    for d in (1, 2, 3):
        got = fgrad.at[pl.ds(pl.multiple_of(turn(z, -d) * 32, 32), 32), :]
        ar(10 + d, got, got, z_peer[d]).wait_recv()

    def finish(zz, carry):
        rs(2, zz, ps3, pr3, sibling).wait_recv()
        rs(1, zz, ps2, pr2, across).wait_recv()
        at_cols = pl.ds(pl.multiple_of(zz * depth, depth), depth)
        total = acc[mine, at_cols] + pr3[zz].astype(F32) + pr2[zz].astype(F32)
        tgrad[:, at_cols] = total.astype(BF16)
        return carry

    lax.fori_loop(0, NZ, finish, 0)

    def drain(g, carry):
        p0(g).wait_send()
        for phase in range(4):
            for half in (0, 1):
                for way in (0, 1):
                    ring(g, phase, half, way, 0).wait_send()
        rs(0, g, ps1, pr1, sibling).wait_send()
        rs(1, g, ps2, pr2, across).wait_send()
        rs(2, g, ps3, pr3, sibling).wait_send()
        return carry

    lax.fori_loop(0, GROUPS, drain, 0)
    for which in range(3):
        token_copy(which).wait_send()
    for c in z_out + x_out + [h_out, h_back] + x_back + z_back:
        c.wait_send()


def shards(tokens, proj_weight, filter_taps, skip_gain, out_grad):
    rows, width = out_grad.shape
    depth = tokens.shape[1]
    forward, inverse = transforms()
    f_hi, f_lo = split_bf16(jnp.asarray(forward))
    i_hi, i_lo = split_bf16(jnp.asarray(inverse))
    w_in = proj_weight.reshape(2, 64, 3, GROUPS, LANES).transpose(3, 0, 1, 2, 4)
    w_in = w_in.reshape(GROUPS, 2, 64, 3 * LANES)
    vmem = pl.BlockSpec(memory_space=pltpu.VMEM)
    hbm = pl.BlockSpec(memory_space=pl.ANY)
    sem = pltpu.SemaphoreType.DMA
    V = pltpu.VMEM
    chunk = depth // NZ
    filtered, tokens_grad, filter_total = pl.pallas_call(
        kernel,
        out_shape=(
            jax.ShapeDtypeStruct((rows, width), BF16),
            jax.ShapeDtypeStruct((TAPS, depth), BF16),
            jax.ShapeDtypeStruct((TAPS, width), F32),
        ),
        in_specs=[hbm, hbm] + [vmem] * 7,
        out_specs=(vmem, vmem, vmem),
        scratch_shapes=[
            V((GROUPS, NZ, NX, NH, 2, 64, 3 * LANES), BF16),
            V((BLOCKS, TAPS, depth), BF16),
            V((rows, depth), F32),
            V((rows, 3 * LANES), F32),
            V((rows, 3 * LANES), BF16),
            V((rows, 3 * LANES), BF16),
            V((BLOCKS, TAPS, LANES), BF16),
            V((BLOCKS, TAPS, LANES), BF16),
            V((GROUPS, TAPS, LANES), BF16),
            V((GROUPS, TAPS, LANES), BF16),
            V((BLOCKS + 1, 2 * TAPS, LANES), F32),
            V((BLOCKS + 1, 2 * TAPS, LANES), F32),
            V((GROUPS, 2 * TAPS, LANES), F32),
            V((TAPS, width), F32),
            V((3, 32, width), F32),
            V((32, width), F32),
            V((3, 8, width), F32),
            V((8, width), F32),
            V((8, width // 2), F32),
        ]
        + [V((NZ, TAPS, chunk), BF16)] * 6
        + [
            sem((GROUPS + 1,)),
            sem((GROUPS,)),
            sem((GROUPS,)),
            sem((GROUPS * 16,)),
            sem((GROUPS * 16,)),
            sem((3,)),
            sem((3,)),
            sem((2 * GROUPS,)),
            sem((2 * GROUPS,)),
            sem((3 * NZ,)),
            sem((3 * NZ,)),
            sem((14,)),
            sem((14,)),
        ],
        compiler_params=pltpu.CompilerParams(
            collective_id=0, has_side_effects=True, vmem_limit_bytes=58 * 2**20
        ),
    )(tokens, w_in, filter_taps, skip_gain[None, :], out_grad, f_hi, f_lo, i_hi, i_lo)
    return filtered, tokens_grad, filter_total.T, filter_total[0]


def solution(mesh):
    placed = (P(("ctx", "tp"), None), P("ctx", None, "tp"), P("tp", None), P("tp"), P("ctx", "tp"))
    return jax.shard_map(
        shards,
        mesh=mesh,
        in_specs=placed,
        out_specs=(P("ctx", "tp"), P(("ctx", "tp"), None), P("tp", None), P("tp")),
        check_vma=False,
    )
```

```python
import functools

import numpy as np
import jax
import jax.numpy as jnp
from jax import lax
from jax.experimental import pallas as pl
from jax.experimental.pallas import tpu as pltpu
from jax.sharding import PartitionSpec as P

MESH = pl.DeviceIdType.MESH
F32 = jnp.float32
BF16 = jnp.bfloat16
TAPS = 128
LANES = 128
BLOCKS = 4
GROUPS = 4
NZ, NX, NH = 4, 4, 2


def transforms():
    k = np.arange(TAPS)[:, None]
    n = np.arange(2 * TAPS)[None, :]
    angle = np.pi * (2 * k + 1) * n / (2 * TAPS)
    both = np.concatenate([np.cos(angle), -np.sin(angle)], 0)
    return both[:, :TAPS].astype(np.float32), (both.T / TAPS).astype(np.float32)


def split_bf16(m):
    hi = m.astype(BF16)
    return hi, (m - hi.astype(F32)).astype(BF16)


def dot(a, b):
    return jnp.dot(a, b, preferred_element_type=F32)


def dot_nt(a, b):
    return lax.dot_general(a, b, (((1,), (1,)), ((), ())), preferred_element_type=F32)


def kernel(
    tokens, w_in, taps, skip, og, f_hi, f_lo, i_hi, i_lo,
    filt, tgrad, fgrad,
    wbuf, slab, acc, pacc, qkv, pg, gbuf, mbuf, hg, hm, vs, us, hs,
    fgmine, fgother, fgbuf, zrecv, s1, xrecv,
    ps1, pr1, ps2, pr2, ps3, pr3,
    loc_sem, p0_send, p0_recv, ring_send, ring_recv, tok_send, tok_recv, halo_send, halo_recv,
    rs_send, rs_recv, ar_send, ar_recv,
):
    ctx = lax.axis_index("ctx")
    tp = lax.axis_index("tp")
    n_ctx = NZ * NX * NH
    z, x, h = ctx // (NX * NH), (ctx // NH) % NX, ctx % NH
    a, b = tp // 2, tp % 2

    def at(zz, xx, hh):
        return {"ctx": (zz * NX + xx) * NH + hh, "tp": tp}

    def turn(v, by):
        return (v + by + 4) % 4

    sibling = {"ctx": ctx, "tp": 2 * a + 1 - b}
    across = {"ctx": ctx, "tp": 2 * (1 - a) + b}
    after = {"ctx": (ctx + 1) % n_ctx, "tp": tp}
    before = {"ctx": (ctx + n_ctx - 1) % n_ctx, "tp": tp}
    h_peer = at(z, x, 1 - h)
    z_peer = [None] + [at(turn(z, d), x, h) for d in (1, 2, 3)]
    x_peer = [None] + [at(z, turn(x, d), h) for d in (1, 2, 3)]

    barrier = pltpu.get_barrier_semaphore()
    greeted = [sibling, across, after, before, h_peer] + z_peer[1:] + x_peer[1:]
    for peer in greeted:
        pl.semaphore_signal(barrier, inc=1, device_id=peer, device_id_type=MESH)

    def remote(src, dst, send, recv, peer):
        return pltpu.make_async_remote_copy(
            src_ref=src, dst_ref=dst, send_sem=send, recv_sem=recv, device_id=peer, device_id_type=MESH
        )

    def p0(g):
        block = wbuf.at[g, z, x, h]
        return remote(block, block, p0_send.at[g], p0_recv.at[g], h_peer)

    def start_own(g):
        for i in range(3):
            for half in (0, 1):
                pltpu.make_async_copy(
                    w_in.at[i, pl.ds(half * 64, 64), pl.ds(g * LANES, LANES)],
                    wbuf.at[g, z, x, h, half, :, pl.ds(i * LANES, LANES)],
                    loc_sem.at[g],
                ).start()

    def wait_own(g):
        block = wbuf.at[g, z, x, h]
        pltpu.make_async_copy(block, block, loc_sem.at[g]).wait()

    def ring(g, phase, half, way, sender):
        step = -1 if way == 0 else 1
        along_x = (half == 0) == (phase < 2)
        zz, xx = z, x
        if along_x:
            xx = turn(x, sender)
            if phase in (1, 3):
                xx = turn(xx, step)
        else:
            zz = turn(z, sender)
            if phase in (1, 3):
                zz = turn(zz, step)
        part = wbuf.at[g]
        if phase == 0:
            ref = part.at[zz, xx, :, half]
        elif phase == 1:
            ref = part.at[zz, xx, way, half]
        elif phase == 2:
            ref = part.at[:, xx, :, half] if along_x else part.at[zz, :, :, half]
        else:
            ref = part.at[:, xx, way, half] if along_x else part.at[zz, :, way, half]
        peer = (x_peer if along_x else z_peer)[1 if way == 0 else 3]
        slot = ((g * 4 + phase) * 2 + half) * 2 + way
        return remote(ref, ref, ring_send.at[slot], ring_recv.at[slot], peer)

    def start_ring(g, phase):
        for half in (0, 1):
            for way in (0, 1):
                ring(g, phase, half, way, 0).start()

    def wait_ring(g, phase):
        for half in (0, 1):
            for way in (0, 1):
                ring(g, phase, half, way, -1 if way == 0 else 1).wait_recv()

    def token_copy(which):
        mine = slab.at[tp]
        far = slab.at[2 * (1 - a) + b]
        if which == 0:
            return remote(tokens, mine, tok_send.at[0], tok_recv.at[0], sibling)
        if which == 1:
            return remote(tokens, mine, tok_send.at[1], tok_recv.at[1], across)
        return remote(far, far, tok_send.at[2], tok_recv.at[2], sibling)

    def token_landed(which):
        ref = slab.at[(2 * a + 1 - b, 2 * (1 - a) + b, 2 * (1 - a) + 1 - b)[which]]
        return remote(ref, ref, tok_send.at[which], tok_recv.at[which], sibling)

    for g in range(GROUPS):
        start_own(g)
    tokens_own = pltpu.make_async_copy(tokens, slab.at[tp], loc_sem.at[GROUPS])
    tokens_own.start()
    pl.semaphore_wait(barrier, len(greeted))
    for g in range(GROUPS):
        wait_own(g)
        p0(g).start()
    token_copy(1).start()
    token_copy(0).start()

    def land_p0(g):
        block = wbuf.at[g, z, x, 1 - h]
        remote(block, block, p0_send.at[g], p0_recv.at[g], h_peer).wait_recv()

    def first_axis(g, carry):
        land_p0(g)
        start_ring(g, 0)
        return carry

    def first_axis_on(g, carry):
        wait_ring(g, 0)
        start_ring(g, 1)
        return carry

    def second_axis(g, carry):
        wait_ring(g, 1)

        @pl.when(g < 2)
        def _():
            start_ring(g, 2)

        return carry

    lax.fori_loop(0, GROUPS, first_axis, 0)
    lax.fori_loop(0, GROUPS, first_axis_on, 0)
    lax.fori_loop(0, GROUPS, second_axis, 0)

    def filter_spectrum(g, carry):
        t_hi, t_lo = split_bf16(taps[pl.ds(g * LANES, LANES), :])
        hs[g] = dot_nt(f_hi[...], t_hi) + (dot_nt(f_hi[...], t_lo) + dot_nt(f_lo[...], t_hi))
        return carry

    lax.fori_loop(0, GROUPS, filter_spectrum, 0)

    def clear(i, carry):
        acc[pl.ds(i * 64, 64), :] = jnp.zeros((64, acc.shape[1]), F32)
        return carry

    lax.fori_loop(0, acc.shape[0] // 64, clear, 0)
    depth = NX * NH * TAPS
    wait_ring(0, 2)
    start_ring(0, 3)
    start_ring(2, 2)

    def halo_up(g):
        return remote(gbuf.at[g, BLOCKS - 1], hg.at[g], halo_send.at[g], halo_recv.at[g], after)

    def halo_down(g):
        return remote(mbuf.at[g, 0], hm.at[g], halo_send.at[GROUPS + g], halo_recv.at[GROUPS + g], before)

    def ar_h(g):
        return remote(fgmine.at[g], fgother.at[g], ar_send.at[g], ar_recv.at[g], h_peer)

    def stage_1(g):
        pacc[...] = jnp.zeros_like(pacc)

        def project(zz, carry):
            w = wbuf[g, zz].reshape(depth, 3 * LANES)
            s = slab[:, :, pl.ds(pl.multiple_of(zz * depth, depth), depth)].reshape(BLOCKS * TAPS, depth)
            pacc[...] += dot(s, w)
            return carry

        lax.fori_loop(0, NZ, project, 0)
        cols = pl.ds(pl.multiple_of(g * LANES, LANES), LANES)
        qkv[g] = pacc[...].astype(BF16)
        q = qkv[g, :, :LANES].astype(F32)
        k = qkv[g, :, LANES : 2 * LANES].astype(F32)
        v = qkv[g, :, 2 * LANES :].astype(F32)
        gbuf[g] = (k * v).astype(BF16).reshape(BLOCKS, TAPS, LANES)
        mbuf[g] = (og[:, cols].astype(F32) * q).astype(BF16).reshape(BLOCKS, TAPS, LANES)
        halo_up(g).start()
        halo_down(g).start()

    def stage_2(g):
        cols = pl.ds(pl.multiple_of(g * LANES, LANES), LANES)
        for i in range(BLOCKS):
            vs[i + 1] = dot(f_hi[...], gbuf[g, i])
            us[i] = dot(f_hi[...], mbuf[g, i])
        halo_up(g).wait_recv()
        halo_down(g).wait_recv()
        zero = jnp.zeros((TAPS, LANES), BF16)
        vs[0] = dot(f_hi[...], jnp.where(ctx == 0, zero, hg[g]))
        us[BLOCKS] = dot(f_hi[...], jnp.where(ctx == n_ctx - 1, zero, hm[g]))
        sign = 1.0 - 2.0 * (lax.broadcasted_iota(jnp.int32, (TAPS, LANES), 0) % 2).astype(F32)
        hr, hi = hs[g, :TAPS], hs[g, TAPS:]
        gain = skip[:, cols]
        cr = jnp.zeros((TAPS, LANES), F32)
        ci = jnp.zeros((TAPS, LANES), F32)
        direct = jnp.zeros((1, LANES), F32)
        for i in range(BLOCKS):
            rows = slice(i * TAPS, (i + 1) * TAPS)
            xr = vs[i, :TAPS] + sign * vs[i + 1, TAPS:]
            xi = vs[i, TAPS:] - sign * vs[i + 1, :TAPS]
            mr = us[i, :TAPS] + sign * us[i + 1, TAPS:]
            mi = us[i, TAPS:] - sign * us[i + 1, :TAPS]
            dr = sign * us[i, TAPS:]
            di = -sign * us[i, :TAPS]
            cr = cr + (dr * xr + di * xi)
            ci = ci + (di * xr - dr * xi)
            y = jnp.concatenate([hr * xr - hi * xi, hr * xi + hi * xr], 0).astype(BF16)
            w = jnp.concatenate([hr * mr + hi * mi, hr * mi - hi * mr], 0).astype(BF16)
            gf, mf = gbuf[g, i].astype(F32), mbuf[g, i].astype(F32)
            mixed = dot(i_hi[TAPS:, :], y) + gain * gf
            back = dot(i_hi[:TAPS, :], w) + gain * mf
            direct = direct + jnp.sum(gf * mf, 0, keepdims=True)
            qb = qkv[g, rows, :LANES].astype(F32)
            kb = qkv[g, rows, LANES : 2 * LANES].astype(F32)
            vb = qkv[g, rows, 2 * LANES :].astype(F32)
            filt[rows, cols] = (qb * mixed).astype(BF16)
            pg[rows, :LANES] = (og[rows, cols].astype(F32) * mixed).astype(BF16)
            pg[rows, LANES : 2 * LANES] = (back * vb).astype(BF16)
            pg[rows, 2 * LANES :] = (back * kb).astype(BF16)
        c_hi, c_lo = split_bf16(jnp.concatenate([cr, ci], 0))
        i_top = i_hi[:TAPS, :]
        part = dot(i_top, c_hi) + (dot(i_top, c_lo) + dot(i_lo[:TAPS, :], c_hi))
        first = lax.broadcasted_iota(jnp.int32, (TAPS, LANES), 0) == 0
        fgmine[g] = jnp.where(first, direct, part).astype(BF16)
        ar_h(g).start()

    def add_terms(g, zz):
        for xx in range(NX):
            w = wbuf[g, zz, xx].reshape(NH * TAPS, 3 * LANES)
            at_cols = pl.ds(pl.multiple_of(zz * depth + xx * NH * TAPS, NH * TAPS), NH * TAPS)
            acc[:, at_cols] += dot_nt(pg[...], w)

    def group(g, carry):
        @pl.when(g < GROUPS - 1)
        def _():
            wait_ring(g + 1, 2)
            start_ring(g + 1, 3)

        @pl.when(g < GROUPS - 3)
        def _():
            start_ring(g + 3, 2)

        @pl.when(g == 0)
        def _():
            token_landed(1).wait_recv()
            token_copy(2).start()
            tokens_own.wait()
            token_landed(0).wait_recv()
            token_landed(2).wait_recv()

        @pl.when(g < GROUPS)
        def _():
            wait_ring(g, 3)
            stage_1(g)

        @pl.when((g > 0) & (g < GROUPS))
        def _():
            stage_2_terms(g - 1)

        return carry

    def stage_2_terms(g):
        stage_2(g)

        def step(zz, carry):
            add_terms(g, zz)
            return carry

        lax.fori_loop(0, NZ, step, 0)

    lax.fori_loop(0, GROUPS, group, 0)
    stage_2(GROUPS - 1)

    def rows_of(t):
        return pl.ds(pl.multiple_of(t * TAPS, TAPS), TAPS)

    mine, near = rows_of(tp), rows_of(2 * a + 1 - b)
    far, far_near = rows_of(2 * (1 - a) + b), rows_of(2 * (1 - a) + 1 - b)

    def rs(kind, zz, src, dst, peer):
        slot = kind * NZ + zz
        return remote(src.at[zz], dst.at[zz], rs_send.at[slot], rs_recv.at[slot], peer)

    def tail(zz, carry):
        @pl.when(zz < NZ)
        def _():
            add_terms(GROUPS - 1, zz)
            at_cols = pl.ds(pl.multiple_of(zz * depth, depth), depth)
            ps1[zz] = acc[far_near, at_cols].astype(BF16)
            rs(0, zz, ps1, pr1, sibling).start()
            ps3[zz] = acc[near, at_cols].astype(BF16)
            rs(2, zz, ps3, pr3, sibling).start()

        @pl.when(zz > 0)
        def _():
            prev = zz - 1
            rs(0, prev, ps1, pr1, sibling).wait_recv()
            at_cols = pl.ds(pl.multiple_of(prev * depth, depth), depth)
            ps2[prev] = (acc[far, at_cols] + pr1[prev].astype(F32)).astype(BF16)
            rs(1, prev, ps2, pr2, across).start()

        return carry

    lax.fori_loop(0, NZ + 1, tail, 0)

    def ar(slot, src, dst, peer):
        return remote(src, dst, ar_send.at[GROUPS + slot], ar_recv.at[GROUPS + slot], peer)

    for g in range(GROUPS):
        ar_h(g).wait_recv()
        fgbuf[:, g * LANES : (g + 1) * LANES] = fgmine[g].astype(F32) + fgother[g].astype(F32)
    z_out = [ar(d - 1, fgbuf.at[pl.ds(turn(z, d) * 32, 32), :], zrecv.at[d - 1], z_peer[d]) for d in (1, 2, 3)]
    for c in z_out:
        c.start()
    for c in z_out:
        c.wait_recv()
    s1[...] = fgbuf[pl.ds(pl.multiple_of(z * 32, 32), 32), :] + zrecv[0] + zrecv[1] + zrecv[2]
    x_out = [ar(2 + d, s1.at[pl.ds(turn(x, d) * 8, 8), :], xrecv.at[d - 1], x_peer[d]) for d in (1, 2, 3)]
    for c in x_out:
        c.start()
    for c in x_out:
        c.wait_recv()
    scale = (BLOCKS * TAPS * n_ctx) ** (-0.5)
    part8 = pl.ds(pl.multiple_of(z * 32 + x * 8, 8), 8)
    fgrad[part8, :] = (s1[pl.ds(pl.multiple_of(x * 8, 8), 8), :] + xrecv[0] + xrecv[1] + xrecv[2]) * scale
    x_back = [ar(5 + d, fgrad.at[part8, :], fgrad.at[part8, :], x_peer[d]) for d in (1, 2, 3)]
    for c in x_back:
        c.start()
    for d in (1, 2, 3):
        got = fgrad.at[pl.ds(pl.multiple_of(z * 32 + turn(x, -d) * 8, 8), 8), :]
        ar(5 + d, got, got, x_peer[d]).wait_recv()
    part32 = pl.ds(pl.multiple_of(z * 32, 32), 32)
    z_back = [ar(8 + d, fgrad.at[part32, :], fgrad.at[part32, :], z_peer[d]) for d in (1, 2, 3)]
    for c in z_back:
        c.start()
    for d in (1, 2, 3):
        got = fgrad.at[pl.ds(pl.multiple_of(turn(z, -d) * 32, 32), 32), :]
        ar(8 + d, got, got, z_peer[d]).wait_recv()

    def finish(zz, carry):
        rs(2, zz, ps3, pr3, sibling).wait_recv()
        rs(1, zz, ps2, pr2, across).wait_recv()
        at_cols = pl.ds(pl.multiple_of(zz * depth, depth), depth)
        total = acc[mine, at_cols] + pr3[zz].astype(F32) + pr2[zz].astype(F32)
        tgrad[:, at_cols] = total.astype(BF16)
        return carry

    lax.fori_loop(0, NZ, finish, 0)

    def drain(g, carry):
        p0(g).wait_send()
        halo_up(g).wait_send()
        halo_down(g).wait_send()
        ar_h(g).wait_send()
        for phase in range(4):
            for half in (0, 1):
                for way in (0, 1):
                    ring(g, phase, half, way, 0).wait_send()
        rs(0, g, ps1, pr1, sibling).wait_send()
        rs(1, g, ps2, pr2, across).wait_send()
        rs(2, g, ps3, pr3, sibling).wait_send()
        return carry

    lax.fori_loop(0, GROUPS, drain, 0)
    for which in range(3):
        token_copy(which).wait_send()
    for c in z_out + x_out + x_back + z_back:
        c.wait_send()


def hand_out(filt, tgrad, total, filt_out, tgrad_out, fgrad_out, skip_out):
    filt_out[...] = filt[...]
    tgrad_out[...] = tgrad[...]
    fgrad_out[...] = total[...].T
    skip_out[...] = total[:1, :]


def shards(tokens, proj_weight, filter_taps, skip_gain, out_grad):
    rows, width = out_grad.shape
    depth = tokens.shape[1]
    forward, inverse = transforms()
    f_hi, f_lo = split_bf16(jnp.asarray(forward))
    i_hi, i_lo = split_bf16(jnp.asarray(inverse))
    w_in = proj_weight.transpose(1, 0, 2)
    vmem = pl.BlockSpec(memory_space=pltpu.VMEM)
    hbm = pl.BlockSpec(memory_space=pl.ANY)
    sem = pltpu.SemaphoreType.DMA
    V = pltpu.VMEM
    chunk = depth // NZ
    filtered, tokens_grad, filter_total = pl.pallas_call(
        kernel,
        out_shape=(
            jax.ShapeDtypeStruct((rows, width), BF16),
            jax.ShapeDtypeStruct((TAPS, depth), BF16),
            jax.ShapeDtypeStruct((TAPS, width), F32),
        ),
        in_specs=[hbm, hbm] + [vmem] * 7,
        out_specs=(vmem, vmem, vmem),
        scratch_shapes=[
            V((GROUPS, NZ, NX, NH, 2, 64, 3 * LANES), BF16),
            V((BLOCKS, TAPS, depth), BF16),
            V((rows, depth), F32),
            V((rows, 3 * LANES), F32),
            V((GROUPS, rows, 3 * LANES), BF16),
            V((rows, 3 * LANES), BF16),
            V((GROUPS, BLOCKS, TAPS, LANES), BF16),
            V((GROUPS, BLOCKS, TAPS, LANES), BF16),
            V((GROUPS, TAPS, LANES), BF16),
            V((GROUPS, TAPS, LANES), BF16),
            V((BLOCKS + 1, 2 * TAPS, LANES), F32),
            V((BLOCKS + 1, 2 * TAPS, LANES), F32),
            V((GROUPS, 2 * TAPS, LANES), F32),
            V((GROUPS, TAPS, LANES), BF16),
            V((GROUPS, TAPS, LANES), BF16),
            V((TAPS, width), F32),
            V((3, 32, width), F32),
            V((32, width), F32),
            V((3, 8, width), F32),
        ]
        + [V((NZ, TAPS, chunk), BF16)] * 6
        + [
            sem((GROUPS + 1,)),
            sem((GROUPS,)),
            sem((GROUPS,)),
            sem((GROUPS * 16,)),
            sem((GROUPS * 16,)),
            sem((3,)),
            sem((3,)),
            sem((2 * GROUPS,)),
            sem((2 * GROUPS,)),
            sem((3 * NZ,)),
            sem((3 * NZ,)),
            sem((GROUPS + 12,)),
            sem((GROUPS + 12,)),
        ],
        compiler_params=pltpu.CompilerParams(
            collective_id=0, has_side_effects=True, vmem_limit_bytes=58 * 2**20
        ),
    )(tokens, w_in, filter_taps, skip_gain[None, :], out_grad, f_hi, f_lo, i_hi, i_lo)
    filtered, tokens_grad, filter_grad, skip_grad = pl.pallas_call(
        hand_out,
        out_shape=(
            jax.ShapeDtypeStruct((rows, width), BF16),
            jax.ShapeDtypeStruct((TAPS, depth), BF16),
            jax.ShapeDtypeStruct((width, TAPS), F32),
            jax.ShapeDtypeStruct((1, width), F32),
        ),
        in_specs=[vmem] * 3,
        out_specs=(vmem,) * 4,
    )(filtered, tokens_grad, filter_total)
    return filtered, tokens_grad, filter_grad, skip_grad[0]


def solution(mesh):
    placed = (P(("ctx", "tp"), None), P("ctx", None, "tp"), P("tp", None), P("tp"), P("ctx", "tp"))
    return jax.shard_map(
        shards,
        mesh=mesh,
        in_specs=placed,
        out_specs=(P("ctx", "tp"), P(("ctx", "tp"), None), P("tp", None), P("tp")),
        check_vma=False,
    )
```

```python
import functools

import numpy as np
import jax
import jax.numpy as jnp
from jax import lax
from jax.experimental import pallas as pl
from jax.experimental.pallas import tpu as pltpu
from jax.sharding import PartitionSpec as P

MESH = pl.DeviceIdType.MESH
F32 = jnp.float32
BF16 = jnp.bfloat16
TAPS = 128
LANES = 128
BLOCKS = 4
GROUPS = 4
NZ, NX, NH = 4, 4, 2
NEAR, ON, FIRST_HALF, SECOND_HALF, LAST = range(5)
PHASES = 5
INNER, OUTER = (1, 2), (0, 3)
CHUNKS = 8


def transforms():
    k = np.arange(TAPS)[:, None]
    n = np.arange(2 * TAPS)[None, :]
    angle = np.pi * (2 * k + 1) * n / (2 * TAPS)
    both = np.concatenate([np.cos(angle), -np.sin(angle)], 0)
    return both[:, :TAPS].astype(np.float32), (both.T / TAPS).astype(np.float32)


def split_bf16(m):
    hi = m.astype(BF16)
    return hi, (m - hi.astype(F32)).astype(BF16)


def dot(a, b):
    return jnp.dot(a, b, preferred_element_type=F32)


def dot_nt(a, b):
    return lax.dot_general(a, b, (((1,), (1,)), ((), ())), preferred_element_type=F32)


def kernel(
    tokens, w_in, taps, skip, og, f_hi, f_lo, i_hi, i_lo,
    filt, tgrad, fgrad,
    wbuf, slab, acc, pacc, qkv, pg, gbuf, mbuf, hg, hm, vs, us, hs,
    cross, straight, fgmine, fgother, fgbuf, zrecv,
    ps1, pr1, ps2, pr2, ps3, pr3,
    loc_sem, p0_send, p0_recv, ring_send, ring_recv, tok_send, tok_recv, halo_send, halo_recv,
    rs_send, rs_recv, ar_send, ar_recv,
):
    ctx = lax.axis_index("ctx")
    tp = lax.axis_index("tp")
    n_ctx = NZ * NX * NH
    z, x, h = ctx // (NX * NH), (ctx // NH) % NX, ctx % NH
    a, b = tp // 2, tp % 2

    def at(zz, xx, hh):
        return {"ctx": (zz * NX + xx) * NH + hh, "tp": tp}

    def turn(v, by):
        return (v + by + 4) % 4

    sibling = {"ctx": ctx, "tp": 2 * a + 1 - b}
    across = {"ctx": ctx, "tp": 2 * (1 - a) + b}
    far_sibling = {"ctx": ctx, "tp": 2 * (1 - a) + 1 - b}
    after = {"ctx": (ctx + 1) % n_ctx, "tp": tp}
    before = {"ctx": (ctx + n_ctx - 1) % n_ctx, "tp": tp}
    h_peer = at(z, x, 1 - h)
    z_peer = [None] + [at(turn(z, d), x, h) for d in (1, 2, 3)]
    x_peer = [None] + [at(z, turn(x, d), h) for d in (1, 2, 3)]

    barrier = pltpu.get_barrier_semaphore()
    greeted = [sibling, across, far_sibling, after, before, h_peer]
    greeted = greeted + [at(turn(z, m // NX), turn(x, m % NX), h) for m in range(1, NZ * NX)]
    for peer in greeted:
        pl.semaphore_signal(barrier, inc=1, device_id=peer, device_id_type=MESH)

    def remote(src, dst, send, recv, peer):
        return pltpu.make_async_remote_copy(
            src_ref=src, dst_ref=dst, send_sem=send, recv_sem=recv, device_id=peer, device_id_type=MESH
        )

    def p0(g):
        block = wbuf.at[g, z, x, h]
        return remote(block, block, p0_send.at[g], p0_recv.at[g], h_peer)

    def start_own(g):
        for i in range(3):
            for half in (0, 1):
                pltpu.make_async_copy(
                    w_in.at[i, pl.ds(half * 64, 64), pl.ds(g * LANES, LANES)],
                    wbuf.at[g, z, x, h, half, :, pl.ds(i * LANES, LANES)],
                    loc_sem.at[g],
                ).start()

    def wait_own(g):
        block = wbuf.at[g, z, x, h]
        pltpu.make_async_copy(block, block, loc_sem.at[g]).wait()

    def ring(g, phase, half, way, sender):
        step = -1 if way == 0 else 1
        along_x = (half == 0) == (phase < FIRST_HALF)
        zz, xx = z, x
        if along_x:
            xx = turn(x, sender)
            if phase in (ON, LAST):
                xx = turn(xx, step)
        else:
            zz = turn(z, sender)
            if phase in (ON, LAST):
                zz = turn(zz, step)
        part = wbuf.at[g]
        hh = {FIRST_HALF: 0, SECOND_HALF: 1, LAST: way}.get(phase)
        if phase == NEAR:
            ref = part.at[zz, xx, :, half]
        elif phase == ON:
            ref = part.at[zz, xx, way, half]
        else:
            ref = part.at[:, xx, hh, half] if along_x else part.at[zz, :, hh, half]
        peer = (x_peer if along_x else z_peer)[1 if way == 0 else 3]
        slot = ((g * PHASES + phase) * 2 + half) * 2 + way
        return remote(ref, ref, ring_send.at[slot], ring_recv.at[slot], peer)

    def start_ring(g, phase):
        for half in (0, 1):
            for way in (0, 1):
                ring(g, phase, half, way, 0).start()

    def wait_ring(g, phase):
        for half in (0, 1):
            for way in (0, 1):
                ring(g, phase, half, way, -1 if way == 0 else 1).wait_recv()

    def token_copy(which):
        mine = slab.at[tp]
        far = slab.at[2 * (1 - a) + b]
        if which == 0:
            return remote(tokens, mine, tok_send.at[0], tok_recv.at[0], sibling)
        if which == 1:
            return remote(tokens, mine, tok_send.at[1], tok_recv.at[1], across)
        return remote(far, far, tok_send.at[2], tok_recv.at[2], sibling)

    def token_landed(which):
        ref = slab.at[(2 * a + 1 - b, 2 * (1 - a) + b, 2 * (1 - a) + 1 - b)[which]]
        return remote(ref, ref, tok_send.at[which], tok_recv.at[which], sibling)

    for g in range(GROUPS):
        start_own(g)
    tokens_own = pltpu.make_async_copy(tokens, slab.at[tp], loc_sem.at[GROUPS])
    tokens_own.start()
    pl.semaphore_wait(barrier, len(greeted))
    for g in range(GROUPS):
        wait_own(g)
        p0(g).start()
    token_copy(1).start()
    token_copy(0).start()

    def land_p0(g):
        block = wbuf.at[g, z, x, 1 - h]
        remote(block, block, p0_send.at[g], p0_recv.at[g], h_peer).wait_recv()

    def first_axis(g, carry):
        land_p0(g)
        start_ring(g, NEAR)
        return carry

    def first_axis_on(g, carry):
        wait_ring(g, NEAR)
        start_ring(g, ON)
        return carry

    def second_axis(g, carry):
        wait_ring(g, ON)
        begin = ((0, FIRST_HALF), (0, SECOND_HALF), (1, FIRST_HALF))
        for i, piece in enumerate(begin):

            @pl.when(g == i)
            def _():
                start_ring(*piece)

        return carry

    lax.fori_loop(0, GROUPS, first_axis, 0)
    lax.fori_loop(0, GROUPS, first_axis_on, 0)
    lax.fori_loop(0, GROUPS, second_axis, 0)

    def filter_spectrum(g, carry):
        t_hi, t_lo = split_bf16(taps[pl.ds(g * LANES, LANES), :])
        hs[g] = dot_nt(f_hi[...], t_hi) + (dot_nt(f_hi[...], t_lo) + dot_nt(f_lo[...], t_hi))
        return carry

    lax.fori_loop(0, GROUPS, filter_spectrum, 0)

    def clear(i, carry):
        acc[pl.ds(i * 64, 64), :] = jnp.zeros((64, acc.shape[1]), F32)
        return carry

    lax.fori_loop(0, acc.shape[0] // 64, clear, 0)
    depth = NX * NH * TAPS
    wait_ring(0, FIRST_HALF)
    start_ring(1, SECOND_HALF)
    wait_ring(0, SECOND_HALF)
    start_ring(0, LAST)
    wait_ring(1, FIRST_HALF)
    start_ring(2, FIRST_HALF)
    wait_ring(1, SECOND_HALF)
    start_ring(2, SECOND_HALF)

    def halo_up(g):
        return remote(gbuf.at[g, BLOCKS - 1], hg.at[g], halo_send.at[g], halo_recv.at[g], after)

    def halo_down(g):
        return remote(mbuf.at[g, 0], hm.at[g], halo_send.at[GROUPS + g], halo_recv.at[GROUPS + g], before)

    def ar_h(g):
        return remote(fgmine.at[g], fgother.at[g], ar_send.at[g], ar_recv.at[g], h_peer)

    def stage_1(g):
        pacc[...] = jnp.zeros_like(pacc)

        def project(zz, carry):
            w = wbuf[g, zz].reshape(depth, 3 * LANES)
            s = slab[:, :, pl.ds(pl.multiple_of(zz * depth, depth), depth)].reshape(BLOCKS * TAPS, depth)
            pacc[...] += dot(s, w)
            return carry

        lax.fori_loop(0, NZ, project, 0)
        cols = pl.ds(pl.multiple_of(g * LANES, LANES), LANES)
        qkv[g] = pacc[...].astype(BF16)
        q = qkv[g, :, :LANES].astype(F32)
        k = qkv[g, :, LANES : 2 * LANES].astype(F32)
        v = qkv[g, :, 2 * LANES :].astype(F32)
        gbuf[g] = (k * v).astype(BF16).reshape(BLOCKS, TAPS, LANES)
        mbuf[g] = (og[:, cols].astype(F32) * q).astype(BF16).reshape(BLOCKS, TAPS, LANES)
        halo_up(g).start()
        halo_down(g).start()

    def spectra(g):
        for i in range(BLOCKS):
            vs[i + 1] = dot(f_hi[...], gbuf[g, i])
            us[i] = dot(f_hi[...], mbuf[g, i])

    def halo_spectra(g):
        halo_up(g).wait_recv()
        halo_down(g).wait_recv()
        zero = jnp.zeros((TAPS, LANES), BF16)
        vs[0] = dot(f_hi[...], jnp.where(ctx == 0, zero, hg[g]))
        us[BLOCKS] = dot(f_hi[...], jnp.where(ctx == n_ctx - 1, zero, hm[g]))

    def stage_2(g, blocks):
        cols = pl.ds(pl.multiple_of(g * LANES, LANES), LANES)
        slot = g % 2
        sign = 1.0 - 2.0 * (lax.broadcasted_iota(jnp.int32, (TAPS, LANES), 0) % 2).astype(F32)
        hr, hi = hs[g, :TAPS], hs[g, TAPS:]
        gain = skip[:, cols]
        cr, ci, direct = 0.0, 0.0, 0.0
        for i in blocks:
            rows = slice(i * TAPS, (i + 1) * TAPS)
            xr = vs[i, :TAPS] + sign * vs[i + 1, TAPS:]
            xi = vs[i, TAPS:] - sign * vs[i + 1, :TAPS]
            mr = us[i, :TAPS] + sign * us[i + 1, TAPS:]
            mi = us[i, TAPS:] - sign * us[i + 1, :TAPS]
            dr = sign * us[i, TAPS:]
            di = -sign * us[i, :TAPS]
            cr = cr + (dr * xr + di * xi)
            ci = ci + (di * xr - dr * xi)
            y = jnp.concatenate([hr * xr - hi * xi, hr * xi + hi * xr], 0).astype(BF16)
            w = jnp.concatenate([hr * mr + hi * mi, hr * mi - hi * mr], 0).astype(BF16)
            gf, mf = gbuf[g, i].astype(F32), mbuf[g, i].astype(F32)
            mixed = dot(i_hi[TAPS:, :], y) + gain * gf
            back = dot(i_hi[:TAPS, :], w) + gain * mf
            direct = direct + jnp.sum(gf * mf, 0, keepdims=True)
            qb = qkv[g, rows, :LANES].astype(F32)
            kb = qkv[g, rows, LANES : 2 * LANES].astype(F32)
            vb = qkv[g, rows, 2 * LANES :].astype(F32)
            filt[rows, cols] = (qb * mixed).astype(BF16)
            pg[slot, rows, :LANES] = (og[rows, cols].astype(F32) * mixed).astype(BF16)
            pg[slot, rows, LANES : 2 * LANES] = (back * vb).astype(BF16)
            pg[slot, rows, 2 * LANES :] = (back * kb).astype(BF16)
        return cr, ci, direct

    def keep(sums):
        cross[:TAPS], cross[TAPS:] = sums[0], sums[1]
        straight[...] = sums[2]

    def filter_part(g, sums):
        cr, ci, direct = cross[:TAPS] + sums[0], cross[TAPS:] + sums[1], straight[...] + sums[2]
        c_hi, c_lo = split_bf16(jnp.concatenate([cr, ci], 0))
        i_top = i_hi[:TAPS, :]
        part = dot(i_top, c_hi) + (dot(i_top, c_lo) + dot(i_lo[:TAPS, :], c_hi))
        first = lax.broadcasted_iota(jnp.int32, (TAPS, LANES), 0) == 0
        fgmine[g] = jnp.where(first, direct, part).astype(BF16)
        ar_h(g).start()

    wide = NH * TAPS
    chunk = tgrad.shape[1] // CHUNKS

    def add_terms(groups, c, row_slices):
        for part in range(chunk // wide):
            zx = c * (chunk // wide) + part
            at_cols = pl.ds(pl.multiple_of(zx * wide, wide), wide)
            total = 0.0
            for g in groups:
                left = jnp.concatenate([pg[g % 2, r, :] for r in row_slices], 0)
                total = total + dot_nt(left, wbuf[g, zx // NX, zx % NX].reshape(wide, 3 * LANES))
            done = 0
            for r in row_slices:
                acc[r, at_cols] += total[done : done + r.stop - r.start]
                done += r.stop - r.start

    def group(g, carry):
        wait_ring(g, LAST)

        @pl.when(g == 0)
        def _():
            start_ring(1, LAST)
            token_landed(1).wait_recv()
            token_copy(2).start()
            tokens_own.wait()
            token_landed(0).wait_recv()
            token_landed(2).wait_recv()

        @pl.when(g == 1)
        def _():
            start_ring(3, SECOND_HALF)

        stage_1(g)

        @pl.when(g == 0)
        def _():
            wait_ring(2, FIRST_HALF)
            start_ring(3, FIRST_HALF)
            wait_ring(2, SECOND_HALF)
            start_ring(2, LAST)

        @pl.when(g == 1)
        def _():
            wait_ring(3, FIRST_HALF)

        @pl.when(g == 2)
        def _():
            wait_ring(3, SECOND_HALF)
            start_ring(3, LAST)

        @pl.when(g > 0)
        def _():
            spectra(g - 1)
            halo_spectra(g - 1)
            keep(stage_2(g - 1, INNER))
            filter_part(g - 1, stage_2(g - 1, OUTER))

        @pl.when((g > 0) & (g < GROUPS - 1))
        def _():
            def step(c, carry):
                add_terms([g - 1], c, [slice(0, BLOCKS * TAPS)])
                return carry

            lax.fori_loop(0, CHUNKS, step, 0)

        return carry

    lax.fori_loop(0, GROUPS, group, 0)

    half_chunks = CHUNKS // 2

    def rows_of(t):
        return pl.ds(pl.multiple_of(t * TAPS, TAPS), TAPS)

    def cols_of(c):
        return pl.ds(pl.multiple_of(c * chunk, chunk), chunk)

    def to_core(kind, j):
        n = kind * half_chunks + j
        return remote(ps1.at[n], pr1.at[n], rs_send.at[n], rs_recv.at[n], sibling)

    def to_chip(kind, j):
        n = kind * half_chunks + j
        c = b * half_chunks + j
        peer = {"ctx": ctx, "tp": (2 - a, 3 - 3 * a)[kind]}
        return remote(ps2.at[n], pr2.at[c], rs_send.at[CHUNKS + n], rs_recv.at[CHUNKS + c], peer)

    def to_owner(c):
        return remote(ps3.at[c], pr3.at[c], rs_send.at[2 * CHUNKS + c], rs_recv.at[2 * CHUNKS + c], sibling)

    def scatter(kind):
        row_slices = ([slice(TAPS, 3 * TAPS)], [slice(0, TAPS), slice(3 * TAPS, 4 * TAPS)])[kind]
        far, near = rows_of((2 - a, 3 - 3 * a)[kind]), (1 + a, 3 * a)[kind]

        def step(i, carry):
            side = (b + 1 + i) % 2

            @pl.when(i < CHUNKS)
            def _():
                c = side * half_chunks + i // 2
                add_terms([GROUPS - 2, GROUPS - 1], c, row_slices)

                @pl.when(i % 2 == 0)
                def _():
                    ps1[kind * half_chunks + i // 2] = acc[far, cols_of(c)].astype(BF16)
                    to_core(kind, i // 2).start()

                @pl.when(tp != near)
                def _():
                    ps3[c] = acc[rows_of(near), cols_of(c)].astype(BF16)
                    to_owner(c).start()

            @pl.when((i > 0) & (i % 2 == 0))
            def _():
                j = i // 2 - 1
                to_core(kind, j).wait_recv()
                n = kind * half_chunks + j
                mine = acc[far, cols_of(b * half_chunks + j)]
                ps2[n] = (mine + pr1[n].astype(F32)).astype(BF16)
                to_chip(kind, j).start()

            return carry

        lax.fori_loop(0, CHUNKS + 1, step, 0)

    others = NZ * NX - 1

    def rows_8(m, sense):
        return pl.ds(pl.multiple_of(32 * turn(z, sense * (m // NX)) + 8 * turn(x, sense * (m % NX)), 8), 8)

    def ar(kind, m, src, dst):
        n = GROUPS + kind * others + m - 1
        return remote(src, dst, ar_send.at[n], ar_recv.at[n], at(turn(z, m // NX), turn(x, m % NX), h))

    def each(act):
        def step(m, carry):
            act(m)
            return carry

        lax.fori_loop(1, others + 1, step, 0)

    last = GROUPS - 1
    early, late = pl.ds(0, last * LANES), pl.ds(last * LANES, LANES)

    def plane(kind, m):
        cols = (early, late)[kind]
        return ar(kind, m, fgbuf.at[rows_8(m, 1), cols], zrecv.at[m - 1, :, cols])

    def back(m):
        mine = fgrad.at[rows_8(0, 1), :]
        return ar(2, m, mine, mine)

    def back_landed(m):
        got = fgrad.at[rows_8(m, -1), :]
        return ar(2, m, got, got)

    def sum_h(g):
        ar_h(g).wait_recv()
        fgbuf[:, g * LANES : (g + 1) * LANES] = fgmine[g].astype(F32) + fgother[g].astype(F32)

    spectra(last)
    keep(stage_2(last, INNER))
    scatter(0)
    for g in range(last):
        sum_h(g)
    each(lambda m: plane(0, m).start())
    halo_spectra(last)
    filter_part(last, stage_2(last, OUTER))
    scatter(1)
    sum_h(last)
    each(lambda m: plane(1, m).start())

    def arrived(m):
        plane(0, m).wait_recv()
        plane(1, m).wait_recv()

    each(arrived)
    total = fgbuf[rows_8(0, 1), :]
    for m in range(others):
        total = total + zrecv[m]
    fgrad[rows_8(0, 1), :] = total * (BLOCKS * TAPS * n_ctx) ** (-0.5)
    each(lambda m: back(m).start())

    def finish(c, carry):
        to_owner(c).wait_recv()
        remote(pr2.at[c], pr2.at[c], rs_send.at[CHUNKS + c], rs_recv.at[CHUNKS + c], across).wait_recv()
        total = acc[rows_of(tp), cols_of(c)] + pr3[c].astype(F32) + pr2[c].astype(F32)
        tgrad[:, cols_of(c)] = total.astype(BF16)
        return carry

    lax.fori_loop(0, CHUNKS, finish, 0)
    each(lambda m: back_landed(m).wait_recv())

    def drain(g, carry):
        p0(g).wait_send()
        halo_up(g).wait_send()
        halo_down(g).wait_send()
        ar_h(g).wait_send()
        for phase in range(PHASES):
            for half in (0, 1):
                for way in (0, 1):
                    ring(g, phase, half, way, 0).wait_send()
        return carry

    def drain_scatter(j, carry):
        for kind in (0, 1):
            to_core(kind, j).wait_send()
            to_chip(kind, j).wait_send()
            to_owner(kind * half_chunks + j).wait_send()
        return carry

    lax.fori_loop(0, GROUPS, drain, 0)
    lax.fori_loop(0, half_chunks, drain_scatter, 0)
    for which in range(3):
        token_copy(which).wait_send()

    def drain_plane(m):
        plane(0, m).wait_send()
        plane(1, m).wait_send()
        back(m).wait_send()

    each(drain_plane)


def hand_out(filt, tgrad, total, filt_out, tgrad_out, fgrad_out, skip_out):
    filt_out[...] = filt[...]
    tgrad_out[...] = tgrad[...]
    fgrad_out[...] = total[...].T
    skip_out[...] = total[:1, :]


def shards(tokens, proj_weight, filter_taps, skip_gain, out_grad):
    rows, width = out_grad.shape
    depth = tokens.shape[1]
    forward, inverse = transforms()
    f_hi, f_lo = split_bf16(jnp.asarray(forward))
    i_hi, i_lo = split_bf16(jnp.asarray(inverse))
    w_in = proj_weight.transpose(1, 0, 2)
    vmem = pl.BlockSpec(memory_space=pltpu.VMEM)
    hbm = pl.BlockSpec(memory_space=pl.ANY)
    sem = pltpu.SemaphoreType.DMA
    V = pltpu.VMEM
    filtered, tokens_grad, filter_total = pl.pallas_call(
        kernel,
        out_shape=(
            jax.ShapeDtypeStruct((rows, width), BF16),
            jax.ShapeDtypeStruct((TAPS, depth), BF16),
            jax.ShapeDtypeStruct((TAPS, width), F32),
        ),
        in_specs=[hbm, hbm] + [vmem] * 7,
        out_specs=(vmem, vmem, vmem),
        scratch_shapes=[
            V((GROUPS, NZ, NX, NH, 2, 64, 3 * LANES), BF16),
            V((BLOCKS, TAPS, depth), BF16),
            V((rows, depth), F32),
            V((rows, 3 * LANES), F32),
            V((GROUPS, rows, 3 * LANES), BF16),
            V((2, rows, 3 * LANES), BF16),
            V((GROUPS, BLOCKS, TAPS, LANES), BF16),
            V((GROUPS, BLOCKS, TAPS, LANES), BF16),
            V((GROUPS, TAPS, LANES), BF16),
            V((GROUPS, TAPS, LANES), BF16),
            V((BLOCKS + 1, 2 * TAPS, LANES), F32),
            V((BLOCKS + 1, 2 * TAPS, LANES), F32),
            V((GROUPS, 2 * TAPS, LANES), F32),
            V((2 * TAPS, LANES), F32),
            V((1, LANES), F32),
            V((GROUPS, TAPS, LANES), BF16),
            V((GROUPS, TAPS, LANES), BF16),
            V((TAPS, width), F32),
            V((NZ * NX - 1, 8, width), F32),
        ]
        + [V((CHUNKS, TAPS, depth // CHUNKS), BF16)] * 6
        + [
            sem((GROUPS + 1,)),
            sem((GROUPS,)),
            sem((GROUPS,)),
            sem((GROUPS * 4 * PHASES,)),
            sem((GROUPS * 4 * PHASES,)),
            sem((3,)),
            sem((3,)),
            sem((2 * GROUPS,)),
            sem((2 * GROUPS,)),
            sem((3 * CHUNKS,)),
            sem((3 * CHUNKS,)),
            sem((GROUPS + 3 * (NZ * NX - 1),)),
            sem((GROUPS + 3 * (NZ * NX - 1),)),
        ],
        compiler_params=pltpu.CompilerParams(
            collective_id=0, has_side_effects=True, vmem_limit_bytes=58 * 2**20
        ),
    )(tokens, w_in, filter_taps, skip_gain[None, :], out_grad, f_hi, f_lo, i_hi, i_lo)
    filtered, tokens_grad, filter_grad, skip_grad = pl.pallas_call(
        hand_out,
        out_shape=(
            jax.ShapeDtypeStruct((rows, width), BF16),
            jax.ShapeDtypeStruct((TAPS, depth), BF16),
            jax.ShapeDtypeStruct((width, TAPS), F32),
            jax.ShapeDtypeStruct((1, width), F32),
        ),
        in_specs=[vmem] * 3,
        out_specs=(vmem,) * 4,
    )(filtered, tokens_grad, filter_total)
    return filtered, tokens_grad, filter_grad, skip_grad[0]


def solution(mesh):
    placed = (P(("ctx", "tp"), None), P("ctx", None, "tp"), P("tp", None), P("tp"), P("ctx", "tp"))
    return jax.shard_map(
        shards,
        mesh=mesh,
        in_specs=placed,
        out_specs=(P("ctx", "tp"), P(("ctx", "tp"), None), P("tp", None), P("tp")),
        check_vma=False,
    )
```

```python
import functools

import numpy as np
import jax
import jax.numpy as jnp
from jax import lax
from jax.experimental import pallas as pl
from jax.experimental.pallas import tpu as pltpu
from jax.sharding import PartitionSpec as P

MESH = pl.DeviceIdType.MESH
F32 = jnp.float32
BF16 = jnp.bfloat16
TAPS = 128
LANES = 128
BLOCKS = 4
GROUPS = 4
NZ, NX, NH = 4, 4, 2
NEAR, PAIR, ON, FIRST_HALF, SECOND_HALF, LAST = range(6)
PHASES = 6
INNER, OUTER = (1, 2), (0, 3)
CHUNKS = 8


def transforms():
    k = np.arange(TAPS)[:, None]
    n = np.arange(2 * TAPS)[None, :]
    angle = np.pi * (2 * k + 1) * n / (2 * TAPS)
    both = np.concatenate([np.cos(angle), -np.sin(angle)], 0)
    return both[:, :TAPS].astype(np.float32), (both.T / TAPS).astype(np.float32)


def split_bf16(m):
    hi = m.astype(BF16)
    return hi, (m - hi.astype(F32)).astype(BF16)


def dot(a, b):
    return jnp.dot(a, b, preferred_element_type=F32)


def dot_nt(a, b):
    return lax.dot_general(a, b, (((1,), (1,)), ((), ())), preferred_element_type=F32)


def kernel(
    tokens, w_in, taps, skip, og, f_hi, f_lo, i_hi, i_lo,
    filt, tgrad, fgrad,
    wbuf, slab, acc, pacc, qkv, pg, gbuf, mbuf, hg, hm, vs, us, hs,
    cross, straight, fgmine, fgother, fgbuf, zrecv,
    ps1, pr1, ps2, pr2, ps3, pr3,
    loc_sem, p0_send, p0_recv, ring_send, ring_recv, tok_send, tok_recv, halo_send, halo_recv,
    rs_send, rs_recv, ar_send, ar_recv,
):
    ctx = lax.axis_index("ctx")
    tp = lax.axis_index("tp")
    n_ctx = NZ * NX * NH
    z, x, h = ctx // (NX * NH), (ctx // NH) % NX, ctx % NH
    a, b = tp // 2, tp % 2

    def at(zz, xx, hh):
        return {"ctx": (zz * NX + xx) * NH + hh, "tp": tp}

    def turn(v, by):
        return (v + by + 4) % 4

    sibling = {"ctx": ctx, "tp": 2 * a + 1 - b}
    across = {"ctx": ctx, "tp": 2 * (1 - a) + b}
    far_sibling = {"ctx": ctx, "tp": 2 * (1 - a) + 1 - b}
    after = {"ctx": (ctx + 1) % n_ctx, "tp": tp}
    before = {"ctx": (ctx + n_ctx - 1) % n_ctx, "tp": tp}
    h_peer = at(z, x, 1 - h)
    z_peer = [None] + [at(turn(z, d), x, h) for d in (1, 2, 3)]
    x_peer = [None] + [at(z, turn(x, d), h) for d in (1, 2, 3)]

    barrier = pltpu.get_barrier_semaphore()
    greeted = [sibling, across, far_sibling, after, before, h_peer]
    greeted = greeted + [at(turn(z, m // NX), turn(x, m % NX), h) for m in range(1, NZ * NX)]
    for peer in greeted:
        pl.semaphore_signal(barrier, inc=1, device_id=peer, device_id_type=MESH)

    def remote(src, dst, send, recv, peer):
        return pltpu.make_async_remote_copy(
            src_ref=src, dst_ref=dst, send_sem=send, recv_sem=recv, device_id=peer, device_id_type=MESH
        )

    def p0(g):
        block = wbuf.at[g, z, x, h]
        return remote(block, block, p0_send.at[g], p0_recv.at[g], h_peer)

    def start_own(g):
        for i in range(3):
            for half in (0, 1):
                pltpu.make_async_copy(
                    w_in.at[i, pl.ds(half * 64, 64), pl.ds(g * LANES, LANES)],
                    wbuf.at[g, z, x, h, half, :, pl.ds(i * LANES, LANES)],
                    loc_sem.at[g],
                ).start()

    def wait_own(g):
        block = wbuf.at[g, z, x, h]
        pltpu.make_async_copy(block, block, loc_sem.at[g]).wait()

    def ring(g, phase, half, way, sender):
        step = -1 if way == 0 else 1
        along_x = (half == 0) == (phase < FIRST_HALF)
        zz, xx = z, x
        if along_x:
            xx = turn(x, sender)
            if phase in (ON, LAST):
                xx = turn(xx, step)
        else:
            zz = turn(z, sender)
            if phase in (ON, LAST):
                zz = turn(zz, step)
        part = wbuf.at[g]
        hh = {NEAR: h, PAIR: 1 - h, ON: way, FIRST_HALF: 0, SECOND_HALF: 1, LAST: way}[phase]
        if phase in (NEAR, PAIR, ON):
            ref = part.at[zz, xx, hh, half]
        else:
            ref = part.at[:, xx, hh, half] if along_x else part.at[zz, :, hh, half]
        peer = (x_peer if along_x else z_peer)[1 if way == 0 else 3]
        slot = ((g * PHASES + phase) * 2 + half) * 2 + way
        return remote(ref, ref, ring_send.at[slot], ring_recv.at[slot], peer)

    def start_ring(g, phase):
        for half in (0, 1):
            for way in (0, 1):
                ring(g, phase, half, way, 0).start()

    def wait_ring(g, phase):
        for half in (0, 1):
            for way in (0, 1):
                ring(g, phase, half, way, -1 if way == 0 else 1).wait_recv()

    def token_copy(which):
        mine = slab.at[tp]
        far = slab.at[2 * (1 - a) + b]
        if which == 0:
            return remote(tokens, mine, tok_send.at[0], tok_recv.at[0], sibling)
        if which == 1:
            return remote(tokens, mine, tok_send.at[1], tok_recv.at[1], across)
        return remote(far, far, tok_send.at[2], tok_recv.at[2], sibling)

    def token_landed(which):
        ref = slab.at[(2 * a + 1 - b, 2 * (1 - a) + b, 2 * (1 - a) + 1 - b)[which]]
        return remote(ref, ref, tok_send.at[which], tok_recv.at[which], sibling)

    for g in range(GROUPS):
        start_own(g)
    tokens_own = pltpu.make_async_copy(tokens, slab.at[tp], loc_sem.at[GROUPS])
    tokens_own.start()
    pl.semaphore_wait(barrier, len(greeted))
    for g in range(GROUPS):
        wait_own(g)
        p0(g).start()
        start_ring(g, NEAR)
    token_copy(1).start()
    token_copy(0).start()

    def land_p0(g):
        block = wbuf.at[g, z, x, 1 - h]
        remote(block, block, p0_send.at[g], p0_recv.at[g], h_peer).wait_recv()

    def first_axis(g, carry):
        land_p0(g)
        start_ring(g, PAIR)
        return carry

    def first_axis_on(g, carry):
        wait_ring(g, NEAR)
        wait_ring(g, PAIR)
        start_ring(g, ON)
        return carry

    def second_axis(g, carry):
        wait_ring(g, ON)
        begin = ((0, FIRST_HALF), (0, SECOND_HALF), (1, FIRST_HALF))
        for i, piece in enumerate(begin):

            @pl.when(g == i)
            def _():
                start_ring(*piece)

        return carry

    lax.fori_loop(0, GROUPS, first_axis, 0)
    lax.fori_loop(0, GROUPS, first_axis_on, 0)
    lax.fori_loop(0, GROUPS, second_axis, 0)

    def filter_spectrum(g, carry):
        t_hi, t_lo = split_bf16(taps[pl.ds(g * LANES, LANES), :])
        hs[g] = dot_nt(f_hi[...], t_hi) + (dot_nt(f_hi[...], t_lo) + dot_nt(f_lo[...], t_hi))
        return carry

    lax.fori_loop(0, GROUPS, filter_spectrum, 0)

    def clear(i, carry):
        acc[pl.ds(i * 64, 64), :] = jnp.zeros((64, acc.shape[1]), F32)
        return carry

    lax.fori_loop(0, acc.shape[0] // 64, clear, 0)
    depth = NX * NH * TAPS
    wait_ring(0, FIRST_HALF)
    start_ring(1, SECOND_HALF)
    wait_ring(0, SECOND_HALF)
    start_ring(0, LAST)
    wait_ring(1, FIRST_HALF)
    start_ring(2, FIRST_HALF)
    wait_ring(1, SECOND_HALF)
    start_ring(2, SECOND_HALF)

    def halo_up(g):
        return remote(gbuf.at[g, BLOCKS - 1], hg.at[g], halo_send.at[g], halo_recv.at[g], after)

    def halo_down(g):
        return remote(mbuf.at[g, 0], hm.at[g], halo_send.at[GROUPS + g], halo_recv.at[GROUPS + g], before)

    def ar_h(g):
        return remote(fgmine.at[g], fgother.at[g], ar_send.at[g], ar_recv.at[g], h_peer)

    def stage_1(g):
        pacc[...] = dot(slab[...].reshape(BLOCKS * TAPS, NZ * depth), wbuf[g].reshape(NZ * depth, 3 * LANES))
        cols = pl.ds(pl.multiple_of(g * LANES, LANES), LANES)
        qkv[g] = pacc[...].astype(BF16)
        q = qkv[g, :, :LANES].astype(F32)
        k = qkv[g, :, LANES : 2 * LANES].astype(F32)
        v = qkv[g, :, 2 * LANES :].astype(F32)
        gbuf[g] = (k * v).astype(BF16).reshape(BLOCKS, TAPS, LANES)
        mbuf[g] = (og[:, cols].astype(F32) * q).astype(BF16).reshape(BLOCKS, TAPS, LANES)
        halo_up(g).start()
        halo_down(g).start()

    def spectra(g):
        for i in range(BLOCKS):
            vs[i + 1] = dot(f_hi[...], gbuf[g, i])
            us[i] = dot(f_hi[...], mbuf[g, i])

    def halo_spectra(g):
        halo_up(g).wait_recv()
        halo_down(g).wait_recv()
        zero = jnp.zeros((TAPS, LANES), BF16)
        vs[0] = dot(f_hi[...], jnp.where(ctx == 0, zero, hg[g]))
        us[BLOCKS] = dot(f_hi[...], jnp.where(ctx == n_ctx - 1, zero, hm[g]))

    def stage_2(g, blocks):
        cols = pl.ds(pl.multiple_of(g * LANES, LANES), LANES)
        slot = g % 2
        sign = 1.0 - 2.0 * (lax.broadcasted_iota(jnp.int32, (TAPS, LANES), 0) % 2).astype(F32)
        hr, hi = hs[g, :TAPS], hs[g, TAPS:]
        gain = skip[:, cols]
        cr, ci, direct = 0.0, 0.0, 0.0
        for i in blocks:
            rows = slice(i * TAPS, (i + 1) * TAPS)
            xr = vs[i, :TAPS] + sign * vs[i + 1, TAPS:]
            xi = vs[i, TAPS:] - sign * vs[i + 1, :TAPS]
            mr = us[i, :TAPS] + sign * us[i + 1, TAPS:]
            mi = us[i, TAPS:] - sign * us[i + 1, :TAPS]
            dr = sign * us[i, TAPS:]
            di = -sign * us[i, :TAPS]
            cr = cr + (dr * xr + di * xi)
            ci = ci + (di * xr - dr * xi)
            y = jnp.concatenate([hr * xr - hi * xi, hr * xi + hi * xr], 0).astype(BF16)
            w = jnp.concatenate([hr * mr + hi * mi, hr * mi - hi * mr], 0).astype(BF16)
            gf, mf = gbuf[g, i].astype(F32), mbuf[g, i].astype(F32)
            mixed = dot(i_hi[TAPS:, :], y) + gain * gf
            back = dot(i_hi[:TAPS, :], w) + gain * mf
            direct = direct + jnp.sum(gf * mf, 0, keepdims=True)
            qb = qkv[g, rows, :LANES].astype(F32)
            kb = qkv[g, rows, LANES : 2 * LANES].astype(F32)
            vb = qkv[g, rows, 2 * LANES :].astype(F32)
            filt[rows, cols] = (qb * mixed).astype(BF16)
            pg[slot, rows, :LANES] = (og[rows, cols].astype(F32) * mixed).astype(BF16)
            pg[slot, rows, LANES : 2 * LANES] = (back * vb).astype(BF16)
            pg[slot, rows, 2 * LANES :] = (back * kb).astype(BF16)
        return cr, ci, direct

    def keep(sums):
        cross[:TAPS], cross[TAPS:] = sums[0], sums[1]
        straight[...] = sums[2]

    def filter_part(g, sums):
        cr, ci, direct = cross[:TAPS] + sums[0], cross[TAPS:] + sums[1], straight[...] + sums[2]
        c_hi, c_lo = split_bf16(jnp.concatenate([cr, ci], 0))
        i_top = i_hi[:TAPS, :]
        part = dot(i_top, c_hi) + (dot(i_top, c_lo) + dot(i_lo[:TAPS, :], c_hi))
        first = lax.broadcasted_iota(jnp.int32, (TAPS, LANES), 0) == 0
        fgmine[g] = jnp.where(first, direct, part).astype(BF16)
        ar_h(g).start()

    wide = NH * TAPS
    chunk = tgrad.shape[1] // CHUNKS

    def add_terms(groups, c, row_slices):
        at_cols = pl.ds(pl.multiple_of(c * chunk, chunk), chunk)
        count = chunk // wide
        zz, xx = c * count // NX, c * count % NX
        total = 0.0
        for g in groups:
            left = jnp.concatenate([pg[g % 2, r, :] for r in row_slices], 0)
            total = total + dot_nt(left, wbuf[g, zz, pl.ds(xx, count)].reshape(chunk, 3 * LANES))
        done = 0
        for r in row_slices:
            acc[r, at_cols] += total[done : done + r.stop - r.start]
            done += r.stop - r.start

    def group(g, carry):
        wait_ring(g, LAST)

        @pl.when(g == 0)
        def _():
            start_ring(1, LAST)
            token_landed(1).wait_recv()
            token_copy(2).start()
            tokens_own.wait()
            token_landed(0).wait_recv()
            token_landed(2).wait_recv()

        @pl.when(g == 1)
        def _():
            start_ring(3, SECOND_HALF)

        stage_1(g)

        @pl.when(g == 0)
        def _():
            wait_ring(2, FIRST_HALF)
            start_ring(3, FIRST_HALF)
            wait_ring(2, SECOND_HALF)
            start_ring(2, LAST)

        @pl.when(g == 1)
        def _():
            wait_ring(3, FIRST_HALF)

        @pl.when(g == 2)
        def _():
            wait_ring(3, SECOND_HALF)
            start_ring(3, LAST)

        def finish_group(done, carry):
            spectra(done)
            halo_spectra(done)
            keep(stage_2(done, INNER))
            filter_part(done, stage_2(done, OUTER))

            @pl.when(done < GROUPS - 2)
            def _():
                def step(c, carry):
                    add_terms([done], c, [slice(0, BLOCKS * TAPS)])
                    return carry

                lax.fori_loop(0, CHUNKS, step, 0)

            return carry

        begin = jnp.where(g == GROUPS - 1, g, jnp.maximum(g - 1, 0))
        end = jnp.where(g == GROUPS - 2, g + 1, g)
        lax.fori_loop(begin, end, finish_group, 0)
        return carry

    lax.fori_loop(0, GROUPS, group, 0)

    half_chunks = CHUNKS // 2

    def rows_of(t):
        return pl.ds(pl.multiple_of(t * TAPS, TAPS), TAPS)

    def cols_of(c):
        return pl.ds(pl.multiple_of(c * chunk, chunk), chunk)

    def to_core(kind, j):
        n = kind * half_chunks + j
        return remote(ps1.at[n], pr1.at[n], rs_send.at[n], rs_recv.at[n], sibling)

    def to_chip(kind, j):
        n = kind * half_chunks + j
        c = b * half_chunks + j
        peer = {"ctx": ctx, "tp": (2 - a, 3 - 3 * a)[kind]}
        return remote(ps2.at[n], pr2.at[c], rs_send.at[CHUNKS + n], rs_recv.at[CHUNKS + c], peer)

    def to_owner(c):
        return remote(ps3.at[c], pr3.at[c], rs_send.at[2 * CHUNKS + c], rs_recv.at[2 * CHUNKS + c], sibling)

    def scatter(kind):
        row_slices = ([slice(TAPS, 3 * TAPS)], [slice(0, TAPS), slice(3 * TAPS, 4 * TAPS)])[kind]
        far, near = rows_of((2 - a, 3 - 3 * a)[kind]), (1 + a, 3 * a)[kind]

        def step(i, carry):
            side = (b + 1 + i) % 2

            @pl.when(i < CHUNKS)
            def _():
                c = side * half_chunks + i // 2
                add_terms([GROUPS - 2, GROUPS - 1], c, row_slices)

                @pl.when(i % 2 == 0)
                def _():
                    ps1[kind * half_chunks + i // 2] = acc[far, cols_of(c)].astype(BF16)
                    to_core(kind, i // 2).start()

                @pl.when(tp != near)
                def _():
                    ps3[c] = acc[rows_of(near), cols_of(c)].astype(BF16)
                    to_owner(c).start()

            @pl.when((i > 0) & (i % 2 == 0))
            def _():
                j = i // 2 - 1
                to_core(kind, j).wait_recv()
                n = kind * half_chunks + j
                mine = acc[far, cols_of(b * half_chunks + j)]
                ps2[n] = (mine + pr1[n].astype(F32)).astype(BF16)
                to_chip(kind, j).start()

            return carry

        lax.fori_loop(0, CHUNKS + 1, step, 0)

    others = NZ * NX - 1

    def rows_8(m, sense):
        return pl.ds(pl.multiple_of(32 * turn(z, sense * (m // NX)) + 8 * turn(x, sense * (m % NX)), 8), 8)

    def ar(kind, m, src, dst):
        n = GROUPS + kind * others + m - 1
        return remote(src, dst, ar_send.at[n], ar_recv.at[n], at(turn(z, m // NX), turn(x, m % NX), h))

    def each(act):
        def step(m, carry):
            act(m)
            return carry

        lax.fori_loop(1, others + 1, step, 0)

    last = GROUPS - 1
    early, late = pl.ds(0, last * LANES), pl.ds(last * LANES, LANES)

    def plane(kind, m):
        cols = (early, late)[kind]
        return ar(kind, m, fgbuf.at[rows_8(m, 1), cols], zrecv.at[m - 1, :, cols])

    def back(m):
        mine = fgrad.at[rows_8(0, 1), :]
        return ar(2, m, mine, mine)

    def back_landed(m):
        got = fgrad.at[rows_8(m, -1), :]
        return ar(2, m, got, got)

    def sum_h(g):
        ar_h(g).wait_recv()
        fgbuf[:, g * LANES : (g + 1) * LANES] = fgmine[g].astype(F32) + fgother[g].astype(F32)

    spectra(last)
    keep(stage_2(last, INNER))
    scatter(0)
    for g in range(last):
        sum_h(g)
    each(lambda m: plane(0, m).start())
    halo_spectra(last)
    filter_part(last, stage_2(last, OUTER))
    scatter(1)
    sum_h(last)
    each(lambda m: plane(1, m).start())

    def arrived(m):
        plane(0, m).wait_recv()
        plane(1, m).wait_recv()

    each(arrived)
    total = fgbuf[rows_8(0, 1), :]
    for m in range(others):
        total = total + zrecv[m]
    fgrad[rows_8(0, 1), :] = total * (BLOCKS * TAPS * n_ctx) ** (-0.5)
    each(lambda m: back(m).start())

    def finish(c, carry):
        to_owner(c).wait_recv()
        remote(pr2.at[c], pr2.at[c], rs_send.at[CHUNKS + c], rs_recv.at[CHUNKS + c], across).wait_recv()
        total = acc[rows_of(tp), cols_of(c)] + pr3[c].astype(F32) + pr2[c].astype(F32)
        tgrad[:, cols_of(c)] = total.astype(BF16)
        return carry

    lax.fori_loop(0, CHUNKS, finish, 0)
    each(lambda m: back_landed(m).wait_recv())

    def drain(g, carry):
        p0(g).wait_send()
        halo_up(g).wait_send()
        halo_down(g).wait_send()
        ar_h(g).wait_send()
        for phase in range(PHASES):
            for half in (0, 1):
                for way in (0, 1):
                    ring(g, phase, half, way, 0).wait_send()
        return carry

    def drain_scatter(j, carry):
        for kind in (0, 1):
            to_core(kind, j).wait_send()
            to_chip(kind, j).wait_send()
            to_owner(kind * half_chunks + j).wait_send()
        return carry

    lax.fori_loop(0, GROUPS, drain, 0)
    lax.fori_loop(0, half_chunks, drain_scatter, 0)
    for which in range(3):
        token_copy(which).wait_send()

    def drain_plane(m):
        plane(0, m).wait_send()
        plane(1, m).wait_send()
        back(m).wait_send()

    each(drain_plane)


def hand_out(filt, tgrad, total, filt_out, tgrad_out, fgrad_out, skip_out):
    filt_out[...] = filt[...]
    tgrad_out[...] = tgrad[...]
    fgrad_out[...] = total[...].T
    skip_out[...] = total[:1, :]


def shards(tokens, proj_weight, filter_taps, skip_gain, out_grad):
    rows, width = out_grad.shape
    depth = tokens.shape[1]
    forward, inverse = transforms()
    f_hi, f_lo = split_bf16(jnp.asarray(forward))
    i_hi, i_lo = split_bf16(jnp.asarray(inverse))
    w_in = proj_weight.transpose(1, 0, 2)
    vmem = pl.BlockSpec(memory_space=pltpu.VMEM)
    hbm = pl.BlockSpec(memory_space=pl.ANY)
    sem = pltpu.SemaphoreType.DMA
    V = pltpu.VMEM
    filtered, tokens_grad, filter_total = pl.pallas_call(
        kernel,
        out_shape=(
            jax.ShapeDtypeStruct((rows, width), BF16),
            jax.ShapeDtypeStruct((TAPS, depth), BF16),
            jax.ShapeDtypeStruct((TAPS, width), F32),
        ),
        in_specs=[hbm, hbm] + [vmem] * 7,
        out_specs=(vmem, vmem, vmem),
        scratch_shapes=[
            V((GROUPS, NZ, NX, NH, 2, 64, 3 * LANES), BF16),
            V((BLOCKS, TAPS, depth), BF16),
            V((rows, depth), F32),
            V((rows, 3 * LANES), F32),
            V((GROUPS, rows, 3 * LANES), BF16),
            V((2, rows, 3 * LANES), BF16),
            V((GROUPS, BLOCKS, TAPS, LANES), BF16),
            V((GROUPS, BLOCKS, TAPS, LANES), BF16),
            V((GROUPS, TAPS, LANES), BF16),
            V((GROUPS, TAPS, LANES), BF16),
            V((BLOCKS + 1, 2 * TAPS, LANES), F32),
            V((BLOCKS + 1, 2 * TAPS, LANES), F32),
            V((GROUPS, 2 * TAPS, LANES), F32),
            V((2 * TAPS, LANES), F32),
            V((1, LANES), F32),
            V((GROUPS, TAPS, LANES), BF16),
            V((GROUPS, TAPS, LANES), BF16),
            V((TAPS, width), F32),
            V((NZ * NX - 1, 8, width), F32),
        ]
        + [V((CHUNKS, TAPS, depth // CHUNKS), BF16)] * 6
        + [
            sem((GROUPS + 1,)),
            sem((GROUPS,)),
            sem((GROUPS,)),
            sem((GROUPS * 4 * PHASES,)),
            sem((GROUPS * 4 * PHASES,)),
            sem((3,)),
            sem((3,)),
            sem((2 * GROUPS,)),
            sem((2 * GROUPS,)),
            sem((3 * CHUNKS,)),
            sem((3 * CHUNKS,)),
            sem((GROUPS + 3 * (NZ * NX - 1),)),
            sem((GROUPS + 3 * (NZ * NX - 1),)),
        ],
        compiler_params=pltpu.CompilerParams(
            collective_id=0, has_side_effects=True, vmem_limit_bytes=58 * 2**20
        ),
    )(tokens, w_in, filter_taps, skip_gain[None, :], out_grad, f_hi, f_lo, i_hi, i_lo)
    filtered, tokens_grad, filter_grad, skip_grad = pl.pallas_call(
        hand_out,
        out_shape=(
            jax.ShapeDtypeStruct((rows, width), BF16),
            jax.ShapeDtypeStruct((TAPS, depth), BF16),
            jax.ShapeDtypeStruct((width, TAPS), F32),
            jax.ShapeDtypeStruct((1, width), F32),
        ),
        in_specs=[vmem] * 3,
        out_specs=(vmem,) * 4,
    )(filtered, tokens_grad, filter_total)
    return filtered, tokens_grad, filter_grad, skip_grad[0]


def solution(mesh):
    placed = (P(("ctx", "tp"), None), P("ctx", None, "tp"), P("tp", None), P("tp"), P("ctx", "tp"))
    return jax.shard_map(
        shards,
        mesh=mesh,
        in_specs=placed,
        out_specs=(P("ctx", "tp"), P(("ctx", "tp"), None), P("tp", None), P("tp")),
        check_vma=False,
    )
```

```python
import functools

import numpy as np
import jax
import jax.numpy as jnp
from jax import lax
from jax.experimental import pallas as pl
from jax.experimental.pallas import tpu as pltpu
from jax.sharding import PartitionSpec as P

MESH = pl.DeviceIdType.MESH
F32 = jnp.float32
BF16 = jnp.bfloat16
TAPS = 128
LANES = 128
BLOCKS = 4
GROUPS = 4
NZ, NX, NH = 4, 4, 2
NEAR, PAIR, ON, FIRST_HALF, SECOND_HALF, LAST = range(6)
PHASES = 6
INNER, OUTER = (1, 2), (0, 3)
CHUNKS = 8


def transforms():
    k = np.arange(TAPS)[:, None]
    n = np.arange(2 * TAPS)[None, :]
    angle = np.pi * (2 * k + 1) * n / (2 * TAPS)
    both = np.concatenate([np.cos(angle), -np.sin(angle)], 0)
    return both[:, :TAPS].astype(np.float32), (both.T / TAPS).astype(np.float32)


def split_bf16(m):
    hi = m.astype(BF16)
    return hi, (m - hi.astype(F32)).astype(BF16)


def dot(a, b):
    return jnp.dot(a, b, preferred_element_type=F32)


def dot_nt(a, b):
    return lax.dot_general(a, b, (((1,), (1,)), ((), ())), preferred_element_type=F32)


def kernel(
    tokens, w_in, taps_in, skip, og_in, f_hi, f_lo, i_hi, i_lo,
    filt, tgrad, fgrad,
    taps, og, wbuf, slab, acc, pacc, qkv, pg, gbuf, mbuf, hg, hm, vs, us, hs,
    cross, straight, fgmine, fgother, fgbuf, zrecv,
    ps1, pr1, ps2, pr2, ps3, pr3,
    loc_sem, p0_send, p0_recv, ring_send, ring_recv, tok_send, tok_recv, halo_send, halo_recv,
    rs_send, rs_recv, ar_send, ar_recv,
):
    ctx = lax.axis_index("ctx")
    tp = lax.axis_index("tp")
    n_ctx = NZ * NX * NH
    z, x, h = ctx // (NX * NH), (ctx // NH) % NX, ctx % NH
    a, b = tp // 2, tp % 2

    def at(zz, xx, hh):
        return {"ctx": (zz * NX + xx) * NH + hh, "tp": tp}

    def turn(v, by):
        return (v + by + 4) % 4

    sibling = {"ctx": ctx, "tp": 2 * a + 1 - b}
    across = {"ctx": ctx, "tp": 2 * (1 - a) + b}
    far_sibling = {"ctx": ctx, "tp": 2 * (1 - a) + 1 - b}
    after = {"ctx": (ctx + 1) % n_ctx, "tp": tp}
    before = {"ctx": (ctx + n_ctx - 1) % n_ctx, "tp": tp}
    h_peer = at(z, x, 1 - h)
    z_peer = [None] + [at(turn(z, d), x, h) for d in (1, 2, 3)]
    x_peer = [None] + [at(z, turn(x, d), h) for d in (1, 2, 3)]

    barrier = pltpu.get_barrier_semaphore()
    greeted = [sibling, across, far_sibling, after, before, h_peer]
    greeted = greeted + [at(turn(z, m // NX), turn(x, m % NX), h) for m in range(1, NZ * NX)]
    for peer in greeted:
        pl.semaphore_signal(barrier, inc=1, device_id=peer, device_id_type=MESH)

    def remote(src, dst, send, recv, peer):
        return pltpu.make_async_remote_copy(
            src_ref=src, dst_ref=dst, send_sem=send, recv_sem=recv, device_id=peer, device_id_type=MESH
        )

    def p0(g):
        block = wbuf.at[g, z, x, h]
        return remote(block, block, p0_send.at[g], p0_recv.at[g], h_peer)

    def start_own(g):
        for i in range(3):
            pltpu.make_async_copy(
                w_in.at[i, :, :, pl.ds(g * LANES, LANES)],
                wbuf.at[g, z, x, h, :, :, pl.ds(i * LANES, LANES)],
                loc_sem.at[g],
            ).start()

    def wait_own(g):
        block = wbuf.at[g, z, x, h]
        pltpu.make_async_copy(block, block, loc_sem.at[g]).wait()

    def ring(g, phase, half, way, sender):
        step = -1 if way == 0 else 1
        along_x = (half == 0) == (phase < FIRST_HALF)
        zz, xx = z, x
        if along_x:
            xx = turn(x, sender)
            if phase in (ON, LAST):
                xx = turn(xx, step)
        else:
            zz = turn(z, sender)
            if phase in (ON, LAST):
                zz = turn(zz, step)
        part = wbuf.at[g]
        hh = {NEAR: h, PAIR: 1 - h, ON: way, FIRST_HALF: 0, SECOND_HALF: 1, LAST: way}[phase]
        if phase in (NEAR, PAIR, ON):
            ref = part.at[zz, xx, hh, half]
        else:
            ref = part.at[:, xx, hh, half] if along_x else part.at[zz, :, hh, half]
        peer = (x_peer if along_x else z_peer)[1 if way == 0 else 3]
        slot = ((g * PHASES + phase) * 2 + half) * 2 + way
        return remote(ref, ref, ring_send.at[slot], ring_recv.at[slot], peer)

    def start_ring(g, phase):
        for half in (0, 1):
            for way in (0, 1):
                ring(g, phase, half, way, 0).start()

    def wait_ring(g, phase):
        for half in (0, 1):
            for way in (0, 1):
                ring(g, phase, half, way, -1 if way == 0 else 1).wait_recv()

    def token_copy(which):
        mine = slab.at[tp]
        far = slab.at[2 * (1 - a) + b]
        if which == 0:
            return remote(tokens, mine, tok_send.at[0], tok_recv.at[0], sibling)
        if which == 1:
            return remote(tokens, mine, tok_send.at[1], tok_recv.at[1], across)
        return remote(far, far, tok_send.at[2], tok_recv.at[2], sibling)

    def token_landed(which):
        ref = slab.at[(2 * a + 1 - b, 2 * (1 - a) + b, 2 * (1 - a) + 1 - b)[which]]
        return remote(ref, ref, tok_send.at[which], tok_recv.at[which], sibling)

    for g in range(GROUPS):
        start_own(g)
    tokens_own = pltpu.make_async_copy(tokens, slab.at[tp], loc_sem.at[GROUPS])
    tokens_own.start()
    og_own = pltpu.make_async_copy(og_in, og, loc_sem.at[GROUPS + 1])
    taps_own = pltpu.make_async_copy(taps_in, taps, loc_sem.at[GROUPS + 2])
    og_own.start()
    taps_own.start()
    pl.semaphore_wait(barrier, len(greeted))
    for g in range(GROUPS):
        wait_own(g)
        p0(g).start()
        start_ring(g, NEAR)
    token_copy(1).start()
    token_copy(0).start()

    def land_p0(g):
        block = wbuf.at[g, z, x, 1 - h]
        remote(block, block, p0_send.at[g], p0_recv.at[g], h_peer).wait_recv()

    def first_axis(g, carry):
        land_p0(g)
        start_ring(g, PAIR)
        return carry

    def first_axis_on(g, carry):
        wait_ring(g, NEAR)
        wait_ring(g, PAIR)
        start_ring(g, ON)
        return carry

    def second_axis(g, carry):
        wait_ring(g, ON)
        begin = ((0, FIRST_HALF), (0, SECOND_HALF), (1, FIRST_HALF))
        for i, piece in enumerate(begin):

            @pl.when(g == i)
            def _():
                start_ring(*piece)

        return carry

    lax.fori_loop(0, GROUPS, first_axis, 0)
    lax.fori_loop(0, GROUPS, first_axis_on, 0)
    lax.fori_loop(0, GROUPS, second_axis, 0)

    def filter_spectrum(g, carry):
        t_hi, t_lo = split_bf16(taps[pl.ds(g * LANES, LANES), :])
        hs[g] = dot_nt(f_hi[...], t_hi) + (dot_nt(f_hi[...], t_lo) + dot_nt(f_lo[...], t_hi))
        return carry

    og_own.wait()
    taps_own.wait()
    lax.fori_loop(0, GROUPS, filter_spectrum, 0)

    def clear(i, carry):
        acc[pl.ds(i * 64, 64), :] = jnp.zeros((64, acc.shape[1]), F32)
        return carry

    lax.fori_loop(0, acc.shape[0] // 64, clear, 0)
    depth = NX * NH * TAPS
    wait_ring(0, FIRST_HALF)
    start_ring(1, SECOND_HALF)
    wait_ring(0, SECOND_HALF)
    start_ring(0, LAST)
    wait_ring(1, FIRST_HALF)
    start_ring(2, FIRST_HALF)
    wait_ring(1, SECOND_HALF)
    start_ring(2, SECOND_HALF)

    def halo_up(g):
        return remote(gbuf.at[g, BLOCKS - 1], hg.at[g], halo_send.at[g], halo_recv.at[g], after)

    def halo_down(g):
        return remote(mbuf.at[g, 0], hm.at[g], halo_send.at[GROUPS + g], halo_recv.at[GROUPS + g], before)

    def ar_h(g):
        return remote(fgmine.at[g], fgother.at[g], ar_send.at[g], ar_recv.at[g], h_peer)

    def stage_1(g):
        pacc[...] = dot(slab[...].reshape(BLOCKS * TAPS, NZ * depth), wbuf[g].reshape(NZ * depth, 3 * LANES))
        cols = pl.ds(pl.multiple_of(g * LANES, LANES), LANES)
        qkv[g] = pacc[...].astype(BF16)
        q = qkv[g, :, :LANES].astype(F32)
        k = qkv[g, :, LANES : 2 * LANES].astype(F32)
        v = qkv[g, :, 2 * LANES :].astype(F32)
        gbuf[g] = (k * v).astype(BF16).reshape(BLOCKS, TAPS, LANES)
        mbuf[g] = (og[:, cols].astype(F32) * q).astype(BF16).reshape(BLOCKS, TAPS, LANES)
        halo_up(g).start()
        halo_down(g).start()

    def spectra(g):
        for i in range(BLOCKS):
            vs[i + 1] = dot(f_hi[...], gbuf[g, i])
            us[i] = dot(f_hi[...], mbuf[g, i])

    def halo_spectra(g):
        halo_up(g).wait_recv()
        halo_down(g).wait_recv()
        zero = jnp.zeros((TAPS, LANES), BF16)
        vs[0] = dot(f_hi[...], jnp.where(ctx == 0, zero, hg[g]))
        us[BLOCKS] = dot(f_hi[...], jnp.where(ctx == n_ctx - 1, zero, hm[g]))

    def stage_2(g, blocks):
        cols = pl.ds(pl.multiple_of(g * LANES, LANES), LANES)
        sign = 1.0 - 2.0 * (lax.broadcasted_iota(jnp.int32, (TAPS, LANES), 0) % 2).astype(F32)
        hr, hi = hs[g, :TAPS], hs[g, TAPS:]
        gain = skip[:, cols]
        cr, ci, direct = 0.0, 0.0, 0.0
        for i in blocks:
            rows = slice(i * TAPS, (i + 1) * TAPS)
            xr = vs[i, :TAPS] + sign * vs[i + 1, TAPS:]
            xi = vs[i, TAPS:] - sign * vs[i + 1, :TAPS]
            mr = us[i, :TAPS] + sign * us[i + 1, TAPS:]
            mi = us[i, TAPS:] - sign * us[i + 1, :TAPS]
            dr = sign * us[i, TAPS:]
            di = -sign * us[i, :TAPS]
            cr = cr + (dr * xr + di * xi)
            ci = ci + (di * xr - dr * xi)
            y = jnp.concatenate([hr * xr - hi * xi, hr * xi + hi * xr], 0).astype(BF16)
            w = jnp.concatenate([hr * mr + hi * mi, hr * mi - hi * mr], 0).astype(BF16)
            gf, mf = gbuf[g, i].astype(F32), mbuf[g, i].astype(F32)
            mixed = dot(i_hi[TAPS:, :], y) + gain * gf
            back = dot(i_hi[:TAPS, :], w) + gain * mf
            direct = direct + jnp.sum(gf * mf, 0, keepdims=True)
            qb = qkv[g, rows, :LANES].astype(F32)
            kb = qkv[g, rows, LANES : 2 * LANES].astype(F32)
            vb = qkv[g, rows, 2 * LANES :].astype(F32)
            filt[rows, cols] = (qb * mixed).astype(BF16)
            pg[g, rows, :LANES] = (og[rows, cols].astype(F32) * mixed).astype(BF16)
            pg[g, rows, LANES : 2 * LANES] = (back * vb).astype(BF16)
            pg[g, rows, 2 * LANES :] = (back * kb).astype(BF16)
        return cr, ci, direct

    def keep(sums):
        cross[:TAPS], cross[TAPS:] = sums[0], sums[1]
        straight[...] = sums[2]

    def filter_part(g, sums):
        cr, ci, direct = cross[:TAPS] + sums[0], cross[TAPS:] + sums[1], straight[...] + sums[2]
        c_hi, c_lo = split_bf16(jnp.concatenate([cr, ci], 0))
        i_top = i_hi[:TAPS, :]
        part = dot(i_top, c_hi) + (dot(i_top, c_lo) + dot(i_lo[:TAPS, :], c_hi))
        first = lax.broadcasted_iota(jnp.int32, (TAPS, LANES), 0) == 0
        fgmine[g] = jnp.where(first, direct, part).astype(BF16)
        ar_h(g).start()

    wide = NH * TAPS
    chunk = tgrad.shape[1] // CHUNKS

    def add_terms(groups, c, row_slices):
        at_cols = pl.ds(pl.multiple_of(c * chunk, chunk), chunk)
        count = chunk // wide
        zz, xx = c * count // NX, c * count % NX
        total = 0.0
        for g in groups:
            left = jnp.concatenate([pg[g, r, :] for r in row_slices], 0)
            total = total + dot_nt(left, wbuf[g, zz, pl.ds(xx, count)].reshape(chunk, 3 * LANES))
        done = 0
        for r in row_slices:
            acc[r, at_cols] += total[done : done + r.stop - r.start]
            done += r.stop - r.start

    def group(g, carry):
        wait_ring(g, LAST)

        @pl.when(g == 0)
        def _():
            start_ring(1, LAST)
            token_landed(1).wait_recv()
            token_copy(2).start()
            tokens_own.wait()
            token_landed(0).wait_recv()
            token_landed(2).wait_recv()

        @pl.when(g == 1)
        def _():
            start_ring(3, SECOND_HALF)

        stage_1(g)

        @pl.when(g == 0)
        def _():
            wait_ring(2, FIRST_HALF)
            start_ring(3, FIRST_HALF)
            wait_ring(2, SECOND_HALF)
            start_ring(2, LAST)

        @pl.when(g == 2)
        def _():
            wait_ring(3, FIRST_HALF)
            wait_ring(3, SECOND_HALF)
            start_ring(3, LAST)

        def finish_group(done, carry):
            spectra(done)
            halo_spectra(done)
            keep(stage_2(done, INNER))
            filter_part(done, stage_2(done, OUTER))

            @pl.when(done < 1)
            def _():
                def step(c, carry):
                    add_terms([done], c, [slice(0, BLOCKS * TAPS)])
                    return carry

                lax.fori_loop(0, CHUNKS, step, 0)

            return carry

        begin = jnp.where(g == GROUPS - 1, g, jnp.maximum(g - 1, 0))
        end = jnp.where(g == GROUPS - 2, g + 1, g)
        lax.fori_loop(begin, end, finish_group, 0)
        return carry

    lax.fori_loop(0, GROUPS, group, 0)

    half_chunks = CHUNKS // 2

    def rows_of(t):
        return pl.ds(pl.multiple_of(t * TAPS, TAPS), TAPS)

    def cols_of(c):
        return pl.ds(pl.multiple_of(c * chunk, chunk), chunk)

    def to_core(kind, j):
        n = kind * half_chunks + j
        return remote(ps1.at[n], pr1.at[n], rs_send.at[n], rs_recv.at[n], sibling)

    def to_chip(kind, j):
        n = kind * half_chunks + j
        c = b * half_chunks + j
        peer = {"ctx": ctx, "tp": (2 - a, 3 - 3 * a)[kind]}
        return remote(ps2.at[n], pr2.at[c], rs_send.at[CHUNKS + n], rs_recv.at[CHUNKS + c], peer)

    def to_owner(c):
        return remote(ps3.at[c], pr3.at[c], rs_send.at[2 * CHUNKS + c], rs_recv.at[2 * CHUNKS + c], sibling)

    def scatter(kind):
        row_slices = ([slice(TAPS, 3 * TAPS)], [slice(0, TAPS), slice(3 * TAPS, 4 * TAPS)])[kind]
        far, near = rows_of((2 - a, 3 - 3 * a)[kind]), (1 + a, 3 * a)[kind]

        def step(i, carry):
            side = (b + 1 + i) % 2

            @pl.when(i < CHUNKS)
            def _():
                c = side * half_chunks + i // 2
                add_terms(range(1, GROUPS), c, row_slices)

                @pl.when(i % 2 == 0)
                def _():
                    ps1[kind * half_chunks + i // 2] = acc[far, cols_of(c)].astype(BF16)
                    to_core(kind, i // 2).start()

                @pl.when(tp != near)
                def _():
                    ps3[c] = acc[rows_of(near), cols_of(c)].astype(BF16)
                    to_owner(c).start()

            @pl.when((i > 0) & (i % 2 == 0))
            def _():
                j = i // 2 - 1
                to_core(kind, j).wait_recv()
                n = kind * half_chunks + j
                mine = acc[far, cols_of(b * half_chunks + j)]
                ps2[n] = (mine + pr1[n].astype(F32)).astype(BF16)
                to_chip(kind, j).start()

            return carry

        lax.fori_loop(0, CHUNKS + 1, step, 0)

    others = NZ * NX - 1

    def rows_8(m, sense):
        return pl.ds(pl.multiple_of(32 * turn(z, sense * (m // NX)) + 8 * turn(x, sense * (m % NX)), 8), 8)

    def ar(kind, m, src, dst):
        n = GROUPS + kind * others + m - 1
        return remote(src, dst, ar_send.at[n], ar_recv.at[n], at(turn(z, m // NX), turn(x, m % NX), h))

    def each(act):
        def step(m, carry):
            act(m)
            return carry

        lax.fori_loop(1, others + 1, step, 0)

    last = GROUPS - 1
    early, late = pl.ds(0, last * LANES), pl.ds(last * LANES, LANES)

    def plane(kind, m):
        cols = (early, late)[kind]
        return ar(kind, m, fgbuf.at[rows_8(m, 1), cols], zrecv.at[m - 1, :, cols])

    def back(m):
        mine = fgrad.at[rows_8(0, 1), :]
        return ar(2, m, mine, mine)

    def back_landed(m):
        got = fgrad.at[rows_8(m, -1), :]
        return ar(2, m, got, got)

    def sum_h(g):
        ar_h(g).wait_recv()
        fgbuf[:, g * LANES : (g + 1) * LANES] = fgmine[g].astype(F32) + fgother[g].astype(F32)

    spectra(last)
    keep(stage_2(last, INNER))
    scatter(0)
    for g in range(last):
        sum_h(g)
    each(lambda m: plane(0, m).start())
    halo_spectra(last)
    filter_part(last, stage_2(last, OUTER))
    scatter(1)
    sum_h(last)
    each(lambda m: plane(1, m).start())

    def arrived(m):
        plane(0, m).wait_recv()
        plane(1, m).wait_recv()

    each(arrived)
    total = fgbuf[rows_8(0, 1), :]
    for m in range(others):
        total = total + zrecv[m]
    fgrad[rows_8(0, 1), :] = total * (BLOCKS * TAPS * n_ctx) ** (-0.5)
    each(lambda m: back(m).start())

    def finish(c, carry):
        to_owner(c).wait_recv()
        remote(pr2.at[c], pr2.at[c], rs_send.at[CHUNKS + c], rs_recv.at[CHUNKS + c], across).wait_recv()
        total = acc[rows_of(tp), cols_of(c)] + pr3[c].astype(F32) + pr2[c].astype(F32)
        tgrad[:, cols_of(c)] = total.astype(BF16)
        return carry

    lax.fori_loop(0, CHUNKS, finish, 0)
    each(lambda m: back_landed(m).wait_recv())

    def drain(g, carry):
        p0(g).wait_send()
        halo_up(g).wait_send()
        halo_down(g).wait_send()
        ar_h(g).wait_send()
        for phase in range(PHASES):
            for half in (0, 1):
                for way in (0, 1):
                    ring(g, phase, half, way, 0).wait_send()
        return carry

    def drain_scatter(j, carry):
        for kind in (0, 1):
            to_core(kind, j).wait_send()
            to_chip(kind, j).wait_send()
            to_owner(kind * half_chunks + j).wait_send()
        return carry

    lax.fori_loop(0, GROUPS, drain, 0)
    lax.fori_loop(0, half_chunks, drain_scatter, 0)
    for which in range(3):
        token_copy(which).wait_send()

    def drain_plane(m):
        plane(0, m).wait_send()
        plane(1, m).wait_send()
        back(m).wait_send()

    each(drain_plane)


def hand_out(filt, tgrad, total, filt_out, tgrad_out, fgrad_out, skip_out):
    filt_out[...] = filt[...]
    tgrad_out[...] = tgrad[...]
    fgrad_out[...] = total[...].T
    skip_out[...] = total[:1, :]


def shards(tokens, proj_weight, filter_taps, skip_gain, out_grad):
    rows, width = out_grad.shape
    depth = tokens.shape[1]
    forward, inverse = transforms()
    f_hi, f_lo = split_bf16(jnp.asarray(forward))
    i_hi, i_lo = split_bf16(jnp.asarray(inverse))
    w_in = proj_weight.transpose(1, 0, 2).reshape(3, 2, 64, width)
    vmem = pl.BlockSpec(memory_space=pltpu.VMEM)
    hbm = pl.BlockSpec(memory_space=pl.ANY)
    sem = pltpu.SemaphoreType.DMA
    V = pltpu.VMEM
    filtered, tokens_grad, filter_total = pl.pallas_call(
        kernel,
        out_shape=(
            jax.ShapeDtypeStruct((rows, width), BF16),
            jax.ShapeDtypeStruct((TAPS, depth), BF16),
            jax.ShapeDtypeStruct((TAPS, width), F32),
        ),
        in_specs=[hbm, hbm, hbm, vmem, hbm] + [vmem] * 4,
        out_specs=(vmem, vmem, vmem),
        scratch_shapes=[
            V((width, TAPS), F32),
            V((rows, width), BF16),
            V((GROUPS, NZ, NX, NH, 2, 64, 3 * LANES), BF16),
            V((BLOCKS, TAPS, depth), BF16),
            V((rows, depth), F32),
            V((rows, 3 * LANES), F32),
            V((GROUPS, rows, 3 * LANES), BF16),
            V((GROUPS, rows, 3 * LANES), BF16),
            V((GROUPS, BLOCKS, TAPS, LANES), BF16),
            V((GROUPS, BLOCKS, TAPS, LANES), BF16),
            V((GROUPS, TAPS, LANES), BF16),
            V((GROUPS, TAPS, LANES), BF16),
            V((BLOCKS + 1, 2 * TAPS, LANES), F32),
            V((BLOCKS + 1, 2 * TAPS, LANES), F32),
            V((GROUPS, 2 * TAPS, LANES), F32),
            V((2 * TAPS, LANES), F32),
            V((1, LANES), F32),
            V((GROUPS, TAPS, LANES), BF16),
            V((GROUPS, TAPS, LANES), BF16),
            V((TAPS, width), F32),
            V((NZ * NX - 1, 8, width), F32),
        ]
        + [V((CHUNKS, TAPS, depth // CHUNKS), BF16)] * 6
        + [
            sem((GROUPS + 3,)),
            sem((GROUPS,)),
            sem((GROUPS,)),
            sem((GROUPS * 4 * PHASES,)),
            sem((GROUPS * 4 * PHASES,)),
            sem((3,)),
            sem((3,)),
            sem((2 * GROUPS,)),
            sem((2 * GROUPS,)),
            sem((3 * CHUNKS,)),
            sem((3 * CHUNKS,)),
            sem((GROUPS + 3 * (NZ * NX - 1),)),
            sem((GROUPS + 3 * (NZ * NX - 1),)),
        ],
        compiler_params=pltpu.CompilerParams(
            collective_id=0, has_side_effects=True, vmem_limit_bytes=58 * 2**20
        ),
    )(tokens, w_in, filter_taps, skip_gain[None, :], out_grad, f_hi, f_lo, i_hi, i_lo)
    filtered, tokens_grad, filter_grad, skip_grad = pl.pallas_call(
        hand_out,
        out_shape=(
            jax.ShapeDtypeStruct((rows, width), BF16),
            jax.ShapeDtypeStruct((TAPS, depth), BF16),
            jax.ShapeDtypeStruct((width, TAPS), F32),
            jax.ShapeDtypeStruct((1, width), F32),
        ),
        in_specs=[vmem] * 3,
        out_specs=(vmem,) * 4,
    )(filtered, tokens_grad, filter_total)
    return filtered, tokens_grad, filter_grad, skip_grad[0]


def solution(mesh):
    placed = (P(("ctx", "tp"), None), P("ctx", None, "tp"), P("tp", None), P("tp"), P("ctx", "tp"))
    return jax.shard_map(
        shards,
        mesh=mesh,
        in_specs=placed,
        out_specs=(P("ctx", "tp"), P(("ctx", "tp"), None), P("tp", None), P("tp")),
        check_vma=False,
    )
```

```python
import functools

import numpy as np
import jax
import jax.numpy as jnp
from jax import lax
from jax.experimental import pallas as pl
from jax.experimental.pallas import tpu as pltpu
from jax.sharding import PartitionSpec as P

MESH = pl.DeviceIdType.MESH
F32 = jnp.float32
BF16 = jnp.bfloat16
TAPS = 128
LANES = 128
BLOCKS = 4
GROUPS = 4
NZ, NX, NH = 4, 4, 2
NEAR, PAIR, ON, FIRST_HALF, SECOND_HALF, LAST = range(6)
PHASES = 6
INNER, OUTER = (1, 2), (0, 3)
CHUNKS = 8


def transforms():
    k = np.arange(TAPS)[:, None]
    n = np.arange(2 * TAPS)[None, :]
    angle = np.pi * (2 * k + 1) * n / (2 * TAPS)
    both = np.concatenate([np.cos(angle), -np.sin(angle)], 0)
    return both[:, :TAPS].astype(np.float32), (both.T / TAPS).astype(np.float32)


def split_bf16(m):
    hi = m.astype(BF16)
    return hi, (m - hi.astype(F32)).astype(BF16)


def dot(a, b):
    return jnp.dot(a, b, preferred_element_type=F32)


def dot_nt(a, b):
    return lax.dot_general(a, b, (((1,), (1,)), ((), ())), preferred_element_type=F32)


def kernel(
    tokens, w_in, taps_in, skip, og_in, f_hi, f_lo, i_hi, i_lo,
    filt, tgrad, fgrad,
    taps, og, wbuf, slab, acc, pacc, qkv, pg, gbuf, mbuf, hg, hm, vs, us, hs,
    cross, straight, fgmine, fgother, fgbuf, zrecv,
    ps1, pr1, ps2, pr2, ps3, pr3,
    loc_sem, p0_send, p0_recv, ring_send, ring_recv, tok_send, tok_recv, halo_send, halo_recv,
    rs_send, rs_recv, ar_send, ar_recv,
):
    ctx = lax.axis_index("ctx")
    tp = lax.axis_index("tp")
    n_ctx = NZ * NX * NH
    z, x, h = ctx // (NX * NH), (ctx // NH) % NX, ctx % NH
    a, b = tp // 2, tp % 2

    def at(zz, xx, hh):
        return {"ctx": (zz * NX + xx) * NH + hh, "tp": tp}

    def turn(v, by):
        return (v + by + 4) % 4

    sibling = {"ctx": ctx, "tp": 2 * a + 1 - b}
    across = {"ctx": ctx, "tp": 2 * (1 - a) + b}
    far_sibling = {"ctx": ctx, "tp": 2 * (1 - a) + 1 - b}
    after = {"ctx": (ctx + 1) % n_ctx, "tp": tp}
    before = {"ctx": (ctx + n_ctx - 1) % n_ctx, "tp": tp}
    h_peer = at(z, x, 1 - h)
    z_peer = [None] + [at(turn(z, d), x, h) for d in (1, 2, 3)]
    x_peer = [None] + [at(z, turn(x, d), h) for d in (1, 2, 3)]

    barrier = pltpu.get_barrier_semaphore()
    greeted = [sibling, across, far_sibling, after, before, h_peer]
    greeted = greeted + [at(turn(z, m // NX), turn(x, m % NX), h) for m in range(1, NZ * NX)]
    for peer in greeted:
        pl.semaphore_signal(barrier, inc=1, device_id=peer, device_id_type=MESH)

    def remote(src, dst, send, recv, peer):
        return pltpu.make_async_remote_copy(
            src_ref=src, dst_ref=dst, send_sem=send, recv_sem=recv, device_id=peer, device_id_type=MESH
        )

    def p0(g):
        block = wbuf.at[g, z, x, h]
        return remote(block, block, p0_send.at[g], p0_recv.at[g], h_peer)

    def start_own(g):
        for i in range(3):
            pltpu.make_async_copy(
                w_in.at[i, :, :, pl.ds(g * LANES, LANES)],
                wbuf.at[g, z, x, h, :, :, pl.ds(i * LANES, LANES)],
                loc_sem.at[g],
            ).start()

    def wait_own(g):
        block = wbuf.at[g, z, x, h]
        pltpu.make_async_copy(block, block, loc_sem.at[g]).wait()

    def ring(g, phase, half, way, sender):
        step = -1 if way == 0 else 1
        along_x = (half == 0) == (phase < FIRST_HALF)
        zz, xx = z, x
        if along_x:
            xx = turn(x, sender)
            if phase in (ON, LAST):
                xx = turn(xx, step)
        else:
            zz = turn(z, sender)
            if phase in (ON, LAST):
                zz = turn(zz, step)
        part = wbuf.at[g]
        hh = {NEAR: h, PAIR: 1 - h, ON: way, FIRST_HALF: 0, SECOND_HALF: 1, LAST: way}[phase]
        if phase in (NEAR, PAIR, ON):
            ref = part.at[zz, xx, hh, half]
        else:
            ref = part.at[:, xx, hh, half] if along_x else part.at[zz, :, hh, half]
        peer = (x_peer if along_x else z_peer)[1 if way == 0 else 3]
        slot = ((g * PHASES + phase) * 2 + half) * 2 + way
        return remote(ref, ref, ring_send.at[slot], ring_recv.at[slot], peer)

    def start_ring(g, phase):
        for half in (0, 1):
            for way in (0, 1):
                ring(g, phase, half, way, 0).start()

    def wait_ring(g, phase):
        for half in (0, 1):
            for way in (0, 1):
                ring(g, phase, half, way, -1 if way == 0 else 1).wait_recv()

    def token_copy(which):
        mine = slab.at[tp]
        far = slab.at[2 * (1 - a) + b]
        if which == 0:
            return remote(tokens, mine, tok_send.at[0], tok_recv.at[0], sibling)
        if which == 1:
            return remote(tokens, mine, tok_send.at[1], tok_recv.at[1], across)
        return remote(far, far, tok_send.at[2], tok_recv.at[2], sibling)

    def token_landed(which):
        ref = slab.at[(2 * a + 1 - b, 2 * (1 - a) + b, 2 * (1 - a) + 1 - b)[which]]
        return remote(ref, ref, tok_send.at[which], tok_recv.at[which], sibling)

    for g in range(GROUPS):
        start_own(g)
    tokens_own = pltpu.make_async_copy(tokens, slab.at[tp], loc_sem.at[GROUPS])
    tokens_own.start()
    og_own = pltpu.make_async_copy(og_in, og, loc_sem.at[GROUPS + 1])
    taps_own = pltpu.make_async_copy(taps_in, taps, loc_sem.at[GROUPS + 2])
    og_own.start()
    taps_own.start()
    pl.semaphore_wait(barrier, len(greeted))
    for g in range(GROUPS):
        wait_own(g)
        p0(g).start()
        start_ring(g, NEAR)
    token_copy(1).start()
    token_copy(0).start()

    def land_p0(g):
        block = wbuf.at[g, z, x, 1 - h]
        remote(block, block, p0_send.at[g], p0_recv.at[g], h_peer).wait_recv()

    def first_axis(g, carry):
        land_p0(g)
        start_ring(g, PAIR)
        return carry

    def first_axis_on(g, carry):
        wait_ring(g, NEAR)
        wait_ring(g, PAIR)
        start_ring(g, ON)
        return carry

    def second_axis(g, carry):
        wait_ring(g, ON)
        begin = ((0, FIRST_HALF), (0, SECOND_HALF), (1, FIRST_HALF))
        for i, piece in enumerate(begin):

            @pl.when(g == i)
            def _():
                start_ring(*piece)

        return carry

    lax.fori_loop(0, GROUPS, first_axis, 0)
    lax.fori_loop(0, GROUPS, first_axis_on, 0)
    lax.fori_loop(0, GROUPS, second_axis, 0)

    def filter_spectrum(g, carry):
        t_hi, t_lo = split_bf16(taps[pl.ds(g * LANES, LANES), :])
        hs[g] = dot_nt(f_hi[...], t_hi) + (dot_nt(f_hi[...], t_lo) + dot_nt(f_lo[...], t_hi))
        return carry

    og_own.wait()
    taps_own.wait()
    lax.fori_loop(0, GROUPS, filter_spectrum, 0)

    def clear(i, carry):
        acc[pl.ds(i * 64, 64), :] = jnp.zeros((64, acc.shape[1]), F32)
        return carry

    lax.fori_loop(0, acc.shape[0] // 64, clear, 0)
    depth = NX * NH * TAPS
    wait_ring(0, FIRST_HALF)
    start_ring(1, SECOND_HALF)
    wait_ring(0, SECOND_HALF)
    start_ring(0, LAST)
    wait_ring(1, FIRST_HALF)
    start_ring(2, FIRST_HALF)
    wait_ring(1, SECOND_HALF)
    start_ring(2, SECOND_HALF)

    def halo_up(g):
        return remote(gbuf.at[g, BLOCKS - 1], hg.at[g], halo_send.at[g], halo_recv.at[g], after)

    def halo_down(g):
        return remote(mbuf.at[g, 0], hm.at[g], halo_send.at[GROUPS + g], halo_recv.at[GROUPS + g], before)

    def ar_h(g):
        return remote(fgmine.at[g], fgother.at[g], ar_send.at[g], ar_recv.at[g], h_peer)

    def stage_1(g):
        pacc[...] = dot(slab[...].reshape(BLOCKS * TAPS, NZ * depth), wbuf[g].reshape(NZ * depth, 3 * LANES))
        cols = pl.ds(pl.multiple_of(g * LANES, LANES), LANES)
        qkv[g] = pacc[...].astype(BF16)
        q = qkv[g, :, :LANES].astype(F32)
        k = qkv[g, :, LANES : 2 * LANES].astype(F32)
        v = qkv[g, :, 2 * LANES :].astype(F32)
        gbuf[g] = (k * v).astype(BF16).reshape(BLOCKS, TAPS, LANES)
        mbuf[g] = (og[:, cols].astype(F32) * q).astype(BF16).reshape(BLOCKS, TAPS, LANES)
        halo_up(g).start()
        halo_down(g).start()

    def forward(block):
        return dot(f_hi[...], block) + dot(f_lo[...], block)

    def inverse(half, re, im):
        rows = slice(half * TAPS, (half + 1) * TAPS)
        hi, lo = split_bf16(jnp.concatenate([re, im], 0))
        return dot(i_hi[rows, :], hi) + (dot(i_hi[rows, :], lo) + dot(i_lo[rows, :], hi))

    def spectra(g):
        for i in range(BLOCKS):
            vs[i + 1] = forward(gbuf[g, i])
            us[i] = forward(mbuf[g, i])

    def halo_spectra(g):
        halo_up(g).wait_recv()
        halo_down(g).wait_recv()
        zero = jnp.zeros((TAPS, LANES), BF16)
        vs[0] = forward(jnp.where(ctx == 0, zero, hg[g]))
        us[BLOCKS] = forward(jnp.where(ctx == n_ctx - 1, zero, hm[g]))

    def stage_2(g, blocks):
        cols = pl.ds(pl.multiple_of(g * LANES, LANES), LANES)
        sign = 1.0 - 2.0 * (lax.broadcasted_iota(jnp.int32, (TAPS, LANES), 0) % 2).astype(F32)
        hr, hi = hs[g, :TAPS], hs[g, TAPS:]
        gain = skip[:, cols]
        cr, ci, direct = 0.0, 0.0, 0.0
        for i in blocks:
            rows = slice(i * TAPS, (i + 1) * TAPS)
            xr = vs[i, :TAPS] + sign * vs[i + 1, TAPS:]
            xi = vs[i, TAPS:] - sign * vs[i + 1, :TAPS]
            mr = us[i, :TAPS] + sign * us[i + 1, TAPS:]
            mi = us[i, TAPS:] - sign * us[i + 1, :TAPS]
            dr = sign * us[i, TAPS:]
            di = -sign * us[i, :TAPS]
            cr = cr + (dr * xr + di * xi)
            ci = ci + (di * xr - dr * xi)
            gf, mf = gbuf[g, i].astype(F32), mbuf[g, i].astype(F32)
            mixed = inverse(1, hr * xr - hi * xi, hr * xi + hi * xr) + gain * gf
            back = inverse(0, hr * mr + hi * mi, hr * mi - hi * mr) + gain * mf
            direct = direct + jnp.sum(gf * mf, 0, keepdims=True)
            qb = qkv[g, rows, :LANES].astype(F32)
            kb = qkv[g, rows, LANES : 2 * LANES].astype(F32)
            vb = qkv[g, rows, 2 * LANES :].astype(F32)
            filt[rows, cols] = (qb * mixed).astype(BF16)
            pg[g, rows, :LANES] = (og[rows, cols].astype(F32) * mixed).astype(BF16)
            pg[g, rows, LANES : 2 * LANES] = (back * vb).astype(BF16)
            pg[g, rows, 2 * LANES :] = (back * kb).astype(BF16)
        return cr, ci, direct

    def keep(sums):
        cross[:TAPS], cross[TAPS:] = sums[0], sums[1]
        straight[...] = sums[2]

    def filter_part(g, sums):
        cr, ci, direct = cross[:TAPS] + sums[0], cross[TAPS:] + sums[1], straight[...] + sums[2]
        part = inverse(0, cr, ci)
        first = lax.broadcasted_iota(jnp.int32, (TAPS, LANES), 0) == 0
        fgmine[g] = jnp.where(first, direct, part).astype(BF16)
        ar_h(g).start()

    wide = NH * TAPS
    chunk = tgrad.shape[1] // CHUNKS

    def add_terms(groups, c, row_slices):
        at_cols = pl.ds(pl.multiple_of(c * chunk, chunk), chunk)
        count = chunk // wide
        zz, xx = c * count // NX, c * count % NX
        total = 0.0
        for g in groups:
            left = jnp.concatenate([pg[g, r, :] for r in row_slices], 0)
            total = total + dot_nt(left, wbuf[g, zz, pl.ds(xx, count)].reshape(chunk, 3 * LANES))
        done = 0
        for r in row_slices:
            acc[r, at_cols] += total[done : done + r.stop - r.start]
            done += r.stop - r.start

    def group(g, carry):
        wait_ring(g, LAST)

        @pl.when(g == 0)
        def _():
            start_ring(1, LAST)
            token_landed(1).wait_recv()
            token_copy(2).start()
            tokens_own.wait()
            token_landed(0).wait_recv()
            token_landed(2).wait_recv()

        @pl.when(g == 1)
        def _():
            start_ring(3, SECOND_HALF)

        stage_1(g)

        @pl.when(g == 0)
        def _():
            wait_ring(2, FIRST_HALF)
            start_ring(3, FIRST_HALF)
            wait_ring(2, SECOND_HALF)
            start_ring(2, LAST)

        @pl.when(g == 2)
        def _():
            wait_ring(3, FIRST_HALF)
            wait_ring(3, SECOND_HALF)
            start_ring(3, LAST)

        def finish_group(done, carry):
            spectra(done)
            halo_spectra(done)
            keep(stage_2(done, INNER))
            filter_part(done, stage_2(done, OUTER))

            @pl.when(done < 1)
            def _():
                def step(c, carry):
                    add_terms([done], c, [slice(0, BLOCKS * TAPS)])
                    return carry

                lax.fori_loop(0, CHUNKS, step, 0)

            return carry

        begin = jnp.where(g == GROUPS - 1, g, jnp.maximum(g - 1, 0))
        end = jnp.where(g == GROUPS - 2, g + 1, g)
        lax.fori_loop(begin, end, finish_group, 0)
        return carry

    lax.fori_loop(0, GROUPS, group, 0)

    half_chunks = CHUNKS // 2

    def rows_of(t):
        return pl.ds(pl.multiple_of(t * TAPS, TAPS), TAPS)

    def cols_of(c):
        return pl.ds(pl.multiple_of(c * chunk, chunk), chunk)

    def to_core(kind, j):
        n = kind * half_chunks + j
        return remote(ps1.at[n], pr1.at[n], rs_send.at[n], rs_recv.at[n], sibling)

    def to_chip(kind, j):
        n = kind * half_chunks + j
        c = b * half_chunks + j
        peer = {"ctx": ctx, "tp": (2 - a, 3 - 3 * a)[kind]}
        return remote(ps2.at[n], pr2.at[c], rs_send.at[CHUNKS + n], rs_recv.at[CHUNKS + c], peer)

    def to_owner(c):
        return remote(ps3.at[c], pr3.at[c], rs_send.at[2 * CHUNKS + c], rs_recv.at[2 * CHUNKS + c], sibling)

    def scatter(kind):
        row_slices = ([slice(TAPS, 3 * TAPS)], [slice(0, TAPS), slice(3 * TAPS, 4 * TAPS)])[kind]
        far, near = rows_of((2 - a, 3 - 3 * a)[kind]), (1 + a, 3 * a)[kind]

        def step(i, carry):
            side = (b + 1 + i) % 2

            @pl.when(i < CHUNKS)
            def _():
                c = side * half_chunks + i // 2
                add_terms(range(1, GROUPS), c, row_slices)

                @pl.when(i % 2 == 0)
                def _():
                    ps1[kind * half_chunks + i // 2] = acc[far, cols_of(c)].astype(BF16)
                    to_core(kind, i // 2).start()

                @pl.when(tp != near)
                def _():
                    ps3[c] = acc[rows_of(near), cols_of(c)].astype(BF16)
                    to_owner(c).start()

            @pl.when((i > 0) & (i % 2 == 0))
            def _():
                j = i // 2 - 1
                to_core(kind, j).wait_recv()
                n = kind * half_chunks + j
                mine = acc[far, cols_of(b * half_chunks + j)]
                ps2[n] = (mine + pr1[n].astype(F32)).astype(BF16)
                to_chip(kind, j).start()

            return carry

        lax.fori_loop(0, CHUNKS + 1, step, 0)

    others = NZ * NX - 1

    def rows_8(m, sense):
        return pl.ds(pl.multiple_of(32 * turn(z, sense * (m // NX)) + 8 * turn(x, sense * (m % NX)), 8), 8)

    def ar(kind, m, src, dst):
        n = GROUPS + kind * others + m - 1
        return remote(src, dst, ar_send.at[n], ar_recv.at[n], at(turn(z, m // NX), turn(x, m % NX), h))

    def each(act):
        def step(m, carry):
            act(m)
            return carry

        lax.fori_loop(1, others + 1, step, 0)

    last = GROUPS - 1
    early, late = pl.ds(0, last * LANES), pl.ds(last * LANES, LANES)

    def plane(kind, m):
        cols = (early, late)[kind]
        return ar(kind, m, fgbuf.at[rows_8(m, 1), cols], zrecv.at[m - 1, :, cols])

    def back(m):
        mine = fgrad.at[rows_8(0, 1), :]
        return ar(2, m, mine, mine)

    def back_landed(m):
        got = fgrad.at[rows_8(m, -1), :]
        return ar(2, m, got, got)

    def sum_h(g):
        ar_h(g).wait_recv()
        fgbuf[:, g * LANES : (g + 1) * LANES] = fgmine[g].astype(F32) + fgother[g].astype(F32)

    spectra(last)
    keep(stage_2(last, INNER))
    scatter(0)
    for g in range(last):
        sum_h(g)
    each(lambda m: plane(0, m).start())
    halo_spectra(last)
    filter_part(last, stage_2(last, OUTER))
    scatter(1)
    sum_h(last)
    each(lambda m: plane(1, m).start())

    def arrived(m):
        plane(0, m).wait_recv()
        plane(1, m).wait_recv()

    each(arrived)
    total = fgbuf[rows_8(0, 1), :]
    for m in range(others):
        total = total + zrecv[m]
    fgrad[rows_8(0, 1), :] = total * (BLOCKS * TAPS * n_ctx) ** (-0.5)
    each(lambda m: back(m).start())

    def finish(c, carry):
        to_owner(c).wait_recv()
        remote(pr2.at[c], pr2.at[c], rs_send.at[CHUNKS + c], rs_recv.at[CHUNKS + c], across).wait_recv()
        total = acc[rows_of(tp), cols_of(c)] + pr3[c].astype(F32) + pr2[c].astype(F32)
        tgrad[:, cols_of(c)] = total.astype(BF16)
        return carry

    lax.fori_loop(0, CHUNKS, finish, 0)
    each(lambda m: back_landed(m).wait_recv())

    def drain(g, carry):
        p0(g).wait_send()
        halo_up(g).wait_send()
        halo_down(g).wait_send()
        ar_h(g).wait_send()
        for phase in range(PHASES):
            for half in (0, 1):
                for way in (0, 1):
                    ring(g, phase, half, way, 0).wait_send()
        return carry

    def drain_scatter(j, carry):
        for kind in (0, 1):
            to_core(kind, j).wait_send()
            to_chip(kind, j).wait_send()
            to_owner(kind * half_chunks + j).wait_send()
        return carry

    lax.fori_loop(0, GROUPS, drain, 0)
    lax.fori_loop(0, half_chunks, drain_scatter, 0)
    for which in range(3):
        token_copy(which).wait_send()

    def drain_plane(m):
        plane(0, m).wait_send()
        plane(1, m).wait_send()
        back(m).wait_send()

    each(drain_plane)


def hand_out(filt, tgrad, total, filt_out, tgrad_out, fgrad_out, skip_out):
    filt_out[...] = filt[...]
    tgrad_out[...] = tgrad[...]
    fgrad_out[...] = total[...].T
    skip_out[...] = total[:1, :]


def shards(tokens, proj_weight, filter_taps, skip_gain, out_grad):
    rows, width = out_grad.shape
    depth = tokens.shape[1]
    forward, inverse = transforms()
    f_hi, f_lo = split_bf16(jnp.asarray(forward))
    i_hi, i_lo = split_bf16(jnp.asarray(inverse))
    w_in = proj_weight.transpose(1, 0, 2).reshape(3, 2, 64, width)
    vmem = pl.BlockSpec(memory_space=pltpu.VMEM)
    hbm = pl.BlockSpec(memory_space=pl.ANY)
    sem = pltpu.SemaphoreType.DMA
    V = pltpu.VMEM
    filtered, tokens_grad, filter_total = pl.pallas_call(
        kernel,
        out_shape=(
            jax.ShapeDtypeStruct((rows, width), BF16),
            jax.ShapeDtypeStruct((TAPS, depth), BF16),
            jax.ShapeDtypeStruct((TAPS, width), F32),
        ),
        in_specs=[hbm, hbm, hbm, vmem, hbm] + [vmem] * 4,
        out_specs=(vmem, vmem, vmem),
        scratch_shapes=[
            V((width, TAPS), F32),
            V((rows, width), BF16),
            V((GROUPS, NZ, NX, NH, 2, 64, 3 * LANES), BF16),
            V((BLOCKS, TAPS, depth), BF16),
            V((rows, depth), F32),
            V((rows, 3 * LANES), F32),
            V((GROUPS, rows, 3 * LANES), BF16),
            V((GROUPS, rows, 3 * LANES), BF16),
            V((GROUPS, BLOCKS, TAPS, LANES), BF16),
            V((GROUPS, BLOCKS, TAPS, LANES), BF16),
            V((GROUPS, TAPS, LANES), BF16),
            V((GROUPS, TAPS, LANES), BF16),
            V((BLOCKS + 1, 2 * TAPS, LANES), F32),
            V((BLOCKS + 1, 2 * TAPS, LANES), F32),
            V((GROUPS, 2 * TAPS, LANES), F32),
            V((2 * TAPS, LANES), F32),
            V((1, LANES), F32),
            V((GROUPS, TAPS, LANES), BF16),
            V((GROUPS, TAPS, LANES), BF16),
            V((TAPS, width), F32),
            V((NZ * NX - 1, 8, width), F32),
        ]
        + [V((CHUNKS, TAPS, depth // CHUNKS), BF16)] * 6
        + [
            sem((GROUPS + 3,)),
            sem((GROUPS,)),
            sem((GROUPS,)),
            sem((GROUPS * 4 * PHASES,)),
            sem((GROUPS * 4 * PHASES,)),
            sem((3,)),
            sem((3,)),
            sem((2 * GROUPS,)),
            sem((2 * GROUPS,)),
            sem((3 * CHUNKS,)),
            sem((3 * CHUNKS,)),
            sem((GROUPS + 3 * (NZ * NX - 1),)),
            sem((GROUPS + 3 * (NZ * NX - 1),)),
        ],
        compiler_params=pltpu.CompilerParams(
            collective_id=0, has_side_effects=True, vmem_limit_bytes=58 * 2**20
        ),
    )(tokens, w_in, filter_taps, skip_gain[None, :], out_grad, f_hi, f_lo, i_hi, i_lo)
    filtered, tokens_grad, filter_grad, skip_grad = pl.pallas_call(
        hand_out,
        out_shape=(
            jax.ShapeDtypeStruct((rows, width), BF16),
            jax.ShapeDtypeStruct((TAPS, depth), BF16),
            jax.ShapeDtypeStruct((width, TAPS), F32),
            jax.ShapeDtypeStruct((1, width), F32),
        ),
        in_specs=[vmem] * 3,
        out_specs=(vmem,) * 4,
    )(filtered, tokens_grad, filter_total)
    return filtered, tokens_grad, filter_grad, skip_grad[0]


def solution(mesh):
    placed = (P(("ctx", "tp"), None), P("ctx", None, "tp"), P("tp", None), P("tp"), P("ctx", "tp"))
    return jax.shard_map(
        shards,
        mesh=mesh,
        in_specs=placed,
        out_specs=(P("ctx", "tp"), P(("ctx", "tp"), None), P("tp", None), P("tp")),
        check_vma=False,
    )
```

```python
import functools

import numpy as np
import jax
import jax.numpy as jnp
from jax import lax
from jax.experimental import pallas as pl
from jax.experimental.pallas import tpu as pltpu
from jax.sharding import PartitionSpec as P

MESH = pl.DeviceIdType.MESH
F32 = jnp.float32
BF16 = jnp.bfloat16
TAPS = 128
LANES = 128
BLOCKS = 4
GROUPS = 4
NZ, NX, NH = 4, 4, 2
NEAR, PAIR, ON, FIRST_HALF, SECOND_HALF, LAST = range(6)
PHASES = 6
INNER, OUTER = (1, 2), (0, 3)
CHUNKS = 8


def transforms():
    k = np.arange(TAPS)[:, None]
    n = np.arange(2 * TAPS)[None, :]
    angle = np.pi * (2 * k + 1) * n / (2 * TAPS)
    both = np.concatenate([np.cos(angle), -np.sin(angle)], 0)
    return both[:, :TAPS].astype(np.float32), (both.T / TAPS).astype(np.float32)


def split_bf16(m):
    hi = m.astype(BF16)
    return hi, (m - hi.astype(F32)).astype(BF16)


def dot(a, b):
    return jnp.dot(a, b, preferred_element_type=F32)


def dot_nt(a, b):
    return lax.dot_general(a, b, (((1,), (1,)), ((), ())), preferred_element_type=F32)


def kernel(
    tokens, w_in, taps_in, skip, og_in, f_hi, f_lo, i_hi, i_lo,
    filt, tgrad, fgrad,
    taps, og, wbuf, slab, acc, pacc, qkv, pg, gbuf, mbuf, hg, hm, vs, us, hs,
    cross, straight, fgmine, fgother, fgbuf, zrecv,
    ps1, pr1, ps2, pr2, ps3, pr3,
    loc_sem, p0_send, p0_recv, ring_send, ring_recv, tok_send, tok_recv, halo_send, halo_recv,
    rs_send, rs_recv, ar_send, ar_recv,
):
    ctx = lax.axis_index("ctx")
    tp = lax.axis_index("tp")
    n_ctx = NZ * NX * NH
    z, x, h = ctx // (NX * NH), (ctx // NH) % NX, ctx % NH
    a, b = tp // 2, tp % 2

    def at(zz, xx, hh):
        return {"ctx": (zz * NX + xx) * NH + hh, "tp": tp}

    def turn(v, by):
        return (v + by + 4) % 4

    sibling = {"ctx": ctx, "tp": 2 * a + 1 - b}
    across = {"ctx": ctx, "tp": 2 * (1 - a) + b}
    far_sibling = {"ctx": ctx, "tp": 2 * (1 - a) + 1 - b}
    after = {"ctx": (ctx + 1) % n_ctx, "tp": tp}
    before = {"ctx": (ctx + n_ctx - 1) % n_ctx, "tp": tp}
    h_peer = at(z, x, 1 - h)
    z_peer = [None] + [at(turn(z, d), x, h) for d in (1, 2, 3)]
    x_peer = [None] + [at(z, turn(x, d), h) for d in (1, 2, 3)]

    barrier = pltpu.get_barrier_semaphore()
    greeted = [sibling, across, far_sibling, after, before, h_peer]
    greeted = greeted + [at(turn(z, m // NX), turn(x, m % NX), h) for m in range(1, NZ * NX)]
    for peer in greeted:
        pl.semaphore_signal(barrier, inc=1, device_id=peer, device_id_type=MESH)

    def remote(src, dst, send, recv, peer):
        return pltpu.make_async_remote_copy(
            src_ref=src, dst_ref=dst, send_sem=send, recv_sem=recv, device_id=peer, device_id_type=MESH
        )

    def p0(g):
        block = wbuf.at[g, z, x, h]
        return remote(block, block, p0_send.at[g], p0_recv.at[g], h_peer)

    def start_own(g):
        for i in range(3):
            pltpu.make_async_copy(
                w_in.at[i, :, :, pl.ds(g * LANES, LANES)],
                wbuf.at[g, z, x, h, :, :, pl.ds(i * LANES, LANES)],
                loc_sem.at[g],
            ).start()

    def wait_own(g):
        block = wbuf.at[g, z, x, h]
        pltpu.make_async_copy(block, block, loc_sem.at[g]).wait()

    def ring(g, phase, half, way, sender):
        step = -1 if way == 0 else 1
        along_x = (half == 0) == (phase < FIRST_HALF)
        zz, xx = z, x
        if along_x:
            xx = turn(x, sender)
            if phase in (ON, LAST):
                xx = turn(xx, step)
        else:
            zz = turn(z, sender)
            if phase in (ON, LAST):
                zz = turn(zz, step)
        part = wbuf.at[g]
        hh = {NEAR: h, PAIR: 1 - h, ON: way, FIRST_HALF: 0, SECOND_HALF: 1, LAST: way}[phase]
        if phase in (NEAR, PAIR, ON):
            ref = part.at[zz, xx, hh, half]
        else:
            ref = part.at[:, xx, hh, half] if along_x else part.at[zz, :, hh, half]
        peer = (x_peer if along_x else z_peer)[1 if way == 0 else 3]
        slot = ((g * PHASES + phase) * 2 + half) * 2 + way
        return remote(ref, ref, ring_send.at[slot], ring_recv.at[slot], peer)

    def start_ring(g, phase):
        for half in (0, 1):
            for way in (0, 1):
                ring(g, phase, half, way, 0).start()

    def wait_ring(g, phase):
        for half in (0, 1):
            for way in (0, 1):
                ring(g, phase, half, way, -1 if way == 0 else 1).wait_recv()

    def token_copy(which):
        mine = slab.at[tp]
        far = slab.at[2 * (1 - a) + b]
        if which == 0:
            return remote(tokens, mine, tok_send.at[0], tok_recv.at[0], sibling)
        if which == 1:
            return remote(tokens, mine, tok_send.at[1], tok_recv.at[1], across)
        return remote(far, far, tok_send.at[2], tok_recv.at[2], sibling)

    def token_landed(which):
        ref = slab.at[(2 * a + 1 - b, 2 * (1 - a) + b, 2 * (1 - a) + 1 - b)[which]]
        return remote(ref, ref, tok_send.at[which], tok_recv.at[which], sibling)

    for g in range(GROUPS):
        start_own(g)
    tokens_own = pltpu.make_async_copy(tokens, slab.at[tp], loc_sem.at[GROUPS])
    tokens_own.start()
    og_own = pltpu.make_async_copy(og_in, og, loc_sem.at[GROUPS + 1])
    taps_own = pltpu.make_async_copy(taps_in, taps, loc_sem.at[GROUPS + 2])
    og_own.start()
    taps_own.start()
    pl.semaphore_wait(barrier, len(greeted))
    for g in range(GROUPS):
        wait_own(g)
        p0(g).start()
        start_ring(g, NEAR)
    token_copy(1).start()
    token_copy(0).start()

    def land_p0(g):
        block = wbuf.at[g, z, x, 1 - h]
        remote(block, block, p0_send.at[g], p0_recv.at[g], h_peer).wait_recv()

    def first_axis(g, carry):
        land_p0(g)
        start_ring(g, PAIR)
        return carry

    def first_axis_on(g, carry):
        wait_ring(g, NEAR)
        wait_ring(g, PAIR)
        start_ring(g, ON)
        return carry

    def second_axis(g, carry):
        wait_ring(g, ON)
        begin = ((0, FIRST_HALF), (0, SECOND_HALF), (1, FIRST_HALF))
        for i, piece in enumerate(begin):

            @pl.when(g == i)
            def _():
                start_ring(*piece)

        return carry

    lax.fori_loop(0, GROUPS, first_axis, 0)
    lax.fori_loop(0, GROUPS, first_axis_on, 0)
    lax.fori_loop(0, GROUPS, second_axis, 0)

    def filter_spectrum(g, carry):
        t_hi, t_lo = split_bf16(taps[pl.ds(g * LANES, LANES), :])
        hs[g] = dot_nt(f_hi[...], t_hi) + (dot_nt(f_hi[...], t_lo) + dot_nt(f_lo[...], t_hi))
        return carry

    og_own.wait()
    taps_own.wait()
    lax.fori_loop(0, GROUPS, filter_spectrum, 0)

    def clear(i, carry):
        acc[pl.ds(i * 64, 64), :] = jnp.zeros((64, acc.shape[1]), F32)
        return carry

    lax.fori_loop(0, acc.shape[0] // 64, clear, 0)
    depth = NX * NH * TAPS
    wait_ring(0, FIRST_HALF)
    start_ring(1, SECOND_HALF)
    wait_ring(0, SECOND_HALF)
    start_ring(0, LAST)
    wait_ring(1, FIRST_HALF)
    start_ring(2, FIRST_HALF)
    wait_ring(1, SECOND_HALF)
    start_ring(2, SECOND_HALF)

    def halo_up(g):
        return remote(gbuf.at[g, BLOCKS - 1], hg.at[g], halo_send.at[g], halo_recv.at[g], after)

    def halo_down(g):
        return remote(mbuf.at[g, 0], hm.at[g], halo_send.at[GROUPS + g], halo_recv.at[GROUPS + g], before)

    def ar_h(g):
        return remote(fgmine.at[g], fgother.at[g], ar_send.at[g], ar_recv.at[g], h_peer)

    def stage_1(g):
        pacc[...] = dot(slab[...].reshape(BLOCKS * TAPS, NZ * depth), wbuf[g].reshape(NZ * depth, 3 * LANES))
        cols = pl.ds(pl.multiple_of(g * LANES, LANES), LANES)
        qkv[g] = pacc[...].astype(BF16)
        q = qkv[g, :, :LANES].astype(F32)
        k = qkv[g, :, LANES : 2 * LANES].astype(F32)
        v = qkv[g, :, 2 * LANES :].astype(F32)
        gbuf[g] = (k * v).astype(BF16).reshape(BLOCKS, TAPS, LANES)
        mbuf[g] = (og[:, cols].astype(F32) * q).astype(BF16).reshape(BLOCKS, TAPS, LANES)
        halo_up(g).start()
        halo_down(g).start()

    def forward(block):
        return dot(f_hi[...], block) + dot(f_lo[...], block)

    def inverse(half, re, im):
        rows = slice(half * TAPS, (half + 1) * TAPS)
        hi, lo = split_bf16(jnp.concatenate([re, im], 0))
        return dot(i_hi[rows, :], hi) + (dot(i_hi[rows, :], lo) + dot(i_lo[rows, :], hi))

    def spectra(g):
        for i in range(BLOCKS):
            vs[i + 1] = forward(gbuf[g, i])
            us[i] = forward(mbuf[g, i])

    def halo_spectra(g):
        halo_up(g).wait_recv()
        halo_down(g).wait_recv()
        zero = jnp.zeros((TAPS, LANES), BF16)
        vs[0] = forward(jnp.where(ctx == 0, zero, hg[g]))
        us[BLOCKS] = forward(jnp.where(ctx == n_ctx - 1, zero, hm[g]))

    def stage_2(g, blocks):
        cols = pl.ds(pl.multiple_of(g * LANES, LANES), LANES)
        sign = 1.0 - 2.0 * (lax.broadcasted_iota(jnp.int32, (TAPS, LANES), 0) % 2).astype(F32)
        hr, hi = hs[g, :TAPS], hs[g, TAPS:]
        gain = skip[:, cols]
        cr, ci, direct = 0.0, 0.0, 0.0
        for i in blocks:
            rows = slice(i * TAPS, (i + 1) * TAPS)
            xr = vs[i, :TAPS] + sign * vs[i + 1, TAPS:]
            xi = vs[i, TAPS:] - sign * vs[i + 1, :TAPS]
            mr = us[i, :TAPS] + sign * us[i + 1, TAPS:]
            mi = us[i, TAPS:] - sign * us[i + 1, :TAPS]
            dr = sign * us[i, TAPS:]
            di = -sign * us[i, :TAPS]
            cr = cr + (dr * xr + di * xi)
            ci = ci + (di * xr - dr * xi)
            gf, mf = gbuf[g, i].astype(F32), mbuf[g, i].astype(F32)
            mixed = inverse(1, hr * xr - hi * xi, hr * xi + hi * xr) + gain * gf
            back = inverse(0, hr * mr + hi * mi, hr * mi - hi * mr) + gain * mf
            direct = direct + jnp.sum(gf * mf, 0, keepdims=True)
            qb = qkv[g, rows, :LANES].astype(F32)
            kb = qkv[g, rows, LANES : 2 * LANES].astype(F32)
            vb = qkv[g, rows, 2 * LANES :].astype(F32)
            filt[rows, cols] = (qb * mixed).astype(BF16)
            pg[g, rows, :LANES] = (og[rows, cols].astype(F32) * mixed).astype(BF16)
            pg[g, rows, LANES : 2 * LANES] = (back * vb).astype(BF16)
            pg[g, rows, 2 * LANES :] = (back * kb).astype(BF16)
        return cr, ci, direct

    def keep(sums):
        cross[:TAPS], cross[TAPS:] = sums[0], sums[1]
        straight[...] = sums[2]

    def filter_part(g, sums):
        cr, ci, direct = cross[:TAPS] + sums[0], cross[TAPS:] + sums[1], straight[...] + sums[2]
        part = inverse(0, cr, ci)
        first = lax.broadcasted_iota(jnp.int32, (TAPS, LANES), 0) == 0
        fgmine[g] = jnp.where(first, direct, part).astype(BF16)
        ar_h(g).start()

    wide = NH * TAPS
    chunk = tgrad.shape[1] // CHUNKS

    def add_terms(groups, c, row_slices):
        at_cols = pl.ds(pl.multiple_of(c * chunk, chunk), chunk)
        count = chunk // wide
        zz, xx = c * count // NX, c * count % NX
        total = 0.0
        for g in groups:
            left = jnp.concatenate([pg[g, r, :] for r in row_slices], 0)
            total = total + dot_nt(left, wbuf[g, zz, pl.ds(xx, count)].reshape(chunk, 3 * LANES))
        done = 0
        for r in row_slices:
            acc[r, at_cols] += total[done : done + r.stop - r.start]
            done += r.stop - r.start

    def group(g, carry):
        wait_ring(g, LAST)

        @pl.when(g == 0)
        def _():
            start_ring(1, LAST)
            token_landed(1).wait_recv()
            token_copy(2).start()
            tokens_own.wait()
            token_landed(0).wait_recv()
            token_landed(2).wait_recv()

        @pl.when(g == 1)
        def _():
            start_ring(3, SECOND_HALF)

        stage_1(g)

        @pl.when(g == 0)
        def _():
            wait_ring(2, FIRST_HALF)
            start_ring(3, FIRST_HALF)
            wait_ring(2, SECOND_HALF)
            start_ring(2, LAST)

        @pl.when(g == 2)
        def _():
            wait_ring(3, FIRST_HALF)
            wait_ring(3, SECOND_HALF)
            start_ring(3, LAST)

        def finish_group(done, carry):
            spectra(done)
            halo_spectra(done)
            keep(stage_2(done, INNER))
            filter_part(done, stage_2(done, OUTER))

            @pl.when(done < 1)
            def _():
                def step(c, carry):
                    add_terms([done], c, [slice(0, BLOCKS * TAPS)])
                    return carry

                lax.fori_loop(0, CHUNKS, step, 0)

            @pl.when(done == 1)
            def _():
                for side in (0, 1):
                    add_terms([done], side * (CHUNKS // 2), [slice(TAPS, 3 * TAPS)])

            return carry

        begin = jnp.where(g == GROUPS - 1, g, jnp.maximum(g - 1, 0))
        end = jnp.where(g == GROUPS - 2, g + 1, g)
        lax.fori_loop(begin, end, finish_group, 0)
        return carry

    lax.fori_loop(0, GROUPS, group, 0)

    half_chunks = CHUNKS // 2

    def rows_of(t):
        return pl.ds(pl.multiple_of(t * TAPS, TAPS), TAPS)

    def cols_of(c):
        return pl.ds(pl.multiple_of(c * chunk, chunk), chunk)

    def to_core(kind, j):
        n = kind * half_chunks + j
        return remote(ps1.at[n], pr1.at[n], rs_send.at[n], rs_recv.at[n], sibling)

    def to_chip(kind, j):
        n = kind * half_chunks + j
        c = b * half_chunks + j
        peer = {"ctx": ctx, "tp": (2 - a, 3 - 3 * a)[kind]}
        return remote(ps2.at[n], pr2.at[c], rs_send.at[CHUNKS + n], rs_recv.at[CHUNKS + c], peer)

    def to_owner(c):
        return remote(ps3.at[c], pr3.at[c], rs_send.at[2 * CHUNKS + c], rs_recv.at[2 * CHUNKS + c], sibling)

    def scatter(kind, beside):
        row_slices = ([slice(TAPS, 3 * TAPS)], [slice(0, TAPS), slice(3 * TAPS, 4 * TAPS)])[kind]
        far, near = rows_of((2 - a, 3 - 3 * a)[kind]), (1 + a, 3 * a)[kind]

        def step(i, carry):
            side = (b + 1 + i) % 2

            @pl.when(i < CHUNKS)
            def _():
                c = side * half_chunks + i // 2
                head = (i < 2) if kind == 0 else False

                @pl.when(jnp.logical_not(head))
                def _():
                    add_terms(range(1, GROUPS), c, row_slices)

                @pl.when(head)
                def _():
                    add_terms(range(2, GROUPS), c, row_slices)

                @pl.when(i % 2 == 0)
                def _():
                    ps1[kind * half_chunks + i // 2] = acc[far, cols_of(c)].astype(BF16)
                    to_core(kind, i // 2).start()

                @pl.when(tp != near)
                def _():
                    ps3[c] = acc[rows_of(near), cols_of(c)].astype(BF16)
                    to_owner(c).start()

            pl.when(i == CHUNKS // 2 + 1)(beside)

            @pl.when((i > 0) & (i % 2 == 0))
            def _():
                j = i // 2 - 1
                to_core(kind, j).wait_recv()
                n = kind * half_chunks + j
                mine = acc[far, cols_of(b * half_chunks + j)]
                ps2[n] = (mine + pr1[n].astype(F32)).astype(BF16)
                to_chip(kind, j).start()

            return carry

        lax.fori_loop(0, CHUNKS + 1, step, 0)

    others = NZ * NX - 1

    def rows_8(m, sense):
        return pl.ds(pl.multiple_of(32 * turn(z, sense * (m // NX)) + 8 * turn(x, sense * (m % NX)), 8), 8)

    def ar(kind, m, src, dst):
        n = GROUPS + kind * others + m - 1
        return remote(src, dst, ar_send.at[n], ar_recv.at[n], at(turn(z, m // NX), turn(x, m % NX), h))

    def each(act):
        def step(m, carry):
            act(m)
            return carry

        lax.fori_loop(1, others + 1, step, 0)

    last = GROUPS - 1
    early, late = pl.ds(0, last * LANES), pl.ds(last * LANES, LANES)

    def plane(kind, m):
        cols = (early, late)[kind]
        return ar(kind, m, fgbuf.at[rows_8(m, 1), cols], zrecv.at[m - 1, :, cols])

    def back(m):
        mine = fgrad.at[rows_8(0, 1), :]
        return ar(2, m, mine, mine)

    def back_landed(m):
        got = fgrad.at[rows_8(m, -1), :]
        return ar(2, m, got, got)

    def sum_h(g):
        ar_h(g).wait_recv()
        fgbuf[:, g * LANES : (g + 1) * LANES] = fgmine[g].astype(F32) + fgother[g].astype(F32)

    spectra(last)
    keep(stage_2(last, INNER))

    def early_groups():
        for g in range(last):
            sum_h(g)
        each(lambda m: plane(0, m).start())

    def last_group():
        sum_h(last)
        each(lambda m: plane(1, m).start())

    scatter(0, early_groups)
    halo_spectra(last)
    filter_part(last, stage_2(last, OUTER))
    scatter(1, last_group)

    def arrived(m):
        plane(0, m).wait_recv()
        plane(1, m).wait_recv()

    each(arrived)
    total = fgbuf[rows_8(0, 1), :]
    for m in range(others):
        total = total + zrecv[m]
    fgrad[rows_8(0, 1), :] = total * (BLOCKS * TAPS * n_ctx) ** (-0.5)
    each(lambda m: back(m).start())

    def finish(c, carry):
        to_owner(c).wait_recv()
        remote(pr2.at[c], pr2.at[c], rs_send.at[CHUNKS + c], rs_recv.at[CHUNKS + c], across).wait_recv()
        total = acc[rows_of(tp), cols_of(c)] + pr3[c].astype(F32) + pr2[c].astype(F32)
        tgrad[:, cols_of(c)] = total.astype(BF16)
        return carry

    lax.fori_loop(0, CHUNKS, finish, 0)
    each(lambda m: back_landed(m).wait_recv())

    def drain(g, carry):
        p0(g).wait_send()
        halo_up(g).wait_send()
        halo_down(g).wait_send()
        ar_h(g).wait_send()
        for phase in range(PHASES):
            for half in (0, 1):
                for way in (0, 1):
                    ring(g, phase, half, way, 0).wait_send()
        return carry

    def drain_scatter(j, carry):
        for kind in (0, 1):
            to_core(kind, j).wait_send()
            to_chip(kind, j).wait_send()
            to_owner(kind * half_chunks + j).wait_send()
        return carry

    lax.fori_loop(0, GROUPS, drain, 0)
    lax.fori_loop(0, half_chunks, drain_scatter, 0)
    for which in range(3):
        token_copy(which).wait_send()

    def drain_plane(m):
        plane(0, m).wait_send()
        plane(1, m).wait_send()
        back(m).wait_send()

    each(drain_plane)


def hand_out(filt, tgrad, total, filt_out, tgrad_out, fgrad_out, skip_out):
    filt_out[...] = filt[...]
    tgrad_out[...] = tgrad[...]
    fgrad_out[...] = total[...].T
    skip_out[...] = total[:1, :]


def shards(tokens, proj_weight, filter_taps, skip_gain, out_grad):
    rows, width = out_grad.shape
    depth = tokens.shape[1]
    forward, inverse = transforms()
    f_hi, f_lo = split_bf16(jnp.asarray(forward))
    i_hi, i_lo = split_bf16(jnp.asarray(inverse))
    w_in = proj_weight.transpose(1, 0, 2).reshape(3, 2, 64, width)
    vmem = pl.BlockSpec(memory_space=pltpu.VMEM)
    hbm = pl.BlockSpec(memory_space=pl.ANY)
    sem = pltpu.SemaphoreType.DMA
    V = pltpu.VMEM
    filtered, tokens_grad, filter_total = pl.pallas_call(
        kernel,
        out_shape=(
            jax.ShapeDtypeStruct((rows, width), BF16),
            jax.ShapeDtypeStruct((TAPS, depth), BF16),
            jax.ShapeDtypeStruct((TAPS, width), F32),
        ),
        in_specs=[hbm, hbm, hbm, vmem, hbm] + [vmem] * 4,
        out_specs=(vmem, vmem, vmem),
        scratch_shapes=[
            V((width, TAPS), F32),
            V((rows, width), BF16),
            V((GROUPS, NZ, NX, NH, 2, 64, 3 * LANES), BF16),
            V((BLOCKS, TAPS, depth), BF16),
            V((rows, depth), F32),
            V((rows, 3 * LANES), F32),
            V((GROUPS, rows, 3 * LANES), BF16),
            V((GROUPS, rows, 3 * LANES), BF16),
            V((GROUPS, BLOCKS, TAPS, LANES), BF16),
            V((GROUPS, BLOCKS, TAPS, LANES), BF16),
            V((GROUPS, TAPS, LANES), BF16),
            V((GROUPS, TAPS, LANES), BF16),
            V((BLOCKS + 1, 2 * TAPS, LANES), F32),
            V((BLOCKS + 1, 2 * TAPS, LANES), F32),
            V((GROUPS, 2 * TAPS, LANES), F32),
            V((2 * TAPS, LANES), F32),
            V((1, LANES), F32),
            V((GROUPS, TAPS, LANES), BF16),
            V((GROUPS, TAPS, LANES), BF16),
            V((TAPS, width), F32),
            V((NZ * NX - 1, 8, width), F32),
        ]
        + [V((CHUNKS, TAPS, depth // CHUNKS), BF16)] * 6
        + [
            sem((GROUPS + 3,)),
            sem((GROUPS,)),
            sem((GROUPS,)),
            sem((GROUPS * 4 * PHASES,)),
            sem((GROUPS * 4 * PHASES,)),
            sem((3,)),
            sem((3,)),
            sem((2 * GROUPS,)),
            sem((2 * GROUPS,)),
            sem((3 * CHUNKS,)),
            sem((3 * CHUNKS,)),
            sem((GROUPS + 3 * (NZ * NX - 1),)),
            sem((GROUPS + 3 * (NZ * NX - 1),)),
        ],
        compiler_params=pltpu.CompilerParams(
            collective_id=0, has_side_effects=True, vmem_limit_bytes=58 * 2**20
        ),
    )(tokens, w_in, filter_taps, skip_gain[None, :], out_grad, f_hi, f_lo, i_hi, i_lo)
    filtered, tokens_grad, filter_grad, skip_grad = pl.pallas_call(
        hand_out,
        out_shape=(
            jax.ShapeDtypeStruct((rows, width), BF16),
            jax.ShapeDtypeStruct((TAPS, depth), BF16),
            jax.ShapeDtypeStruct((width, TAPS), F32),
            jax.ShapeDtypeStruct((1, width), F32),
        ),
        in_specs=[vmem] * 3,
        out_specs=(vmem,) * 4,
    )(filtered, tokens_grad, filter_total)
    return filtered, tokens_grad, filter_grad, skip_grad[0]


def solution(mesh):
    placed = (P(("ctx", "tp"), None), P("ctx", None, "tp"), P("tp", None), P("tp"), P("ctx", "tp"))
    return jax.shard_map(
        shards,
        mesh=mesh,
        in_specs=placed,
        out_specs=(P("ctx", "tp"), P(("ctx", "tp"), None), P("tp", None), P("tp")),
        check_vma=False,
    )
```

```python
import functools

import numpy as np
import jax
import jax.numpy as jnp
from jax import lax
from jax.experimental import pallas as pl
from jax.experimental.pallas import tpu as pltpu
from jax.sharding import PartitionSpec as P

MESH = pl.DeviceIdType.MESH
F32 = jnp.float32
BF16 = jnp.bfloat16
TAPS = 128
LANES = 128
BLOCKS = 4
GROUPS = 4
NZ, NX, NH = 4, 4, 2
NEAR, PAIR, ON, FIRST_HALF, SECOND_HALF, LAST = range(6)
PHASES = 6
INNER, OUTER = (1, 2), (0, 3)
CHUNKS = 8


def transforms():
    k = np.arange(TAPS)[:, None]
    n = np.arange(2 * TAPS)[None, :]
    angle = np.pi * (2 * k + 1) * n / (2 * TAPS)
    both = np.concatenate([np.cos(angle), -np.sin(angle)], 0)
    return both[:, :TAPS].astype(np.float32), (both.T / TAPS).astype(np.float32)


def split_bf16(m):
    hi = m.astype(BF16)
    return hi, (m - hi.astype(F32)).astype(BF16)


def dot(a, b):
    return jnp.dot(a, b, preferred_element_type=F32)


def dot_nt(a, b):
    return lax.dot_general(a, b, (((1,), (1,)), ((), ())), preferred_element_type=F32)


def kernel(
    tokens, w_in, taps_in, skip, og_in, f_hi, f_lo, i_hi, i_lo,
    filt_out, tgrad_out, fgrad,
    filt, tgrad, taps, og, wbuf, slab, acc, pacc, qkv, pg, gbuf, mbuf, hg, hm, vs, us, hs,
    cross, straight, fgmine, fgother, fgbuf, zrecv,
    ps1, pr1, ps2, pr2, ps3, pr3,
    loc_sem, p0_send, p0_recv, ring_send, ring_recv, tok_send, tok_recv, halo_send, halo_recv,
    rs_send, rs_recv, ar_send, ar_recv,
):
    ctx = lax.axis_index("ctx")
    tp = lax.axis_index("tp")
    n_ctx = NZ * NX * NH
    z, x, h = ctx // (NX * NH), (ctx // NH) % NX, ctx % NH
    a, b = tp // 2, tp % 2

    def at(zz, xx, hh):
        return {"ctx": (zz * NX + xx) * NH + hh, "tp": tp}

    def turn(v, by):
        return (v + by + 4) % 4

    sibling = {"ctx": ctx, "tp": 2 * a + 1 - b}
    across = {"ctx": ctx, "tp": 2 * (1 - a) + b}
    far_sibling = {"ctx": ctx, "tp": 2 * (1 - a) + 1 - b}
    after = {"ctx": (ctx + 1) % n_ctx, "tp": tp}
    before = {"ctx": (ctx + n_ctx - 1) % n_ctx, "tp": tp}
    h_peer = at(z, x, 1 - h)
    z_peer = [None] + [at(turn(z, d), x, h) for d in (1, 2, 3)]
    x_peer = [None] + [at(z, turn(x, d), h) for d in (1, 2, 3)]

    barrier = pltpu.get_barrier_semaphore()
    greeted = [sibling, across, far_sibling, after, before, h_peer]
    greeted = greeted + [at(turn(z, m // NX), turn(x, m % NX), h) for m in range(1, NZ * NX)]
    for peer in greeted:
        pl.semaphore_signal(barrier, inc=1, device_id=peer, device_id_type=MESH)

    def remote(src, dst, send, recv, peer):
        return pltpu.make_async_remote_copy(
            src_ref=src, dst_ref=dst, send_sem=send, recv_sem=recv, device_id=peer, device_id_type=MESH
        )

    def p0(g):
        block = wbuf.at[g, z, x, h]
        return remote(block, block, p0_send.at[g], p0_recv.at[g], h_peer)

    def start_own(g):
        for i in range(3):
            pltpu.make_async_copy(
                w_in.at[i, :, :, pl.ds(g * LANES, LANES)],
                wbuf.at[g, z, x, h, :, :, pl.ds(i * LANES, LANES)],
                loc_sem.at[g],
            ).start()

    def wait_own(g):
        block = wbuf.at[g, z, x, h]
        pltpu.make_async_copy(block, block, loc_sem.at[g]).wait()

    def ring(g, phase, half, way, sender):
        step = -1 if way == 0 else 1
        along_x = (half == 0) == (phase < FIRST_HALF)
        zz, xx = z, x
        if along_x:
            xx = turn(x, sender)
            if phase in (ON, LAST):
                xx = turn(xx, step)
        else:
            zz = turn(z, sender)
            if phase in (ON, LAST):
                zz = turn(zz, step)
        part = wbuf.at[g]
        hh = {NEAR: h, PAIR: 1 - h, ON: way, FIRST_HALF: 0, SECOND_HALF: 1, LAST: way}[phase]
        if phase in (NEAR, PAIR, ON):
            ref = part.at[zz, xx, hh, half]
        else:
            ref = part.at[:, xx, hh, half] if along_x else part.at[zz, :, hh, half]
        peer = (x_peer if along_x else z_peer)[1 if way == 0 else 3]
        slot = ((g * PHASES + phase) * 2 + half) * 2 + way
        return remote(ref, ref, ring_send.at[slot], ring_recv.at[slot], peer)

    def start_ring(g, phase):
        for half in (0, 1):
            for way in (0, 1):
                ring(g, phase, half, way, 0).start()

    def wait_ring(g, phase):
        for half in (0, 1):
            for way in (0, 1):
                ring(g, phase, half, way, -1 if way == 0 else 1).wait_recv()

    def token_copy(which):
        mine = slab.at[tp]
        far = slab.at[2 * (1 - a) + b]
        if which == 0:
            return remote(tokens, mine, tok_send.at[0], tok_recv.at[0], sibling)
        if which == 1:
            return remote(tokens, mine, tok_send.at[1], tok_recv.at[1], across)
        return remote(far, far, tok_send.at[2], tok_recv.at[2], sibling)

    def token_landed(which):
        ref = slab.at[(2 * a + 1 - b, 2 * (1 - a) + b, 2 * (1 - a) + 1 - b)[which]]
        return remote(ref, ref, tok_send.at[which], tok_recv.at[which], sibling)

    for g in range(GROUPS):
        start_own(g)
    tokens_own = pltpu.make_async_copy(tokens, slab.at[tp], loc_sem.at[GROUPS])
    tokens_own.start()
    og_own = pltpu.make_async_copy(og_in, og, loc_sem.at[GROUPS + 1])
    taps_own = pltpu.make_async_copy(taps_in, taps, loc_sem.at[GROUPS + 2])
    og_own.start()
    taps_own.start()
    pl.semaphore_wait(barrier, len(greeted))
    for g in range(GROUPS):
        wait_own(g)
        p0(g).start()
        start_ring(g, NEAR)
    token_copy(1).start()
    token_copy(0).start()

    def land_p0(g):
        block = wbuf.at[g, z, x, 1 - h]
        remote(block, block, p0_send.at[g], p0_recv.at[g], h_peer).wait_recv()

    def first_axis(g, carry):
        land_p0(g)
        start_ring(g, PAIR)
        return carry

    def first_axis_on(g, carry):
        wait_ring(g, NEAR)
        wait_ring(g, PAIR)
        start_ring(g, ON)
        return carry

    def second_axis(g, carry):
        wait_ring(g, ON)
        begin = ((0, FIRST_HALF), (0, SECOND_HALF), (1, FIRST_HALF))
        for i, piece in enumerate(begin):

            @pl.when(g == i)
            def _():
                start_ring(*piece)

        return carry

    lax.fori_loop(0, GROUPS, first_axis, 0)
    lax.fori_loop(0, GROUPS, first_axis_on, 0)
    lax.fori_loop(0, GROUPS, second_axis, 0)

    def filter_spectrum(g, carry):
        t_hi, t_lo = split_bf16(taps[pl.ds(g * LANES, LANES), :])
        hs[g] = dot_nt(f_hi[...], t_hi) + (dot_nt(f_hi[...], t_lo) + dot_nt(f_lo[...], t_hi))
        return carry

    og_own.wait()
    taps_own.wait()
    lax.fori_loop(0, GROUPS, filter_spectrum, 0)

    def clear(i, carry):
        acc[pl.ds(i * 64, 64), :] = jnp.zeros((64, acc.shape[1]), F32)
        return carry

    lax.fori_loop(0, acc.shape[0] // 64, clear, 0)
    depth = NX * NH * TAPS
    wait_ring(0, FIRST_HALF)
    start_ring(1, SECOND_HALF)
    wait_ring(0, SECOND_HALF)
    start_ring(0, LAST)
    wait_ring(1, FIRST_HALF)
    start_ring(2, FIRST_HALF)
    wait_ring(1, SECOND_HALF)
    start_ring(2, SECOND_HALF)

    def halo_up(g):
        return remote(gbuf.at[g, BLOCKS - 1], hg.at[g], halo_send.at[g], halo_recv.at[g], after)

    def halo_down(g):
        return remote(mbuf.at[g, 0], hm.at[g], halo_send.at[GROUPS + g], halo_recv.at[GROUPS + g], before)

    def ar_h(g):
        return remote(fgmine.at[g], fgother.at[g], ar_send.at[g], ar_recv.at[g], h_peer)

    def stage_1(g):
        pacc[...] = dot(slab[...].reshape(BLOCKS * TAPS, NZ * depth), wbuf[g].reshape(NZ * depth, 3 * LANES))
        cols = pl.ds(pl.multiple_of(g * LANES, LANES), LANES)
        qkv[g] = pacc[...].astype(BF16)
        q = qkv[g, :, :LANES].astype(F32)
        k = qkv[g, :, LANES : 2 * LANES].astype(F32)
        v = qkv[g, :, 2 * LANES :].astype(F32)
        gbuf[g] = (k * v).astype(BF16).reshape(BLOCKS, TAPS, LANES)
        mbuf[g] = (og[:, cols].astype(F32) * q).astype(BF16).reshape(BLOCKS, TAPS, LANES)
        halo_up(g).start()
        halo_down(g).start()

    def forward(block):
        return dot(f_hi[...], block) + dot(f_lo[...], block)

    def inverse(half, re, im):
        rows = slice(half * TAPS, (half + 1) * TAPS)
        hi, lo = split_bf16(jnp.concatenate([re, im], 0))
        return dot(i_hi[rows, :], hi) + (dot(i_hi[rows, :], lo) + dot(i_lo[rows, :], hi))

    def spectra(g):
        for i in range(BLOCKS):
            vs[i + 1] = forward(gbuf[g, i])
            us[i] = forward(mbuf[g, i])

    def halo_spectra(g):
        halo_up(g).wait_recv()
        halo_down(g).wait_recv()
        zero = jnp.zeros((TAPS, LANES), BF16)
        vs[0] = forward(jnp.where(ctx == 0, zero, hg[g]))
        us[BLOCKS] = forward(jnp.where(ctx == n_ctx - 1, zero, hm[g]))

    def stage_2(g, blocks):
        cols = pl.ds(pl.multiple_of(g * LANES, LANES), LANES)
        sign = 1.0 - 2.0 * (lax.broadcasted_iota(jnp.int32, (TAPS, LANES), 0) % 2).astype(F32)
        hr, hi = hs[g, :TAPS], hs[g, TAPS:]
        gain = skip[:, cols]
        cr, ci, direct = 0.0, 0.0, 0.0
        for i in blocks:
            rows = slice(i * TAPS, (i + 1) * TAPS)
            xr = vs[i, :TAPS] + sign * vs[i + 1, TAPS:]
            xi = vs[i, TAPS:] - sign * vs[i + 1, :TAPS]
            mr = us[i, :TAPS] + sign * us[i + 1, TAPS:]
            mi = us[i, TAPS:] - sign * us[i + 1, :TAPS]
            dr = sign * us[i, TAPS:]
            di = -sign * us[i, :TAPS]
            cr = cr + (dr * xr + di * xi)
            ci = ci + (di * xr - dr * xi)
            gf, mf = gbuf[g, i].astype(F32), mbuf[g, i].astype(F32)
            mixed = inverse(1, hr * xr - hi * xi, hr * xi + hi * xr) + gain * gf
            back = inverse(0, hr * mr + hi * mi, hr * mi - hi * mr) + gain * mf
            direct = direct + jnp.sum(gf * mf, 0, keepdims=True)
            qb = qkv[g, rows, :LANES].astype(F32)
            kb = qkv[g, rows, LANES : 2 * LANES].astype(F32)
            vb = qkv[g, rows, 2 * LANES :].astype(F32)
            filt[rows, cols] = (qb * mixed).astype(BF16)
            pg[g, rows, :LANES] = (og[rows, cols].astype(F32) * mixed).astype(BF16)
            pg[g, rows, LANES : 2 * LANES] = (back * vb).astype(BF16)
            pg[g, rows, 2 * LANES :] = (back * kb).astype(BF16)
        return cr, ci, direct

    def keep(sums):
        cross[:TAPS], cross[TAPS:] = sums[0], sums[1]
        straight[...] = sums[2]

    def filter_part(g, sums):
        cr, ci, direct = cross[:TAPS] + sums[0], cross[TAPS:] + sums[1], straight[...] + sums[2]
        part = inverse(0, cr, ci)
        first = lax.broadcasted_iota(jnp.int32, (TAPS, LANES), 0) == 0
        fgmine[g] = jnp.where(first, direct, part).astype(BF16)
        ar_h(g).start()

    wide = NH * TAPS
    chunk = tgrad.shape[1] // CHUNKS

    def add_terms(groups, c, row_slices):
        at_cols = pl.ds(pl.multiple_of(c * chunk, chunk), chunk)
        count = chunk // wide
        zz, xx = c * count // NX, c * count % NX
        total = 0.0
        for g in groups:
            left = jnp.concatenate([pg[g, r, :] for r in row_slices], 0)
            total = total + dot_nt(left, wbuf[g, zz, pl.ds(xx, count)].reshape(chunk, 3 * LANES))
        done = 0
        for r in row_slices:
            acc[r, at_cols] += total[done : done + r.stop - r.start]
            done += r.stop - r.start

    def group(g, carry):
        wait_ring(g, LAST)

        @pl.when(g == 0)
        def _():
            start_ring(1, LAST)
            token_landed(1).wait_recv()
            token_copy(2).start()
            tokens_own.wait()
            token_landed(0).wait_recv()
            token_landed(2).wait_recv()

        @pl.when(g == 1)
        def _():
            start_ring(3, SECOND_HALF)

        stage_1(g)

        @pl.when(g == 0)
        def _():
            wait_ring(2, FIRST_HALF)
            start_ring(3, FIRST_HALF)
            wait_ring(2, SECOND_HALF)
            start_ring(2, LAST)

        @pl.when(g == 2)
        def _():
            wait_ring(3, FIRST_HALF)
            wait_ring(3, SECOND_HALF)
            start_ring(3, LAST)

        def finish_group(done, carry):
            spectra(done)
            halo_spectra(done)
            keep(stage_2(done, INNER))
            filter_part(done, stage_2(done, OUTER))

            @pl.when(done < 1)
            def _():
                def step(c, carry):
                    add_terms([done], c, [slice(0, BLOCKS * TAPS)])
                    return carry

                lax.fori_loop(0, CHUNKS, step, 0)

            @pl.when(done == 1)
            def _():
                for side in (0, 1):
                    add_terms([done], side * (CHUNKS // 2), [slice(TAPS, 3 * TAPS)])

            return carry

        begin = jnp.where(g == GROUPS - 1, g, jnp.maximum(g - 1, 0))
        end = jnp.where(g == GROUPS - 2, g + 1, g)
        lax.fori_loop(begin, end, finish_group, 0)
        return carry

    lax.fori_loop(0, GROUPS, group, 0)

    half_chunks = CHUNKS // 2

    def rows_of(t):
        return pl.ds(pl.multiple_of(t * TAPS, TAPS), TAPS)

    def cols_of(c):
        return pl.ds(pl.multiple_of(c * chunk, chunk), chunk)

    def to_core(kind, j):
        n = kind * half_chunks + j
        return remote(ps1.at[n], pr1.at[n], rs_send.at[n], rs_recv.at[n], sibling)

    def to_chip(kind, j):
        n = kind * half_chunks + j
        c = b * half_chunks + j
        peer = {"ctx": ctx, "tp": (2 - a, 3 - 3 * a)[kind]}
        return remote(ps2.at[n], pr2.at[c], rs_send.at[CHUNKS + n], rs_recv.at[CHUNKS + c], peer)

    def to_owner(c):
        return remote(ps3.at[c], pr3.at[c], rs_send.at[2 * CHUNKS + c], rs_recv.at[2 * CHUNKS + c], sibling)

    def scatter(kind, beside):
        row_slices = ([slice(TAPS, 3 * TAPS)], [slice(0, TAPS), slice(3 * TAPS, 4 * TAPS)])[kind]
        far, near = rows_of((2 - a, 3 - 3 * a)[kind]), (1 + a, 3 * a)[kind]

        def step(i, carry):
            side = (b + 1 + i) % 2

            @pl.when(i < CHUNKS)
            def _():
                c = side * half_chunks + i // 2
                head = (i < 2) if kind == 0 else False

                @pl.when(jnp.logical_not(head))
                def _():
                    add_terms(range(1, GROUPS), c, row_slices)

                @pl.when(head)
                def _():
                    add_terms(range(2, GROUPS), c, row_slices)

                @pl.when(i % 2 == 0)
                def _():
                    ps1[kind * half_chunks + i // 2] = acc[far, cols_of(c)].astype(BF16)
                    to_core(kind, i // 2).start()

                @pl.when(tp != near)
                def _():
                    ps3[c] = acc[rows_of(near), cols_of(c)].astype(BF16)
                    to_owner(c).start()

            pl.when(i == CHUNKS // 2 + 1)(beside)

            @pl.when((i > 0) & (i % 2 == 0))
            def _():
                j = i // 2 - 1
                to_core(kind, j).wait_recv()
                n = kind * half_chunks + j
                mine = acc[far, cols_of(b * half_chunks + j)]
                ps2[n] = (mine + pr1[n].astype(F32)).astype(BF16)
                to_chip(kind, j).start()

            return carry

        lax.fori_loop(0, CHUNKS + 1, step, 0)

    others = NZ * NX - 1

    def rows_8(m, sense):
        return pl.ds(pl.multiple_of(32 * turn(z, sense * (m // NX)) + 8 * turn(x, sense * (m % NX)), 8), 8)

    def ar(kind, m, src, dst):
        n = GROUPS + kind * others + m - 1
        return remote(src, dst, ar_send.at[n], ar_recv.at[n], at(turn(z, m // NX), turn(x, m % NX), h))

    def each(act):
        def step(m, carry):
            act(m)
            return carry

        lax.fori_loop(1, others + 1, step, 0)

    last = GROUPS - 1
    early, late = pl.ds(0, last * LANES), pl.ds(last * LANES, LANES)

    def plane(kind, m):
        cols = (early, late)[kind]
        return ar(kind, m, fgbuf.at[rows_8(m, 1), cols], zrecv.at[m - 1, :, cols])

    def back(m):
        mine = fgrad.at[rows_8(0, 1), :]
        return ar(2, m, mine, mine)

    def back_landed(m):
        got = fgrad.at[rows_8(m, -1), :]
        return ar(2, m, got, got)

    def sum_h(g):
        ar_h(g).wait_recv()
        fgbuf[:, g * LANES : (g + 1) * LANES] = fgmine[g].astype(F32) + fgother[g].astype(F32)

    spectra(last)
    keep(stage_2(last, INNER))

    def early_groups():
        for g in range(last):
            sum_h(g)
        each(lambda m: plane(0, m).start())

    def last_group():
        sum_h(last)
        each(lambda m: plane(1, m).start())

    scatter(0, early_groups)
    halo_spectra(last)
    filter_part(last, stage_2(last, OUTER))
    filt_copy = pltpu.make_async_copy(filt, filt_out, loc_sem.at[GROUPS + 3])
    filt_copy.start()
    scatter(1, last_group)

    def arrived(m):
        plane(0, m).wait_recv()
        plane(1, m).wait_recv()

    each(arrived)
    total = fgbuf[rows_8(0, 1), :]
    for m in range(others):
        total = total + zrecv[m]
    fgrad[rows_8(0, 1), :] = total * (BLOCKS * TAPS * n_ctx) ** (-0.5)
    each(lambda m: back(m).start())

    def finish(c, carry):
        to_owner(c).wait_recv()
        remote(pr2.at[c], pr2.at[c], rs_send.at[CHUNKS + c], rs_recv.at[CHUNKS + c], across).wait_recv()
        total = acc[rows_of(tp), cols_of(c)] + pr3[c].astype(F32) + pr2[c].astype(F32)
        tgrad[:, cols_of(c)] = total.astype(BF16)
        ready = tgrad.at[:, cols_of(c)], tgrad_out.at[:, cols_of(c)]
        pltpu.make_async_copy(*ready, loc_sem.at[GROUPS + 4]).start()
        return carry

    lax.fori_loop(0, CHUNKS, finish, 0)
    each(lambda m: back_landed(m).wait_recv())

    def drain(g, carry):
        p0(g).wait_send()
        halo_up(g).wait_send()
        halo_down(g).wait_send()
        ar_h(g).wait_send()
        for phase in range(PHASES):
            for half in (0, 1):
                for way in (0, 1):
                    ring(g, phase, half, way, 0).wait_send()
        return carry

    def drain_scatter(j, carry):
        for kind in (0, 1):
            to_core(kind, j).wait_send()
            to_chip(kind, j).wait_send()
            to_owner(kind * half_chunks + j).wait_send()
        return carry

    lax.fori_loop(0, GROUPS, drain, 0)
    lax.fori_loop(0, half_chunks, drain_scatter, 0)
    for which in range(3):
        token_copy(which).wait_send()

    def drain_plane(m):
        plane(0, m).wait_send()
        plane(1, m).wait_send()
        back(m).wait_send()

    each(drain_plane)
    filt_copy.wait()
    pltpu.make_async_copy(tgrad, tgrad_out, loc_sem.at[GROUPS + 4]).wait()


def hand_out(filt, tgrad, total, filt_out, tgrad_out, fgrad_out, skip_out):
    filt_out[...] = filt[...]
    tgrad_out[...] = tgrad[...]
    fgrad_out[...] = total[...].T
    skip_out[...] = total[:1, :]


def shards(tokens, proj_weight, filter_taps, skip_gain, out_grad):
    rows, width = out_grad.shape
    depth = tokens.shape[1]
    forward, inverse = transforms()
    f_hi, f_lo = split_bf16(jnp.asarray(forward))
    i_hi, i_lo = split_bf16(jnp.asarray(inverse))
    w_in = proj_weight.transpose(1, 0, 2).reshape(3, 2, 64, width)
    vmem = pl.BlockSpec(memory_space=pltpu.VMEM)
    hbm = pl.BlockSpec(memory_space=pl.ANY)
    sem = pltpu.SemaphoreType.DMA
    V = pltpu.VMEM
    filtered, tokens_grad, filter_total = pl.pallas_call(
        kernel,
        out_shape=(
            jax.ShapeDtypeStruct((rows, width), BF16),
            jax.ShapeDtypeStruct((TAPS, depth), BF16),
            jax.ShapeDtypeStruct((TAPS, width), F32),
        ),
        in_specs=[hbm, hbm, hbm, vmem, hbm] + [vmem] * 4,
        out_specs=(hbm, hbm, vmem),
        scratch_shapes=[
            V((rows, width), BF16),
            V((TAPS, depth), BF16),
            V((width, TAPS), F32),
            V((rows, width), BF16),
            V((GROUPS, NZ, NX, NH, 2, 64, 3 * LANES), BF16),
            V((BLOCKS, TAPS, depth), BF16),
            V((rows, depth), F32),
            V((rows, 3 * LANES), F32),
            V((GROUPS, rows, 3 * LANES), BF16),
            V((GROUPS, rows, 3 * LANES), BF16),
            V((GROUPS, BLOCKS, TAPS, LANES), BF16),
            V((GROUPS, BLOCKS, TAPS, LANES), BF16),
            V((GROUPS, TAPS, LANES), BF16),
            V((GROUPS, TAPS, LANES), BF16),
            V((BLOCKS + 1, 2 * TAPS, LANES), F32),
            V((BLOCKS + 1, 2 * TAPS, LANES), F32),
            V((GROUPS, 2 * TAPS, LANES), F32),
            V((2 * TAPS, LANES), F32),
            V((1, LANES), F32),
            V((GROUPS, TAPS, LANES), BF16),
            V((GROUPS, TAPS, LANES), BF16),
            V((TAPS, width), F32),
            V((NZ * NX - 1, 8, width), F32),
        ]
        + [V((CHUNKS, TAPS, depth // CHUNKS), BF16)] * 6
        + [
            sem((GROUPS + 5,)),
            sem((GROUPS,)),
            sem((GROUPS,)),
            sem((GROUPS * 4 * PHASES,)),
            sem((GROUPS * 4 * PHASES,)),
            sem((3,)),
            sem((3,)),
            sem((2 * GROUPS,)),
            sem((2 * GROUPS,)),
            sem((3 * CHUNKS,)),
            sem((3 * CHUNKS,)),
            sem((GROUPS + 3 * (NZ * NX - 1),)),
            sem((GROUPS + 3 * (NZ * NX - 1),)),
        ],
        compiler_params=pltpu.CompilerParams(
            collective_id=0, has_side_effects=True, vmem_limit_bytes=58 * 2**20
        ),
    )(tokens, w_in, filter_taps, skip_gain[None, :], out_grad, f_hi, f_lo, i_hi, i_lo)
    filtered, tokens_grad, filter_grad, skip_grad = pl.pallas_call(
        hand_out,
        out_shape=(
            jax.ShapeDtypeStruct((rows, width), BF16),
            jax.ShapeDtypeStruct((TAPS, depth), BF16),
            jax.ShapeDtypeStruct((width, TAPS), F32),
            jax.ShapeDtypeStruct((1, width), F32),
        ),
        in_specs=[vmem] * 3,
        out_specs=(vmem,) * 4,
    )(filtered, tokens_grad, filter_total)
    return filtered, tokens_grad, filter_grad, skip_grad[0]


def solution(mesh):
    placed = (P(("ctx", "tp"), None), P("ctx", None, "tp"), P("tp", None), P("tp"), P("ctx", "tp"))
    return jax.shard_map(
        shards,
        mesh=mesh,
        in_specs=placed,
        out_specs=(P("ctx", "tp"), P(("ctx", "tp"), None), P("tp", None), P("tp")),
        check_vma=False,
    )
```
